32 devices in a mesh: rep: 8 (over y, x, core), shard: 4 (over z).
Axes of the slice: x: 2, y: 2, z: 4, core: 2. Of those that a mesh axis runs over, the one named last changes fastest.
Arguments:
- tokens: bfloat16 [4096, 1024], P(('rep', 'shard')), may hold values from -6 to 6
- cotangent: bfloat16 [4096, 1024], P(('rep', 'shard')), may hold values from -6 to 6
- lengths: int32 [8], replicated, may hold values from 385 to 512, as said below
- assign: int32 [8], P('rep'), may hold values from 0 to 7, each once
- first_gain: bfloat16 [1024], P('shard'), may hold values from 0.5 to 1.5
- first_shift: bfloat16 [1024], P('shard'), may hold values from -1.5 to 1.5
- qkv_weight: bfloat16 [1024, 3072], P('shard'), may hold values from -0.1875 to 0.1875
- qv_bias: bfloat16 [2048], P('shard'), may hold values from -2.5 to 2.5
- out_weight: bfloat16 [1024, 1024], P('shard'), may hold values from -0.5 to 0.5
- out_bias: bfloat16 [1024], P('shard'), may hold values from -1.5 to 1.5
- second_gain: bfloat16 [1024], P('shard'), may hold values from 0.5 to 1.5
- second_shift: bfloat16 [1024], P('shard'), may hold values from -1.5 to 1.5
- up_weight: bfloat16 [1024, 4096], P('shard'), may hold values from -0.1875 to 0.1875
- up_bias: bfloat16 [4096], P('shard'), may hold values from -2.5 to 2.5
- down_weight: bfloat16 [4096, 1024], P('shard'), may hold values from -0.09375 to 0.09375
- down_bias: bfloat16 [1024], P('shard'), may hold values from -1.5 to 1.5
Outputs:
- layer_out: float32 [4096, 1024], P(('rep', 'shard'))
- tokens_grad: float32 [4096, 1024], P(('rep', 'shard'))
- first_gain_grad: float32 [1024], P(('rep', 'shard'))
- first_shift_grad: float32 [1024], P(('rep', 'shard'))
- qkv_weight_grad: float32 [1024, 3072], P(('rep', 'shard'))
- qv_bias_grad: float32 [2048], P(('rep', 'shard'))
- out_weight_grad: float32 [1024, 1024], P(('rep', 'shard'))
- out_bias_grad: float32 [1024], P(('rep', 'shard'))
- second_gain_grad: float32 [1024], P(('rep', 'shard'))
- second_shift_grad: float32 [1024], P(('rep', 'shard'))
- up_weight_grad: float32 [1024, 4096], P(('rep', 'shard'))
- up_bias_grad: float32 [4096], P(('rep', 'shard'))
- down_weight_grad: float32 [4096, 1024], P(('rep', 'shard'))
- down_bias_grad: float32 [1024], P(('rep', 'shard'))
The draws below stay inside these ranges and needn't reach their ends.
Inputs may be any that keep to these rules, and one draw needn't show every extreme that they name: lengths[i] is the length of sequence i; at least one sequence has 512 tokens. assign holds each sequence number once.
All inputs are finite; a program needn't handle non-finite values.
Results may differ from the reference program's by a relative error of at most 0.015.
Values may be sent and summed in bfloat16 or wider, within the bound.
No kernel may reach another device: no remote copies, remote signals or barrier semaphores. Data moves between devices by JAX's collectives and lax.ppermute only.
A program may use at most 256 MiB of HBM per device.

```python
import math
import jax
import jax.numpy as jnp
from jax import lax

D = 1024
HEADS = 16
FF = 4096
TOK_DEV = 128
GROUP_TOK = 512
SEQS = 8
TOKENS = 4096


def draw_lengths(key, part):
    key = jax.random.fold_in(key, 11)
    first_key, second_key = jax.random.split(key)
    drawn = jax.random.randint(first_key, (SEQS,), GROUP_TOK - TOK_DEV + 1, GROUP_TOK + 1)
    chosen = jax.random.randint(second_key, (), 0, SEQS)
    return jnp.where(jnp.arange(SEQS) == chosen, GROUP_TOK, drawn).astype(jnp.int32)


def block_scale(rng, extent, shards, least, top_value):
    level, own = 1.0, jax.random.fold_in(rng, 6)
    for axis_at, parts in shards:
        heights = jnp.exp(jax.random.uniform(jax.random.fold_in(own, axis_at), (parts,), jnp.float32, least / len(shards), top_value / len(shards)))
        level = level * jnp.repeat(heights, extent[axis_at] // parts).reshape([-1 if axis == axis_at else 1 for axis in range(len(extent))])
    return level


def bell_draw(key, shape, deviation, bound, pieces=(), kind=jnp.bfloat16):
    values = deviation * jax.random.normal(key, shape, jnp.float32)
    if pieces:
        values = values * block_scale(key, shape, pieces, -0.22, 0.18)
    return jnp.clip(values, -bound, bound).astype(kind)


def setup_inputs(seed: int = 0) -> dict:
    key_list = jax.random.split(jax.random.key(seed), 17)
    return {
        "tokens": bell_draw(key_list[0], (TOKENS, D), 1.0, 6.0, ((0, 32),)),
        "cotangent": bell_draw(key_list[1], (TOKENS, D), 1.0, 6.0, ((0, 32),)),
        "lengths": draw_lengths(jax.random.fold_in(key_list[16], 71), 0),
        "assign": jax.random.permutation(key_list[3], SEQS).astype(jnp.int32),
        "first_gain": jnp.clip(1.0 + 0.1 * jax.random.normal(key_list[4], (D,), jnp.float32), 0.5, 1.5).astype(jnp.bfloat16),
        "first_shift": bell_draw(key_list[5], (D,), 0.3, 1.5, ((0, 4),)),
        "qkv_weight": bell_draw(key_list[6], (D, 3 * D), D ** -0.5, 0.1875, ((0, 4),)),
        "qv_bias": bell_draw(key_list[7], (2 * D,), 0.5, 2.5, ((0, 4),)),
        "out_weight": bell_draw(key_list[8], (D, D), (D // 8) ** -0.5, 0.5, ((0, 4),)),
        "out_bias": bell_draw(key_list[9], (D,), 0.3, 1.5, ((0, 4),)),
        "second_gain": jnp.clip(1.0 + 0.1 * jax.random.normal(key_list[10], (D,), jnp.float32), 0.5, 1.5).astype(jnp.bfloat16),
        "second_shift": bell_draw(key_list[11], (D,), 0.3, 1.5, ((0, 4),)),
        "up_weight": bell_draw(key_list[12], (D, FF), D ** -0.5, 0.1875, ((0, 4),)),
        "up_bias": bell_draw(key_list[13], (FF,), 0.5, 2.5, ((0, 4),)),
        "down_weight": bell_draw(key_list[14], (FF, D), FF ** -0.5, 0.09375, ((0, 4),)),
        "down_bias": bell_draw(key_list[15], (D,), 0.3, 1.5, ((0, 4),)),
    }


@jax.custom_vjp
def low(v):
    return lax.optimization_barrier(v.astype(jnp.bfloat16)).astype(jnp.float32)

@jax.custom_vjp
def low_back(v):
    return v

def low_keep(v):
    return (low(v), None)

def low_pass(kept, grad):
    return (grad,)

def back_keep(v):
    return (v, None)

def back_low(kept, grad):
    return (low(grad),)
low.defvjp(low_keep, low_pass)
low_back.defvjp(back_keep, back_low)

def layer_norm(rows_in, norm_gain, norm_shift):
    row_mean = lax.optimization_barrier(jnp.mean(rows_in, -1, keepdims=True))
    centered = rows_in - row_mean
    variance = lax.optimization_barrier(jnp.mean(centered * centered, -1, keepdims=True))
    return centered * lax.rsqrt(variance + 1e-05) * norm_gain + norm_shift

def matmul(left, right):
    return jnp.dot(left, right, precision=lax.Precision.HIGHEST)

def group_forward(rows_in, seq_length, params):
    first_gain = params[0]
    first_shift = params[1]
    qkv_weight = params[2]
    qv_bias = params[3]
    out_weight = params[4]
    out_bias = params[5]
    second_gain = params[6]
    second_shift = params[7]
    up_weight = params[8]
    up_bias = params[9]
    down_weight = params[10]
    down_bias = params[11]
    feature_count = rows_in.shape[1]
    head_size = feature_count // HEADS
    normed = low(layer_norm(rows_in, first_gain, first_shift))
    joint_out = matmul(normed, qkv_weight)
    queries = low_back(low(joint_out[:, :feature_count] + qv_bias[:feature_count]))
    keys_all = low_back(low(joint_out[:, feature_count:2 * feature_count]))
    values_all = low_back(low(joint_out[:, 2 * feature_count:] + qv_bias[feature_count:]))
    query_heads = queries.reshape(-1, HEADS, head_size)
    key_heads = keys_all.reshape(-1, HEADS, head_size)
    value_heads = values_all.reshape(-1, HEADS, head_size)
    positions = jnp.arange(rows_in.shape[0])
    slopes = jnp.exp2(-8.0 * (jnp.arange(HEADS).astype(jnp.float32) + 1.0) / HEADS)
    raw_scores = jnp.einsum('qhd,khd->hqk', query_heads, key_heads, precision=lax.Precision.HIGHEST) * (1.0 / math.sqrt(head_size))
    distance = (positions[:, None] - positions[None, :]).astype(jnp.float32)
    raw_scores = raw_scores - slopes[:, None, None] * distance[None]
    allowed = (positions[None, :] <= positions[:, None]) & (positions[None, :] < seq_length)
    scores = low_back(jnp.where(allowed[None], raw_scores, -1e+30))
    row_top = lax.optimization_barrier(jnp.max(scores, -1, keepdims=True))
    exp_scores = jnp.exp(scores - row_top)
    attn_probs = exp_scores / lax.optimization_barrier(jnp.sum(exp_scores, -1, keepdims=True))
    mixed = jnp.einsum('hqk,khd->qhd', low(attn_probs), value_heads, precision=lax.Precision.HIGHEST)
    mixed = low_back(low(mixed.reshape(-1, feature_count)))
    attended = low_back(matmul(mixed, out_weight) + out_bias)
    middle = rows_in + attended
    normed_two = low(layer_norm(middle, second_gain, second_shift))
    hidden = low_back(matmul(normed_two, up_weight) + up_bias)
    active = low(jax.nn.gelu(hidden, approximate=True))
    branch = low_back(matmul(active, down_weight) + down_bias)
    return middle + branch

def reference(tokens, cotangent, lengths, assign, first_gain, first_shift, qkv_weight, qv_bias, out_weight, out_bias, second_gain, second_shift, up_weight, up_bias, down_weight, down_bias):
    params = tuple((weight_item.astype(jnp.float32) for weight_item in (first_gain, first_shift, qkv_weight, qv_bias, out_weight, out_bias, second_gain, second_shift, up_weight, up_bias, down_weight, down_bias)))
    rows_in = tokens.astype(jnp.float32)
    group_lengths = jnp.take(lengths, assign)

    def forward(rows_all, params_all):
        grouped = rows_all.reshape(SEQS, GROUP_TOK, D)

        def one_group(group_item):
            return group_forward(group_item[0], group_item[1], params_all)
        outputs = lax.map(jax.checkpoint(one_group), (grouped, group_lengths))
        return outputs.reshape(TOKENS, D)
    layer_out, pullback = jax.vjp(forward, rows_in, params)
    positions = jnp.arange(GROUP_TOK)
    row_valid = (positions[None, :] < group_lengths[:, None]).reshape(TOKENS, 1)
    seed_grad = jnp.where(row_valid, cotangent.astype(jnp.float32), 0.0)
    tokens_grad, grads = pullback(seed_grad)
    return (layer_out, tokens_grad, grads[0], grads[1], grads[2], grads[3], grads[4], grads[5], grads[6], grads[7], grads[8], grads[9], grads[10], grads[11])
```

```python
import math

import jax
import jax.numpy as jnp
from jax import lax
from jax.experimental import pallas as pl
from jax.experimental.pallas import tpu as pltpu
from jax.sharding import PartitionSpec as P

HEADS = 16


def for_sending(value):
    return jax.tree.map(lambda a: a.astype(jnp.bfloat16) if a.dtype == jnp.float32 else a, value)


def cut_along(value, dim, devices):
    before, after = (value.shape[:dim], value.shape[dim + 1 :])
    return jnp.moveaxis(value.reshape(*before, devices, -1, *after), dim, 0)


def summed_on_arrival(value, axis, dim):
    blocks = cut_along(value, dim, lax.axis_size(axis))
    arrived = lax.all_to_all(blocks, axis, split_axis=0, concat_axis=0, tiled=True)
    return arrived.astype(jnp.float32).sum(axis=0)


def layer_norm(rows_in, norm_gain, norm_shift):
    row_mean = jnp.mean(rows_in, -1, keepdims=True)
    centered = rows_in - row_mean
    variance = jnp.mean(centered * centered, -1, keepdims=True)
    return centered * lax.rsqrt(variance + 1e-05) * norm_gain + norm_shift


def gelu_tanh(values_in):
    return jax.nn.gelu(values_in, approximate=True)


def owner_order(values):
    rep_count = lax.axis_size("rep")
    shard_count = lax.axis_size("shard")
    lead = values.shape[:-1]
    width = values.shape[-1]
    block = width // (rep_count * shard_count)
    arranged = values.reshape(lead + (rep_count, shard_count, block))
    return jnp.swapaxes(arranged, -3, -2).reshape(lead + (width,))


def settle(grads):
    group_summed = jax.tree.map(
        lambda part: part.astype(jnp.float32),
        lax.psum_scatter(for_sending(grads), "shard", scatter_dimension=0, tiled=True),
    )
    return jax.tree.map(lambda part: summed_on_arrival(part, "rep", 0), for_sending(group_summed))


def head_scores(query_heads, key_heads, query_pos, key_pos, seq_length):
    head_count = query_heads.shape[1]
    score_scale = 1.0 / math.sqrt(query_heads.shape[2])
    slopes = jnp.exp2(-8.0 * (jnp.arange(head_count).astype(jnp.float32) + 1.0) / head_count)
    raw_scores = (
        jnp.einsum("qhd,khd->hqk", query_heads, key_heads, preferred_element_type=jnp.float32)
        * score_scale
    )
    distance = (query_pos[:, None] - key_pos[None, :]).astype(jnp.float32)
    raw_scores = raw_scores - slopes[:, None, None] * distance[None]
    allowed = (key_pos[None, :] <= query_pos[:, None]) & (key_pos[None, :] < seq_length)
    return jnp.where(allowed[None], raw_scores, -1e30)


def body_generic(
    tokens,
    cotangent,
    lengths,
    assign,
    first_gain,
    first_shift,
    qkv_weight,
    qv_bias,
    out_weight,
    out_bias,
    second_gain,
    second_shift,
    up_weight,
    up_bias,
    down_weight,
    down_bias,
):
    rows_in = tokens.astype(jnp.float32)
    row_count = rows_in.shape[0]
    feature_count = rows_in.shape[1]
    head_count = HEADS
    head_size = feature_count // head_count
    score_scale = 1.0 / math.sqrt(head_size)
    group_size = row_count * lax.axis_size("shard")
    seq_length = jnp.sum(jnp.where(jnp.arange(lengths.shape[0]) == assign[0], lengths, 0))
    query_pos = lax.axis_index("shard") * row_count + jnp.arange(row_count)
    key_pos = jnp.arange(group_size)
    row_valid = (query_pos < seq_length)[:, None]
    owned = (
        first_gain,
        first_shift,
        qkv_weight,
        qv_bias,
        out_weight,
        out_bias,
        second_gain,
        second_shift,
        up_weight,
        up_bias,
        down_weight,
        down_bias,
    )
    gathered = (
        lax.all_gather(owned[0], "shard", axis=0, tiled=True),
        lax.all_gather(owned[1], "shard", axis=0, tiled=True),
        lax.all_gather(owned[2], "shard", axis=0, tiled=True),
        lax.all_gather(owned[3], "shard", axis=0, tiled=True),
        lax.all_gather(owned[4], "shard", axis=0, tiled=True),
        lax.all_gather(owned[5], "shard", axis=0, tiled=True),
        lax.all_gather(owned[6], "shard", axis=0, tiled=True),
        lax.all_gather(owned[7], "shard", axis=0, tiled=True),
        lax.all_gather(owned[8], "shard", axis=0, tiled=True),
        lax.all_gather(owned[9], "shard", axis=0, tiled=True),
        lax.all_gather(owned[10], "shard", axis=0, tiled=True),
        lax.all_gather(owned[11], "shard", axis=0, tiled=True),
    )
    gain_first = gathered[0].astype(jnp.float32)
    shift_first = gathered[1].astype(jnp.float32)
    bias_qv = gathered[3].astype(jnp.float32)
    bias_out = gathered[5].astype(jnp.float32)
    gain_second = gathered[6].astype(jnp.float32)
    shift_second = gathered[7].astype(jnp.float32)
    bias_up = gathered[9].astype(jnp.float32)
    bias_down = gathered[11].astype(jnp.float32)
    normed = layer_norm(rows_in, gain_first, shift_first)
    normed_low = normed.astype(jnp.bfloat16)
    joint_out = jnp.dot(normed_low, gathered[2], preferred_element_type=jnp.float32)
    query_low = (joint_out[:, :feature_count] + bias_qv[:feature_count]).astype(jnp.bfloat16)
    key_low = joint_out[:, feature_count : 2 * feature_count].astype(jnp.bfloat16)
    value_low = (joint_out[:, 2 * feature_count :] + bias_qv[feature_count:]).astype(jnp.bfloat16)
    key_all, value_all = (
        lax.all_gather(key_low, "shard", axis=0, tiled=True),
        lax.all_gather(value_low, "shard", axis=0, tiled=True),
    )
    query_heads = query_low.reshape(row_count, head_count, head_size)
    scores = head_scores(
        query_heads,
        key_all.reshape(group_size, head_count, head_size),
        query_pos,
        key_pos,
        seq_length,
    )
    row_top = jnp.max(scores, -1, keepdims=True)
    exp_scores = jnp.exp(scores - row_top)
    row_total = jnp.sum(exp_scores, -1, keepdims=True)
    log_total = row_top + jnp.log(row_total)
    attn_probs = exp_scores / row_total
    mixed_low = (
        jnp.einsum(
            "hqk,khd->qhd",
            attn_probs.astype(jnp.bfloat16),
            value_all.reshape(group_size, head_count, head_size),
            preferred_element_type=jnp.float32,
        )
        .reshape(row_count, feature_count)
        .astype(jnp.bfloat16)
    )
    attended = jnp.dot(mixed_low, gathered[4], preferred_element_type=jnp.float32) + bias_out
    middle = rows_in + attended
    normed_two_low = layer_norm(middle, gain_second, shift_second).astype(jnp.bfloat16)
    hidden = jnp.dot(normed_two_low, gathered[8], preferred_element_type=jnp.float32) + bias_up
    active_low = gelu_tanh(hidden).astype(jnp.bfloat16)
    branch = jnp.dot(active_low, gathered[10], preferred_element_type=jnp.float32) + bias_down
    layer_out = middle + branch
    back_keys = (key_all, value_all)
    key_heads_back = back_keys[0].reshape(group_size, head_count, head_size)
    value_heads_back = back_keys[1].reshape(group_size, head_count, head_size)
    seed_grad = jnp.where(row_valid, cotangent.astype(jnp.float32), 0.0)
    branch_grad = seed_grad.astype(jnp.bfloat16)
    down_grad = jnp.dot(owner_order(active_low).T, branch_grad, preferred_element_type=jnp.float32)
    down_bias_grad = owner_order(jnp.sum(branch_grad.astype(jnp.float32), 0))
    active_grad = jnp.dot(branch_grad, gathered[10].T, preferred_element_type=jnp.float32)
    unused, gelu_pull = jax.vjp(gelu_tanh, hidden)
    hidden_grad = gelu_pull(active_grad)[0].astype(jnp.bfloat16)
    up_grad = jnp.dot(
        owner_order(normed_two_low).T, hidden_grad, preferred_element_type=jnp.float32
    )
    up_bias_grad = owner_order(jnp.sum(hidden_grad.astype(jnp.float32), 0))
    normed_two_grad = jnp.dot(hidden_grad, gathered[8].T, preferred_element_type=jnp.float32)
    unused_two, second_pull = jax.vjp(layer_norm, middle, gain_second, shift_second)
    middle_from_norm, gain_second_grad, shift_second_grad = second_pull(normed_two_grad)
    middle_grad = seed_grad + middle_from_norm
    down_sums = settle((down_grad, down_bias_grad, up_bias_grad))
    up_sums = settle((up_grad, owner_order(gain_second_grad), owner_order(shift_second_grad)))
    attended_grad = middle_grad.astype(jnp.bfloat16)
    out_grad = jnp.dot(owner_order(mixed_low).T, attended_grad, preferred_element_type=jnp.float32)
    out_bias_grad = owner_order(jnp.sum(attended_grad.astype(jnp.float32), 0))
    mixed_grad = (
        jnp.dot(attended_grad, gathered[4].T, preferred_element_type=jnp.float32)
        .astype(jnp.bfloat16)
        .reshape(row_count, head_count, head_size)
    )
    scores_back = head_scores(query_heads, key_heads_back, query_pos, key_pos, seq_length)
    probs_back = jnp.exp(scores_back - log_total)
    probs_grad = jnp.einsum(
        "qhd,khd->hqk", mixed_grad, value_heads_back, preferred_element_type=jnp.float32
    )
    value_part = jnp.einsum(
        "hqk,qhd->khd",
        probs_back.astype(jnp.bfloat16),
        mixed_grad,
        preferred_element_type=jnp.float32,
    ).reshape(group_size, feature_count)
    row_dot = jnp.sum(probs_back * probs_grad, -1, keepdims=True)
    score_grad = (probs_back * (probs_grad - row_dot)).astype(jnp.bfloat16)
    query_grad = (
        jnp.einsum("hqk,khd->qhd", score_grad, key_heads_back, preferred_element_type=jnp.float32)
        * score_scale
    )
    key_part = (
        jnp.einsum(
            "hqk,qhd->khd", score_grad, query_heads, preferred_element_type=jnp.float32
        ).reshape(group_size, feature_count)
        * score_scale
    )
    key_grad, value_grad = (
        lax.psum_scatter(
            key_part.astype(jnp.bfloat16), "shard", scatter_dimension=0, tiled=True
        ).astype(jnp.float32),
        lax.psum_scatter(
            value_part.astype(jnp.bfloat16), "shard", scatter_dimension=0, tiled=True
        ).astype(jnp.float32),
    )
    joint_grad = jnp.concatenate(
        [query_grad.reshape(row_count, feature_count), key_grad, value_grad], 1
    ).astype(jnp.bfloat16)
    qkv_grad = jnp.dot(owner_order(normed_low).T, joint_grad, preferred_element_type=jnp.float32)
    joint_sums = jnp.sum(joint_grad.astype(jnp.float32), 0)
    qv_bias_grad = owner_order(
        jnp.concatenate([joint_sums[:feature_count], joint_sums[2 * feature_count :]], 0)
    )
    normed_grad = jnp.dot(joint_grad, gathered[2].T, preferred_element_type=jnp.float32)
    unused_three, first_pull = jax.vjp(layer_norm, rows_in, gain_first, shift_first)
    rows_from_norm, gain_first_grad, shift_first_grad = first_pull(normed_grad)
    tokens_grad = middle_grad + rows_from_norm
    attn_sums = settle(
        (
            qkv_grad,
            qv_bias_grad,
            out_grad,
            out_bias_grad,
            owner_order(gain_first_grad),
            owner_order(shift_first_grad),
        )
    )
    return (
        layer_out,
        tokens_grad,
        attn_sums[4],
        attn_sums[5],
        attn_sums[0],
        attn_sums[1],
        attn_sums[2],
        attn_sums[3],
        up_sums[1],
        up_sums[2],
        up_sums[0],
        down_sums[2],
        down_sums[0],
        down_sums[1],
    )


PLANE = 8
DEPTH = 4
QUARTERS = 4


def is_planes(mesh):
    return mesh.shape["rep"] == PLANE and mesh.shape["shard"] == DEPTH


def over_rep(value, partner):
    return lax.ppermute(value, "rep", [(i, partner(i)) for i in range(PLANE)])


def over_z(value, step):
    return lax.ppermute(value, "shard", [(i, (i + step) % DEPTH) for i in range(DEPTH)])


def first_way(i):
    return i ^ (4 if i & 1 else 2)


def second_way(i):
    return i ^ (2 if i & 1 else 4)


def sibling(i):
    return i ^ 1


def home_of(index):
    rep, z = index // DEPTH, index % DEPTH
    return ((rep & 1) * 4 + z) * DEPTH + rep // 2


def to_home(value):
    pairs = [(i, home_of(i)) for i in range(PLANE * DEPTH)]
    return lax.ppermute(value, ("rep", "shard"), pairs)


def from_home(value):
    pairs = [(home_of(i), i) for i in range(PLANE * DEPTH)]
    return lax.ppermute(value, ("rep", "shard"), pairs)


def spread(block):
    arrived = jnp.concatenate([over_z(block, step) for step in (1, 2, 3)], 0)
    beside = over_rep(arrived, first_way)
    pair = jnp.concatenate([arrived, beside], 0)
    mine = jnp.concatenate([pair, over_rep(pair, second_way)], 0)
    return mine, over_rep(mine, sibling)


def assemble_kernel(rows, own_ref, mine_ref, other_ref, out_ref, sems):
    rep = lax.axis_index("rep")
    z = lax.axis_index("shard")
    copies = [
        pltpu.make_async_copy(
            own_ref, out_ref.at[pl.ds(z * (PLANE * rows), PLANE * rows)], sems.at[24]
        )
    ]
    for side, held in enumerate((mine_ref, other_ref)):
        base = rep ^ side
        odd = base & 1
        for slot in range(4):
            if slot == 0:
                source = base
            elif slot == 1:
                source = base ^ (2 + 2 * odd)
            elif slot == 2:
                source = base ^ (4 - 2 * odd)
            else:
                source = base ^ 6
            for step in (1, 2, 3):
                plane = lax.rem(z + (DEPTH - step), DEPTH)
                place = plane * (PLANE * rows) + source * rows
                index = slot * 3 + step - 1
                copies.append(
                    pltpu.make_async_copy(
                        held.at[pl.ds(index * rows, rows)],
                        out_ref.at[pl.ds(pl.multiple_of(place, rows), rows)],
                        sems.at[side * 12 + index],
                    )
                )
    for copy in copies:
        copy.start()
    for copy in copies:
        copy.wait()


def assemble(own, pieces):
    rows = own.shape[0] // PLANE

    def kernel(*refs):
        assemble_kernel(rows, *refs)

    whole = (own.shape[0] * DEPTH, own.shape[1])
    return pl.pallas_call(
        kernel,
        out_shape=jax.ShapeDtypeStruct(whole, own.dtype),
        in_specs=[pl.BlockSpec(memory_space=pl.ANY)] * 3,
        out_specs=pl.BlockSpec(memory_space=pltpu.VMEM),
        scratch_shapes=[pltpu.SemaphoreType.DMA((25,))],
        compiler_params=pltpu.CompilerParams(vmem_limit_bytes=24 * 2**20),
        cost_estimate=pl.CostEstimate(
            flops=0, bytes_accessed=4 * whole[0] * whole[1], transcendentals=0
        ),
    )(own, *pieces)


def block_at(blocks, index):
    return lax.dynamic_index_in_dim(blocks, index, 0, keepdims=False)


def summed_over_z(blocks):
    z = lax.axis_index("shard")
    low = blocks.astype(jnp.bfloat16)
    total = block_at(blocks, z)
    for step in (1, 2, 3):
        sent = block_at(low, lax.rem(z + step, DEPTH))
        total = total + over_z(sent, step).astype(jnp.float32)
    return total


def by_plane(value):
    count, width = value.shape
    blocks = jnp.swapaxes(value.reshape(count, PLANE, width // PLANE), 0, 1)
    arrived = lax.all_to_all(blocks, "rep", 0, 0, tiled=True)
    return arrived.reshape(PLANE * count, width // PLANE)


def plane_rows(value):
    return lax.all_gather(value, "rep", axis=0, tiled=True)


def outer(left, right):
    return lax.dot_general(
        left, right, (((0,), (0,)), ((), ())), preferred_element_type=jnp.float32
    )


def column_parts_to_rows(grad):
    rows, width = grad.shape
    parts = grad.reshape(PLANE, DEPTH, rows // (PLANE * DEPTH), width)
    summed = summed_over_z(jnp.swapaxes(parts, 0, 1)).astype(jnp.bfloat16)
    arrived = lax.all_to_all(summed, "rep", 0, 0, tiled=True)
    return jnp.swapaxes(arrived, 0, 1).reshape(-1, PLANE * width).astype(jnp.float32)


def body_planes(
    tokens,
    cotangent,
    lengths,
    assign,
    first_gain,
    first_shift,
    qkv_weight,
    qv_bias,
    out_weight,
    out_bias,
    second_gain,
    second_shift,
    up_weight,
    up_bias,
    down_weight,
    down_bias,
):
    row_count, feature_count = tokens.shape
    head_count = HEADS
    head_size = feature_count // head_count
    score_scale = 1.0 / math.sqrt(head_size)
    group_size = row_count * QUARTERS
    rep = lax.axis_index("rep")
    z = lax.axis_index("shard")
    quarter = rep & 3

    own_length = jnp.sum(jnp.where(jnp.arange(lengths.shape[0]) == assign[0], lengths, 0))
    seq_length = to_home(own_length.astype(jnp.float32).reshape(1, 1)).astype(jnp.int32)[0, 0]
    tokens = to_home(tokens)
    cotangent = to_home(cotangent)

    small = (
        first_gain,
        first_shift,
        qv_bias,
        out_bias,
        second_gain,
        second_shift,
        up_bias,
        down_bias,
    )
    packed = jnp.concatenate(small, 0).reshape(1, -1)
    around = [packed] + [over_z(packed, step) for step in (1, 2, 3)]
    parts = []
    for plane in range(DEPTH):
        back = lax.rem(z + (DEPTH - plane), DEPTH)
        parts.append(
            sum(
                jnp.where(back == step, around[step].astype(jnp.float32), 0.0)
                for step in range(DEPTH)
            )
        )
    stacked = jnp.concatenate(parts, 0)
    whole_small = []
    start = 0
    for item in small:
        size = item.shape[0]
        whole_small.append(stacked[:, start : start + size].reshape(-1))
        start += size
    (
        gain_first,
        shift_first,
        bias_qv,
        bias_out,
        gain_second,
        shift_second,
        bias_up,
        bias_down,
    ) = whole_small

    weights = (qkv_weight, out_weight, up_weight, down_weight)
    eighths = lax.optimization_barrier(
        tuple(
            lax.dynamic_slice_in_dim(w, rep * (w.shape[0] // PLANE), w.shape[0] // PLANE, 0)
            for w in weights
        )
    )
    qkv_all, out_all, up_all, down_all = [
        assemble(w, spread(part)) for w, part in zip(weights, eighths)
    ]

    rows_in = tokens.astype(jnp.float32)
    query_pos = quarter * row_count + jnp.arange(row_count)
    order = jnp.array([0, 2, 1, 3])
    key_pos = ((quarter ^ order)[:, None] * row_count + jnp.arange(row_count)[None]).reshape(-1)
    row_valid = (query_pos < seq_length)[:, None]
    seed_grad = jnp.where(row_valid, cotangent.astype(jnp.float32), 0.0)
    branch_grad = seed_grad.astype(jnp.bfloat16)
    branch_grad_plane = plane_rows(branch_grad)

    normed_low = layer_norm(rows_in, gain_first, shift_first).astype(jnp.bfloat16)
    normed_plane = plane_rows(normed_low)
    joint_out = jnp.dot(normed_low, qkv_all, preferred_element_type=jnp.float32)
    query_low = (joint_out[:, :feature_count] + bias_qv[:feature_count]).astype(jnp.bfloat16)
    key_low = joint_out[:, feature_count : 2 * feature_count].astype(jnp.bfloat16)
    value_low = (joint_out[:, 2 * feature_count :] + bias_qv[feature_count:]).astype(jnp.bfloat16)
    own_pair = jnp.stack([key_low, value_low], 0)
    near = jnp.concatenate([own_pair, over_rep(own_pair, lambda i: i ^ 2)], 1)
    pair_all = jnp.concatenate([near, over_rep(near, sibling)], 1)
    key_heads = pair_all[0].reshape(group_size, head_count, head_size)
    value_heads = pair_all[1].reshape(group_size, head_count, head_size)
    query_heads = query_low.reshape(row_count, head_count, head_size)
    scores = head_scores(query_heads, key_heads, query_pos, key_pos, seq_length)
    row_top = jnp.max(scores, -1, keepdims=True)
    exp_scores = jnp.exp(scores - row_top)
    row_total = jnp.sum(exp_scores, -1, keepdims=True)
    attn_probs = exp_scores / row_total
    probs_low = attn_probs.astype(jnp.bfloat16)
    mixed_low = (
        jnp.einsum("hqk,khd->qhd", probs_low, value_heads, preferred_element_type=jnp.float32)
        .reshape(row_count, feature_count)
        .astype(jnp.bfloat16)
    )
    middle = rows_in + jnp.dot(mixed_low, out_all, preferred_element_type=jnp.float32) + bias_out
    normed_two_low = layer_norm(middle, gain_second, shift_second).astype(jnp.bfloat16)
    normed_two_plane = plane_rows(normed_two_low)
    hidden = jnp.dot(normed_two_low, up_all, preferred_element_type=jnp.float32) + bias_up
    active_low = gelu_tanh(hidden).astype(jnp.bfloat16)
    branch = jnp.dot(active_low, down_all, preferred_element_type=jnp.float32) + bias_down
    layer_out = from_home((middle + branch).astype(jnp.bfloat16)).astype(jnp.float32)

    active_plane = by_plane(active_low)
    active_grad = jnp.dot(branch_grad, down_all.T, preferred_element_type=jnp.float32)
    unused, gelu_pull = jax.vjp(gelu_tanh, hidden)
    hidden_grad = gelu_pull(active_grad)[0].astype(jnp.bfloat16)
    hidden_grad_plane = by_plane(hidden_grad)
    normed_two_grad = jnp.dot(hidden_grad, up_all.T, preferred_element_type=jnp.float32)
    unused_two, second_pull = jax.vjp(layer_norm, middle, gain_second, shift_second)
    middle_from_norm, gain_second_grad, shift_second_grad = second_pull(normed_two_grad)
    middle_grad = seed_grad + middle_from_norm

    down_slice = outer(active_plane, branch_grad_plane)
    down_grad = summed_over_z(down_slice.reshape(DEPTH, -1, feature_count))
    up_grad = column_parts_to_rows(outer(normed_two_plane, hidden_grad_plane))

    attended_grad = middle_grad.astype(jnp.bfloat16)
    attended_grad_plane = plane_rows(attended_grad)
    mixed_plane = by_plane(mixed_low)
    out_slice = outer(mixed_plane, attended_grad_plane)
    out_grad = summed_over_z(out_slice.reshape(DEPTH, -1, feature_count))

    mixed_grad = (
        jnp.dot(attended_grad, out_all.T, preferred_element_type=jnp.float32)
        .astype(jnp.bfloat16)
        .reshape(row_count, head_count, head_size)
    )
    probs_grad = jnp.einsum(
        "qhd,khd->hqk", mixed_grad, value_heads, preferred_element_type=jnp.float32
    )
    value_part = jnp.einsum(
        "hqk,qhd->khd", probs_low, mixed_grad, preferred_element_type=jnp.float32
    ).reshape(group_size, feature_count)
    row_dot = jnp.sum(attn_probs * probs_grad, -1, keepdims=True)
    score_grad = (attn_probs * (probs_grad - row_dot)).astype(jnp.bfloat16)
    query_grad = (
        jnp.einsum("hqk,khd->qhd", score_grad, key_heads, preferred_element_type=jnp.float32)
        * score_scale
    )
    key_part = (
        jnp.einsum(
            "hqk,qhd->khd", score_grad, query_heads, preferred_element_type=jnp.float32
        ).reshape(group_size, feature_count)
        * score_scale
    )
    back = jnp.stack([key_part, value_part], 0)
    half = group_size // 2
    given = over_rep(back[:, half:].astype(jnp.bfloat16), sibling)
    back = back[:, :half] + given.astype(jnp.float32)
    given = over_rep(back[:, row_count:].astype(jnp.bfloat16), lambda i: i ^ 2)
    back = back[:, :row_count] + given.astype(jnp.float32)
    joint_grad = jnp.concatenate(
        [query_grad.reshape(row_count, feature_count), back[0], back[1]], 1
    ).astype(jnp.bfloat16)
    joint_grad_plane = by_plane(joint_grad)
    qkv_grad = column_parts_to_rows(outer(normed_plane, joint_grad_plane))
    normed_grad = jnp.dot(joint_grad, qkv_all.T, preferred_element_type=jnp.float32)
    unused_three, first_pull = jax.vjp(layer_norm, rows_in, gain_first, shift_first)
    rows_from_norm, gain_first_grad, shift_first_grad = first_pull(normed_grad)
    tokens_grad = from_home((middle_grad + rows_from_norm).astype(jnp.bfloat16)).astype(jnp.float32)

    joint_sums = jnp.sum(joint_grad.astype(jnp.float32), 0)
    small_grads = (
        gain_first_grad,
        shift_first_grad,
        jnp.concatenate([joint_sums[:feature_count], joint_sums[2 * feature_count :]], 0),
        jnp.sum(attended_grad.astype(jnp.float32), 0),
        gain_second_grad,
        shift_second_grad,
        jnp.sum(hidden_grad.astype(jnp.float32), 0),
        jnp.sum(branch_grad.astype(jnp.float32), 0),
    )
    devices = PLANE * DEPTH
    small_packed = jnp.concatenate(
        [g.reshape(devices, g.shape[0] // devices) for g in small_grads], 1
    ).astype(jnp.bfloat16)
    small_arrived = lax.all_to_all(small_packed, ("rep", "shard"), 0, 0, tiled=True)
    small_sums = jnp.sum(small_arrived.astype(jnp.float32), 0)
    sums = []
    start = 0
    for g in small_grads:
        size = g.shape[0] // devices
        sums.append(small_sums[start : start + size])
        start += size
    return (
        layer_out,
        tokens_grad,
        sums[0],
        sums[1],
        qkv_grad,
        sums[2],
        out_grad,
        sums[3],
        sums[4],
        sums[5],
        up_grad,
        sums[6],
        down_grad,
        sums[7],
    )


def solution(mesh):
    return jax.shard_map(
        body_planes if is_planes(mesh) else body_generic,
        mesh=mesh,
        in_specs=(
            P(("rep", "shard"), None),
            P(("rep", "shard"), None),
            P(),
            P("rep"),
            P("shard"),
            P("shard"),
            P("shard", None),
            P("shard"),
            P("shard", None),
            P("shard"),
            P("shard"),
            P("shard"),
            P("shard", None),
            P("shard"),
            P("shard", None),
            P("shard"),
        ),
        out_specs=(
            P(("rep", "shard"), None),
            P(("rep", "shard"), None),
            P(("rep", "shard")),
            P(("rep", "shard")),
            P(("rep", "shard"), None),
            P(("rep", "shard")),
            P(("rep", "shard"), None),
            P(("rep", "shard")),
            P(("rep", "shard")),
            P(("rep", "shard")),
            P(("rep", "shard"), None),
            P(("rep", "shard")),
            P(("rep", "shard"), None),
            P(("rep", "shard")),
        ),
        check_vma=False,
    )
```

```python
import math

import jax
import jax.numpy as jnp
from jax import lax
from jax.experimental import pallas as pl
from jax.experimental.pallas import tpu as pltpu
from jax.sharding import PartitionSpec as P

HEADS = 16


def for_sending(value):
    return jax.tree.map(lambda a: a.astype(jnp.bfloat16) if a.dtype == jnp.float32 else a, value)


def cut_along(value, dim, devices):
    before, after = (value.shape[:dim], value.shape[dim + 1 :])
    return jnp.moveaxis(value.reshape(*before, devices, -1, *after), dim, 0)


def summed_on_arrival(value, axis, dim):
    blocks = cut_along(value, dim, lax.axis_size(axis))
    arrived = lax.all_to_all(blocks, axis, split_axis=0, concat_axis=0, tiled=True)
    return arrived.astype(jnp.float32).sum(axis=0)


def layer_norm(rows_in, norm_gain, norm_shift):
    row_mean = jnp.mean(rows_in, -1, keepdims=True)
    centered = rows_in - row_mean
    variance = jnp.mean(centered * centered, -1, keepdims=True)
    return centered * lax.rsqrt(variance + 1e-05) * norm_gain + norm_shift


def gelu_tanh(values_in):
    return jax.nn.gelu(values_in, approximate=True)


def owner_order(values):
    rep_count = lax.axis_size("rep")
    shard_count = lax.axis_size("shard")
    lead = values.shape[:-1]
    width = values.shape[-1]
    block = width // (rep_count * shard_count)
    arranged = values.reshape(lead + (rep_count, shard_count, block))
    return jnp.swapaxes(arranged, -3, -2).reshape(lead + (width,))


def settle(grads):
    group_summed = jax.tree.map(
        lambda part: part.astype(jnp.float32),
        lax.psum_scatter(for_sending(grads), "shard", scatter_dimension=0, tiled=True),
    )
    return jax.tree.map(lambda part: summed_on_arrival(part, "rep", 0), for_sending(group_summed))


def head_scores(query_heads, key_heads, query_pos, key_pos, seq_length):
    head_count = query_heads.shape[1]
    score_scale = 1.0 / math.sqrt(query_heads.shape[2])
    slopes = jnp.exp2(-8.0 * (jnp.arange(head_count).astype(jnp.float32) + 1.0) / head_count)
    raw_scores = (
        jnp.einsum("qhd,khd->hqk", query_heads, key_heads, preferred_element_type=jnp.float32)
        * score_scale
    )
    distance = (query_pos[:, None] - key_pos[None, :]).astype(jnp.float32)
    raw_scores = raw_scores - slopes[:, None, None] * distance[None]
    allowed = (key_pos[None, :] <= query_pos[:, None]) & (key_pos[None, :] < seq_length)
    return jnp.where(allowed[None], raw_scores, -1e30)


def body_generic(
    tokens,
    cotangent,
    lengths,
    assign,
    first_gain,
    first_shift,
    qkv_weight,
    qv_bias,
    out_weight,
    out_bias,
    second_gain,
    second_shift,
    up_weight,
    up_bias,
    down_weight,
    down_bias,
):
    rows_in = tokens.astype(jnp.float32)
    row_count = rows_in.shape[0]
    feature_count = rows_in.shape[1]
    head_count = HEADS
    head_size = feature_count // head_count
    score_scale = 1.0 / math.sqrt(head_size)
    group_size = row_count * lax.axis_size("shard")
    seq_length = jnp.sum(jnp.where(jnp.arange(lengths.shape[0]) == assign[0], lengths, 0))
    query_pos = lax.axis_index("shard") * row_count + jnp.arange(row_count)
    key_pos = jnp.arange(group_size)
    row_valid = (query_pos < seq_length)[:, None]
    owned = (
        first_gain,
        first_shift,
        qkv_weight,
        qv_bias,
        out_weight,
        out_bias,
        second_gain,
        second_shift,
        up_weight,
        up_bias,
        down_weight,
        down_bias,
    )
    gathered = (
        lax.all_gather(owned[0], "shard", axis=0, tiled=True),
        lax.all_gather(owned[1], "shard", axis=0, tiled=True),
        lax.all_gather(owned[2], "shard", axis=0, tiled=True),
        lax.all_gather(owned[3], "shard", axis=0, tiled=True),
        lax.all_gather(owned[4], "shard", axis=0, tiled=True),
        lax.all_gather(owned[5], "shard", axis=0, tiled=True),
        lax.all_gather(owned[6], "shard", axis=0, tiled=True),
        lax.all_gather(owned[7], "shard", axis=0, tiled=True),
        lax.all_gather(owned[8], "shard", axis=0, tiled=True),
        lax.all_gather(owned[9], "shard", axis=0, tiled=True),
        lax.all_gather(owned[10], "shard", axis=0, tiled=True),
        lax.all_gather(owned[11], "shard", axis=0, tiled=True),
    )
    gain_first = gathered[0].astype(jnp.float32)
    shift_first = gathered[1].astype(jnp.float32)
    bias_qv = gathered[3].astype(jnp.float32)
    bias_out = gathered[5].astype(jnp.float32)
    gain_second = gathered[6].astype(jnp.float32)
    shift_second = gathered[7].astype(jnp.float32)
    bias_up = gathered[9].astype(jnp.float32)
    bias_down = gathered[11].astype(jnp.float32)
    normed = layer_norm(rows_in, gain_first, shift_first)
    normed_low = normed.astype(jnp.bfloat16)
    joint_out = jnp.dot(normed_low, gathered[2], preferred_element_type=jnp.float32)
    query_low = (joint_out[:, :feature_count] + bias_qv[:feature_count]).astype(jnp.bfloat16)
    key_low = joint_out[:, feature_count : 2 * feature_count].astype(jnp.bfloat16)
    value_low = (joint_out[:, 2 * feature_count :] + bias_qv[feature_count:]).astype(jnp.bfloat16)
    key_all, value_all = (
        lax.all_gather(key_low, "shard", axis=0, tiled=True),
        lax.all_gather(value_low, "shard", axis=0, tiled=True),
    )
    query_heads = query_low.reshape(row_count, head_count, head_size)
    scores = head_scores(
        query_heads,
        key_all.reshape(group_size, head_count, head_size),
        query_pos,
        key_pos,
        seq_length,
    )
    row_top = jnp.max(scores, -1, keepdims=True)
    exp_scores = jnp.exp(scores - row_top)
    row_total = jnp.sum(exp_scores, -1, keepdims=True)
    log_total = row_top + jnp.log(row_total)
    attn_probs = exp_scores / row_total
    mixed_low = (
        jnp.einsum(
            "hqk,khd->qhd",
            attn_probs.astype(jnp.bfloat16),
            value_all.reshape(group_size, head_count, head_size),
            preferred_element_type=jnp.float32,
        )
        .reshape(row_count, feature_count)
        .astype(jnp.bfloat16)
    )
    attended = jnp.dot(mixed_low, gathered[4], preferred_element_type=jnp.float32) + bias_out
    middle = rows_in + attended
    normed_two_low = layer_norm(middle, gain_second, shift_second).astype(jnp.bfloat16)
    hidden = jnp.dot(normed_two_low, gathered[8], preferred_element_type=jnp.float32) + bias_up
    active_low = gelu_tanh(hidden).astype(jnp.bfloat16)
    branch = jnp.dot(active_low, gathered[10], preferred_element_type=jnp.float32) + bias_down
    layer_out = middle + branch
    back_keys = (key_all, value_all)
    key_heads_back = back_keys[0].reshape(group_size, head_count, head_size)
    value_heads_back = back_keys[1].reshape(group_size, head_count, head_size)
    seed_grad = jnp.where(row_valid, cotangent.astype(jnp.float32), 0.0)
    branch_grad = seed_grad.astype(jnp.bfloat16)
    down_grad = jnp.dot(owner_order(active_low).T, branch_grad, preferred_element_type=jnp.float32)
    down_bias_grad = owner_order(jnp.sum(branch_grad.astype(jnp.float32), 0))
    active_grad = jnp.dot(branch_grad, gathered[10].T, preferred_element_type=jnp.float32)
    unused, gelu_pull = jax.vjp(gelu_tanh, hidden)
    hidden_grad = gelu_pull(active_grad)[0].astype(jnp.bfloat16)
    up_grad = jnp.dot(
        owner_order(normed_two_low).T, hidden_grad, preferred_element_type=jnp.float32
    )
    up_bias_grad = owner_order(jnp.sum(hidden_grad.astype(jnp.float32), 0))
    normed_two_grad = jnp.dot(hidden_grad, gathered[8].T, preferred_element_type=jnp.float32)
    unused_two, second_pull = jax.vjp(layer_norm, middle, gain_second, shift_second)
    middle_from_norm, gain_second_grad, shift_second_grad = second_pull(normed_two_grad)
    middle_grad = seed_grad + middle_from_norm
    down_sums = settle((down_grad, down_bias_grad, up_bias_grad))
    up_sums = settle((up_grad, owner_order(gain_second_grad), owner_order(shift_second_grad)))
    attended_grad = middle_grad.astype(jnp.bfloat16)
    out_grad = jnp.dot(owner_order(mixed_low).T, attended_grad, preferred_element_type=jnp.float32)
    out_bias_grad = owner_order(jnp.sum(attended_grad.astype(jnp.float32), 0))
    mixed_grad = (
        jnp.dot(attended_grad, gathered[4].T, preferred_element_type=jnp.float32)
        .astype(jnp.bfloat16)
        .reshape(row_count, head_count, head_size)
    )
    scores_back = head_scores(query_heads, key_heads_back, query_pos, key_pos, seq_length)
    probs_back = jnp.exp(scores_back - log_total)
    probs_grad = jnp.einsum(
        "qhd,khd->hqk", mixed_grad, value_heads_back, preferred_element_type=jnp.float32
    )
    value_part = jnp.einsum(
        "hqk,qhd->khd",
        probs_back.astype(jnp.bfloat16),
        mixed_grad,
        preferred_element_type=jnp.float32,
    ).reshape(group_size, feature_count)
    row_dot = jnp.sum(probs_back * probs_grad, -1, keepdims=True)
    score_grad = (probs_back * (probs_grad - row_dot)).astype(jnp.bfloat16)
    query_grad = (
        jnp.einsum("hqk,khd->qhd", score_grad, key_heads_back, preferred_element_type=jnp.float32)
        * score_scale
    )
    key_part = (
        jnp.einsum(
            "hqk,qhd->khd", score_grad, query_heads, preferred_element_type=jnp.float32
        ).reshape(group_size, feature_count)
        * score_scale
    )
    key_grad, value_grad = (
        lax.psum_scatter(
            key_part.astype(jnp.bfloat16), "shard", scatter_dimension=0, tiled=True
        ).astype(jnp.float32),
        lax.psum_scatter(
            value_part.astype(jnp.bfloat16), "shard", scatter_dimension=0, tiled=True
        ).astype(jnp.float32),
    )
    joint_grad = jnp.concatenate(
        [query_grad.reshape(row_count, feature_count), key_grad, value_grad], 1
    ).astype(jnp.bfloat16)
    qkv_grad = jnp.dot(owner_order(normed_low).T, joint_grad, preferred_element_type=jnp.float32)
    joint_sums = jnp.sum(joint_grad.astype(jnp.float32), 0)
    qv_bias_grad = owner_order(
        jnp.concatenate([joint_sums[:feature_count], joint_sums[2 * feature_count :]], 0)
    )
    normed_grad = jnp.dot(joint_grad, gathered[2].T, preferred_element_type=jnp.float32)
    unused_three, first_pull = jax.vjp(layer_norm, rows_in, gain_first, shift_first)
    rows_from_norm, gain_first_grad, shift_first_grad = first_pull(normed_grad)
    tokens_grad = middle_grad + rows_from_norm
    attn_sums = settle(
        (
            qkv_grad,
            qv_bias_grad,
            out_grad,
            out_bias_grad,
            owner_order(gain_first_grad),
            owner_order(shift_first_grad),
        )
    )
    return (
        layer_out,
        tokens_grad,
        attn_sums[4],
        attn_sums[5],
        attn_sums[0],
        attn_sums[1],
        attn_sums[2],
        attn_sums[3],
        up_sums[1],
        up_sums[2],
        up_sums[0],
        down_sums[2],
        down_sums[0],
        down_sums[1],
    )


PLANE = 8
DEPTH = 4
QUARTERS = 4
VMEM_BYTES = 48 * 2**20


def is_planes(mesh):
    return mesh.shape["rep"] == PLANE and mesh.shape["shard"] == DEPTH


def over_rep(value, flip):
    return lax.ppermute(value, "rep", [(i, i ^ flip) for i in range(PLANE)])


def over_z(value, step):
    return lax.ppermute(value, "shard", [(i, (i + step) % DEPTH) for i in range(DEPTH)])


def over_all(value, place):
    pairs = [(i, place(i)) for i in range(PLANE * DEPTH) if place(i) is not None]
    return lax.ppermute(value, ("rep", "shard"), pairs)


def home_of(index):
    rep, z = index // DEPTH, index % DEPTH
    return ((rep & 1) * 4 + z) * DEPTH + rep // 2


HOME = [home_of(i) for i in range(PLANE * DEPTH)]


def to_home(value):
    return over_all(value, lambda i: HOME[i])


def from_home(value):
    return over_all(value, HOME.index)


def after(value, *earlier):
    return lax.optimization_barrier((value, *earlier))[0]


def gather_plane(rows):
    beside = [over_rep(rows, flip) for flip in (2, 4, 6)]
    quad = jnp.stack([rows, *beside], 0).reshape(2, 1, 2, *rows.shape)
    return jnp.concatenate([quad, over_rep(quad, 1)], 1).reshape(-1, rows.shape[1])


def scatter_plane(keep, give):
    both = keep.astype(jnp.float32) + over_rep(give, 1).astype(jnp.float32)
    total = both[0, 0]
    for flip, part in ((2, both[0, 1]), (4, both[1, 0]), (6, both[1, 1])):
        total = total + over_rep(part.astype(jnp.bfloat16), flip).astype(jnp.float32)
    return total


def block_at(blocks, index):
    return lax.dynamic_index_in_dim(blocks, index, 0, keepdims=False)


def summed_over_z(blocks):
    z = lax.axis_index("shard")
    low = blocks.astype(jnp.bfloat16)
    total = block_at(blocks, z)
    for step in (1, 2, 3):
        sent = block_at(low, lax.rem(z + step, DEPTH))
        total = total + over_z(sent, step).astype(jnp.float32)
    return total


def outer(left, right):
    return lax.dot_general(
        left, right, (((0,), (0,)), ((), ())), preferred_element_type=jnp.float32
    )


def column_parts_to_rows(grad):
    rows, width = grad.shape
    parts = grad.reshape(PLANE, DEPTH, rows // (PLANE * DEPTH), width)
    summed = summed_over_z(jnp.swapaxes(parts, 0, 1)).astype(jnp.bfloat16)
    arrived = lax.all_to_all(summed, "rep", 0, 0, tiled=True)
    block = rows // (PLANE * DEPTH)
    spread = arrived.reshape(PLANE, block, -1, 128)
    return jnp.transpose(spread, (1, 2, 0, 3)).reshape(block, -1).astype(jnp.float32)


def dot_nn(left, right):
    return jnp.dot(left, right, preferred_element_type=jnp.float32)


def dot_nt(left, right):
    return lax.dot_general(
        left, right, (((1,), (1,)), ((), ())), preferred_element_type=jnp.float32
    )


def place_pieces(pieces, whole, sems):
    z = lax.axis_index("shard")
    rows = pieces[0].shape[0]
    copies = []
    for step, piece in enumerate(pieces):
        plane = lax.rem(z + (DEPTH - step), DEPTH)
        at = pl.ds(pl.multiple_of(plane * rows, rows), rows)
        copies.append(pltpu.make_async_copy(piece, whole.at[at], sems.at[step]))
    for copy in copies:
        copy.start()
    return copies


def wait_all(copies):
    for copy in copies:
        copy.wait()


def row_positions(shape, axis, rep, first):
    index = lax.broadcasted_iota(jnp.int32, shape, axis) + first
    block = index >> 7
    x = (block & 1) ^ ((rep >> 1) & 1)
    core = (block >> 1) ^ (rep & 1)
    return ((x * 2 + core) << 7) + (index & 127)


def scores_of(query, keys, slope, distance, allowed, scale):
    raw = dot_nt(query, keys) * scale - slope * distance
    return jnp.where(allowed, raw, -1e30)


ANYWHERE = pl.BlockSpec(memory_space=pl.ANY)
LOCAL = pl.BlockSpec(memory_space=pltpu.VMEM)
SCALARS = pl.BlockSpec(memory_space=pltpu.SMEM)


def sds(shape, dtype):
    return jax.ShapeDtypeStruct(shape, dtype)


def kernel_call(kernel, ins, outs, scratch, flops, operands):
    return pl.pallas_call(
        kernel,
        out_shape=outs,
        in_specs=ins,
        out_specs=[LOCAL] * len(outs),
        scratch_shapes=scratch,
        compiler_params=pltpu.CompilerParams(vmem_limit_bytes=VMEM_BYTES),
        cost_estimate=pl.CostEstimate(flops=flops, bytes_accessed=2**23, transcendentals=2**20),
    )(*operands)


def attention_forward(lens, slopes, normed, weights, out_part, bias_q, bias_v):
    rows, features = normed.shape
    span = rows // 2
    width = weights[0].shape[1]
    own = width // 3
    head_size = own // 2
    scale = 1.0 / math.sqrt(head_size)
    step_rows = span // QUARTERS

    def kernel(
        lens_ref, slopes_ref, normed_ref, w0, w1, w2, w3, out_ref, bq_ref, bv_ref,
        joint_ref, mixed_ref, keep_ref, give_ref, weight_ref, sems,
    ):
        rep = lax.axis_index("rep")
        wait_all(place_pieces((w0, w1, w2, w3), weight_ref, sems))
        for s in range(2):
            for c in range(2):
                at = pl.ds((2 * s + c) * (span // 2), span // 2)
                joint = dot_nn(normed_ref[at, :], weight_ref[...])
                joint_ref[at, :own] = (joint[:, :own] + bq_ref[...]).astype(jnp.bfloat16)
                joint_ref[at, own : 2 * own] = joint[:, own : 2 * own].astype(jnp.bfloat16)
                joint_ref[at, 2 * own :] = (joint[:, 2 * own :] + bv_ref[...]).astype(jnp.bfloat16)
        lane = lax.broadcasted_iota(jnp.int32, (step_rows, own), 1)
        key_pos = row_positions((1, span), 1, rep, 0)
        for s in range(2):
            keys = joint_ref[pl.ds(s * span, span), own : 2 * own]
            values = joint_ref[pl.ds(s * span, span), 2 * own :]

            @pl.loop(0, QUARTERS)
            def _(i):
                first = pl.multiple_of(i * step_rows, step_rows)
                at = pl.ds(s * span + first, step_rows)
                query_pos = row_positions((step_rows, 1), 0, rep, first)
                allowed = (key_pos <= query_pos) & (key_pos < lens_ref[s])
                distance = (query_pos - key_pos).astype(jnp.float32)
                query = joint_ref[at, :own]
                mixed = jnp.zeros((step_rows, own), jnp.float32)
                for j in range(2):
                    mine = (lane >= j * head_size) & (lane < (j + 1) * head_size)
                    masked = jnp.where(mine, query, jnp.zeros_like(query))
                    scores = scores_of(masked, keys, slopes_ref[j], distance, allowed, scale)
                    top = jnp.max(scores, 1, keepdims=True)
                    exps = jnp.exp(scores - top)
                    probs = exps / jnp.sum(exps, 1, keepdims=True)
                    mixed = jnp.where(mine, dot_nn(probs.astype(jnp.bfloat16), values), mixed)
                mixed_ref[at, :] = mixed.astype(jnp.bfloat16)

            for c, part_ref in enumerate((keep_ref, give_ref)):
                at = pl.ds((2 * s + c) * (span // 2), span // 2)
                part = dot_nn(mixed_ref[at, :], out_ref[...]).astype(jnp.bfloat16)
                part_ref[s] = part.reshape(2, span // 4, features)

    half = sds((2, 2, span // 4, features), jnp.bfloat16)
    return kernel_call(
        kernel,
        [SCALARS, SCALARS, LOCAL] + [ANYWHERE] * 4 + [LOCAL] * 3,
        [sds((rows, width), jnp.bfloat16), sds((rows, own), jnp.bfloat16), half, half],
        [pltpu.VMEM((features, width), jnp.bfloat16), pltpu.SemaphoreType.DMA((DEPTH,))],
        2 * rows * features * (width + own) + 8 * rows * span * own,
        (lens, slopes, normed, *weights, out_part, bias_q, bias_v),
    )


def attention_backward(lens, slopes, grad, joint, weights, out_part):
    rows, features = grad.shape
    span = rows // 2
    width = weights[0].shape[1]
    own = width // 3
    head_size = own // 2
    scale = 1.0 / math.sqrt(head_size)
    step_rows = span // QUARTERS

    def kernel(
        lens_ref, slopes_ref, grad_ref, joint_ref, w0, w1, w2, w3, out_ref,
        joint_grad_ref, sums_ref, keep_ref, give_ref,
        weight_ref, mixed_grad_ref, key_acc, value_acc, sems,
    ):
        rep = lax.axis_index("rep")
        copies = place_pieces((w0, w1, w2, w3), weight_ref, sems)
        for s in range(2):
            for c in range(2):
                at = pl.ds((2 * s + c) * (span // 2), span // 2)
                mixed_grad_ref[at, :] = dot_nt(grad_ref[at, :], out_ref[...]).astype(jnp.bfloat16)
        lane = lax.broadcasted_iota(jnp.int32, (step_rows, own), 1)
        lane_all = lax.broadcasted_iota(jnp.int32, (span, own), 1)
        key_pos = row_positions((1, span), 1, rep, 0)
        for s in range(2):
            keys = joint_ref[pl.ds(s * span, span), own : 2 * own]
            values = joint_ref[pl.ds(s * span, span), 2 * own :]
            key_acc[...] = jnp.zeros_like(key_acc)
            value_acc[...] = jnp.zeros_like(value_acc)

            @pl.loop(0, QUARTERS)
            def _(i):
                first = pl.multiple_of(i * step_rows, step_rows)
                at = pl.ds(s * span + first, step_rows)
                query_pos = row_positions((step_rows, 1), 0, rep, first)
                allowed = (key_pos <= query_pos) & (key_pos < lens_ref[s])
                distance = (query_pos - key_pos).astype(jnp.float32)
                query = joint_ref[at, :own]
                mixed_grad = mixed_grad_ref[at, :]
                query_grad = jnp.zeros((step_rows, own), jnp.float32)
                for j in range(2):
                    mine = (lane >= j * head_size) & (lane < (j + 1) * head_size)
                    masked = jnp.where(mine, query, jnp.zeros_like(query))
                    masked_grad = jnp.where(mine, mixed_grad, jnp.zeros_like(mixed_grad))
                    scores = scores_of(masked, keys, slopes_ref[j], distance, allowed, scale)
                    top = jnp.max(scores, 1, keepdims=True)
                    exps = jnp.exp(scores - top)
                    probs = exps / jnp.sum(exps, 1, keepdims=True)
                    probs_grad = dot_nt(masked_grad, values)
                    row_dot = jnp.sum(probs * probs_grad, 1, keepdims=True)
                    score_grad = (probs * (probs_grad - row_dot)).astype(jnp.bfloat16)
                    query_grad = jnp.where(mine, dot_nn(score_grad, keys), query_grad)
                    key_acc[...] += outer(score_grad, masked)
                    value_acc[...] += outer(probs.astype(jnp.bfloat16), masked_grad)
                joint_grad_ref[at, :own] = (query_grad * scale).astype(jnp.bfloat16)

            at = pl.ds(s * span, span)
            joint_grad_ref[at, own : 2 * own] = (key_acc[...] * scale).astype(jnp.bfloat16)
            joint_grad_ref[at, 2 * own :] = value_acc[...].astype(jnp.bfloat16)
        wait_all(copies)
        total = jnp.zeros((1, width), jnp.float32)
        for s in range(2):
            for c, part_ref in enumerate((keep_ref, give_ref)):
                at = pl.ds((2 * s + c) * (span // 2), span // 2)
                joint_grad = joint_grad_ref[at, :]
                total = total + jnp.sum(joint_grad.astype(jnp.float32), 0, keepdims=True)
                part = dot_nt(joint_grad, weight_ref[...]).astype(jnp.bfloat16)
                part_ref[s] = part.reshape(2, span // 4, features)
        sums_ref[...] = total

    half = sds((2, 2, span // 4, features), jnp.bfloat16)
    return kernel_call(
        kernel,
        [SCALARS, SCALARS, LOCAL, LOCAL] + [ANYWHERE] * 4 + [LOCAL],
        [sds((rows, width), jnp.bfloat16), sds((1, width), jnp.float32), half, half],
        [
            pltpu.VMEM((features, width), jnp.bfloat16),
            pltpu.VMEM((rows, own), jnp.bfloat16),
            pltpu.VMEM((span, own), jnp.float32),
            pltpu.VMEM((span, own), jnp.float32),
            pltpu.SemaphoreType.DMA((DEPTH,)),
        ],
        2 * rows * features * (width + own) + 20 * rows * span * own,
        (lens, slopes, grad, joint, *weights, out_part),
    )


def feed_forward(normed, grad, ups, downs, bias_up):
    rows, features = normed.shape
    units = ups[0].shape[1]
    tile = rows // 4
    root = math.sqrt(2.0 / math.pi)
    bend = 0.044715

    def kernel(
        normed_ref, grad_ref, u0, u1, u2, u3, d0, d1, d2, d3, bias_ref,
        active_ref, hidden_grad_ref, sums_ref, keep_ref, give_ref, back_keep_ref, back_give_ref,
        up_ref, down_ref, sems,
    ):
        up_copies = place_pieces((u0, u1, u2, u3), up_ref, sems.at[0])
        down_copies = place_pieces((d0, d1, d2, d3), down_ref, sems.at[1])
        wait_all(up_copies)
        wait_all(down_copies)
        sums_ref[...] = jnp.zeros_like(sums_ref)

        @pl.loop(0, 2)
        def _(s):
            for c in range(2):
                at = pl.ds(pl.multiple_of((2 * s + c) * tile, tile), tile)
                v = dot_nn(normed_ref[at, :], up_ref[...]) + bias_ref[...]
                square = v * v
                t = jnp.tanh(root * v * (1.0 + bend * square))
                half = 0.5 * (1.0 + t)
                active = (v * half).astype(jnp.bfloat16)
                slope = half + (0.5 * root) * v * (1.0 - t * t) * (1.0 + 3.0 * bend * square)
                active_ref[at, :] = active
                hidden_grad = (dot_nt(grad_ref[at, :], down_ref[...]) * slope).astype(jnp.bfloat16)
                hidden_grad_ref[at, :] = hidden_grad
                sums_ref[...] += jnp.sum(hidden_grad.astype(jnp.float32), 0, keepdims=True)
                part = dot_nn(active, down_ref[...]).astype(jnp.bfloat16)
                (keep_ref, give_ref)[c][s] = part.reshape(2, tile // 2, features)
                back = dot_nt(hidden_grad, up_ref[...]).astype(jnp.bfloat16)
                (back_keep_ref, back_give_ref)[c][s] = back.reshape(2, tile // 2, features)

    half = sds((2, 2, rows // 8, features), jnp.bfloat16)
    wide = sds((rows, units), jnp.bfloat16)
    return kernel_call(
        kernel,
        [LOCAL, LOCAL] + [ANYWHERE] * 8 + [LOCAL],
        [wide, wide, sds((1, units), jnp.float32), half, half, half, half],
        [
            pltpu.VMEM((features, units), jnp.bfloat16),
            pltpu.VMEM((units, features), jnp.bfloat16),
            pltpu.SemaphoreType.DMA((2, DEPTH)),
        ],
        8 * rows * features * units,
        (normed, grad, *ups, *downs, bias_up),
    )


def body_planes(
    tokens,
    cotangent,
    lengths,
    assign,
    first_gain,
    first_shift,
    qkv_weight,
    qv_bias,
    out_weight,
    out_bias,
    second_gain,
    second_shift,
    up_weight,
    up_bias,
    down_weight,
    down_bias,
):
    row_count, feature_count = tokens.shape
    rep = lax.axis_index("rep")
    z = lax.axis_index("shard")
    quarter = rep & 3
    own = feature_count // PLANE

    own_length = jnp.sum(jnp.where(jnp.arange(lengths.shape[0]) == assign[0], lengths, 0))
    ones = jnp.ones((16, feature_count), jnp.float32)
    length_rows = jnp.where(
        jnp.arange(16)[:, None] == 0, ones * (own_length // 16), ones * (own_length % 16)
    )
    moved = to_home(jnp.concatenate([tokens, cotangent, length_rows.astype(jnp.bfloat16)], 0))
    tokens, cotangent = moved[:row_count], moved[row_count : 2 * row_count]
    length_parts = moved[2 * row_count : 2 * row_count + 2, 0].astype(jnp.int32)
    seq_length = 16 * length_parts[0] + length_parts[1]
    other_length = over_rep(seq_length.astype(jnp.float32).reshape(1, 1), 4)
    lens = jnp.stack([seq_length, other_length.astype(jnp.int32)[0, 0]])
    heads = (2 * rep + jnp.arange(2)).astype(jnp.float32)
    slopes = jnp.exp2(-8.0 * (heads + 1.0) / HEADS)

    small = (
        first_gain,
        first_shift,
        qv_bias,
        out_bias,
        second_gain,
        second_shift,
        up_bias,
        down_bias,
    )
    packed = jnp.concatenate([item.reshape(-1, 256) for item in small], 0)
    around = [packed] + [over_z(packed, step) for step in (1, 2, 3)]
    parts = []
    for plane in range(DEPTH):
        back = lax.rem(z + (DEPTH - plane), DEPTH)
        parts.append(
            sum(
                jnp.where(back == step, around[step].astype(jnp.float32), 0.0)
                for step in range(DEPTH)
            )
        )
    stacked = jnp.stack(parts, 0)
    whole_small = []
    start = 0
    for item in small:
        size = item.shape[0] // 256
        whole_small.append(stacked[:, start : start + size].reshape(-1))
        start += size
    (
        gain_first,
        shift_first,
        bias_qv,
        bias_out,
        gain_second,
        shift_second,
        bias_up,
        bias_down,
    ) = whole_small

    def columns(weight):
        blocks = weight.reshape(weight.shape[0], -1, PLANE, 128)
        return lax.dynamic_index_in_dim(blocks, rep, 2, keepdims=False).reshape(weight.shape[0], -1)

    def rows_of(weight, index, count):
        return lax.dynamic_slice_in_dim(weight, index * count, count, 0)

    qkv_own = columns(qkv_weight)
    up_own = columns(up_weight)
    down_own = rows_of(down_weight, rep, down_weight.shape[0] // PLANE)
    out_own = rows_of(out_weight, rep & 1, own)
    qkv_own, up_own, down_own, out_own = lax.optimization_barrier(
        (qkv_own, up_own, down_own, out_own)
    )

    def to_planes(block):
        return [block] + [over_z(block, step) for step in (1, 2, 3)]

    qkv_parts = to_planes(qkv_own)
    out_part = jnp.where(z == rep >> 1, out_own, jnp.zeros_like(out_own))
    for step in (1, 2, 3):
        out_part = out_part + over_all(
            out_own,
            lambda i, step=step: (
                i - i % DEPTH + (i % DEPTH + step) % DEPTH if i % DEPTH == i // 8 else None
            ),
        )
    up_parts = to_planes(up_own)
    down_parts = to_planes(down_own)

    rows_in = tokens.astype(jnp.float32)
    row_valid = (quarter * row_count + jnp.arange(row_count) < seq_length)[:, None]
    seed_grad = jnp.where(row_valid, cotangent.astype(jnp.float32), 0.0)
    branch_grad = seed_grad.astype(jnp.bfloat16)

    normed_low = layer_norm(rows_in, gain_first, shift_first).astype(jnp.bfloat16)
    normed_plane = gather_plane(normed_low)
    bias_blocks = bias_qv.reshape(2, PLANE, own)
    bias_own = lax.dynamic_index_in_dim(bias_blocks, rep, 1, keepdims=False)
    joint, mixed_plane, keep, give = attention_forward(
        lens, slopes, normed_plane, qkv_parts, out_part, bias_own[:1], bias_own[1:]
    )
    branch_grad_plane = gather_plane(branch_grad)
    middle = rows_in + scatter_plane(keep, give) + bias_out
    normed_two_low = layer_norm(middle, gain_second, shift_second).astype(jnp.bfloat16)
    normed_two_plane = gather_plane(normed_two_low)
    bias_up_own = lax.dynamic_index_in_dim(bias_up.reshape(-1, PLANE, 128), rep, 1, keepdims=False)
    active, hidden_grad, hidden_sums, keep, give, back_keep, back_give = feed_forward(
        normed_two_plane, branch_grad_plane, up_parts, down_parts, bias_up_own.reshape(1, -1)
    )
    normed_two_grad = scatter_plane(back_keep, back_give)
    unused_two, second_pull = jax.vjp(layer_norm, middle, gain_second, shift_second)
    middle_from_norm, gain_second_grad, shift_second_grad = second_pull(normed_two_grad)
    middle_grad = seed_grad + middle_from_norm
    attended_grad = middle_grad.astype(jnp.bfloat16)
    attended_grad_plane = gather_plane(attended_grad)
    joint_grad, joint_sums, back_keep, back_give = attention_backward(
        lens, slopes, attended_grad_plane, joint, qkv_parts, out_part
    )
    normed_grad = scatter_plane(back_keep, back_give)
    qkv_grad = column_parts_to_rows(outer(normed_plane, joint_grad))

    branch = scatter_plane(keep, give) + bias_down
    layer_out = from_home((middle + branch).astype(jnp.bfloat16)).astype(jnp.float32)
    down_slice = outer(active, branch_grad_plane).reshape(DEPTH, -1, feature_count)
    down_summed = summed_over_z(down_slice).astype(jnp.bfloat16)
    down_grad = over_all(
        down_summed, lambda i: (2 * (i % DEPTH) + i // 16) * DEPTH + (i // DEPTH) % DEPTH
    ).astype(jnp.float32)
    up_grad = column_parts_to_rows(outer(normed_two_plane, hidden_grad))
    out_slice = outer(mixed_plane, attended_grad_plane)
    out_grad = summed_over_z(out_slice.reshape(DEPTH, -1, feature_count))

    unused_three, first_pull = jax.vjp(layer_norm, rows_in, gain_first, shift_first)
    rows_from_norm, gain_first_grad, shift_first_grad = first_pull(normed_grad)
    tokens_grad = from_home((middle_grad + rows_from_norm).astype(jnp.bfloat16)).astype(jnp.float32)

    at_rep = (jnp.arange(PLANE) == rep)[None, :, None]

    def placed(sums):
        return jnp.where(at_rep, sums.reshape(-1, 1, 128), 0.0).reshape(-1)

    joint_parts = joint_sums.reshape(3, own)
    small_grads = (
        gain_first_grad,
        shift_first_grad,
        placed(jnp.concatenate([joint_parts[:1], joint_parts[2:]], 0)),
        jnp.sum(attended_grad.astype(jnp.float32), 0),
        gain_second_grad,
        shift_second_grad,
        placed(hidden_sums),
        jnp.sum(branch_grad.astype(jnp.float32), 0),
    )
    devices = PLANE * DEPTH
    small_packed = jnp.concatenate(
        [g.reshape(devices, g.shape[0] // devices) for g in small_grads], 1
    ).astype(jnp.bfloat16)
    small_arrived = lax.all_to_all(small_packed, ("rep", "shard"), 0, 0, tiled=True)
    small_sums = jnp.sum(small_arrived.astype(jnp.float32), 0)
    sums = []
    start = 0
    for g in small_grads:
        size = g.shape[0] // devices
        sums.append(small_sums[start : start + size])
        start += size
    return (
        layer_out,
        tokens_grad,
        sums[0],
        sums[1],
        qkv_grad,
        sums[2],
        out_grad,
        sums[3],
        sums[4],
        sums[5],
        up_grad,
        sums[6],
        down_grad,
        sums[7],
    )


def solution(mesh):
    return jax.shard_map(
        body_planes if is_planes(mesh) else body_generic,
        mesh=mesh,
        in_specs=(
            P(("rep", "shard"), None),
            P(("rep", "shard"), None),
            P(),
            P("rep"),
            P("shard"),
            P("shard"),
            P("shard", None),
            P("shard"),
            P("shard", None),
            P("shard"),
            P("shard"),
            P("shard"),
            P("shard", None),
            P("shard"),
            P("shard", None),
            P("shard"),
        ),
        out_specs=(
            P(("rep", "shard"), None),
            P(("rep", "shard"), None),
            P(("rep", "shard")),
            P(("rep", "shard")),
            P(("rep", "shard"), None),
            P(("rep", "shard")),
            P(("rep", "shard"), None),
            P(("rep", "shard")),
            P(("rep", "shard")),
            P(("rep", "shard")),
            P(("rep", "shard"), None),
            P(("rep", "shard")),
            P(("rep", "shard"), None),
            P(("rep", "shard")),
        ),
        check_vma=False,
    )
```

```python
import math

import jax
import jax.numpy as jnp
from jax import lax
from jax.experimental import pallas as pl
from jax.experimental.pallas import tpu as pltpu
from jax.sharding import PartitionSpec as P

HEADS = 16


def for_sending(value):
    return jax.tree.map(lambda a: a.astype(jnp.bfloat16) if a.dtype == jnp.float32 else a, value)


def cut_along(value, dim, devices):
    before, after = (value.shape[:dim], value.shape[dim + 1 :])
    return jnp.moveaxis(value.reshape(*before, devices, -1, *after), dim, 0)


def summed_on_arrival(value, axis, dim):
    blocks = cut_along(value, dim, lax.axis_size(axis))
    arrived = lax.all_to_all(blocks, axis, split_axis=0, concat_axis=0, tiled=True)
    return arrived.astype(jnp.float32).sum(axis=0)


def layer_norm(rows_in, norm_gain, norm_shift):
    row_mean = jnp.mean(rows_in, -1, keepdims=True)
    centered = rows_in - row_mean
    variance = jnp.mean(centered * centered, -1, keepdims=True)
    return centered * lax.rsqrt(variance + 1e-05) * norm_gain + norm_shift


def gelu_tanh(values_in):
    return jax.nn.gelu(values_in, approximate=True)


def owner_order(values):
    rep_count = lax.axis_size("rep")
    shard_count = lax.axis_size("shard")
    lead = values.shape[:-1]
    width = values.shape[-1]
    block = width // (rep_count * shard_count)
    arranged = values.reshape(lead + (rep_count, shard_count, block))
    return jnp.swapaxes(arranged, -3, -2).reshape(lead + (width,))


def settle(grads):
    group_summed = jax.tree.map(
        lambda part: part.astype(jnp.float32),
        lax.psum_scatter(for_sending(grads), "shard", scatter_dimension=0, tiled=True),
    )
    return jax.tree.map(lambda part: summed_on_arrival(part, "rep", 0), for_sending(group_summed))


def head_scores(query_heads, key_heads, query_pos, key_pos, seq_length):
    head_count = query_heads.shape[1]
    score_scale = 1.0 / math.sqrt(query_heads.shape[2])
    slopes = jnp.exp2(-8.0 * (jnp.arange(head_count).astype(jnp.float32) + 1.0) / head_count)
    raw_scores = (
        jnp.einsum("qhd,khd->hqk", query_heads, key_heads, preferred_element_type=jnp.float32)
        * score_scale
    )
    distance = (query_pos[:, None] - key_pos[None, :]).astype(jnp.float32)
    raw_scores = raw_scores - slopes[:, None, None] * distance[None]
    allowed = (key_pos[None, :] <= query_pos[:, None]) & (key_pos[None, :] < seq_length)
    return jnp.where(allowed[None], raw_scores, -1e30)


def body_generic(
    tokens,
    cotangent,
    lengths,
    assign,
    first_gain,
    first_shift,
    qkv_weight,
    qv_bias,
    out_weight,
    out_bias,
    second_gain,
    second_shift,
    up_weight,
    up_bias,
    down_weight,
    down_bias,
):
    rows_in = tokens.astype(jnp.float32)
    row_count = rows_in.shape[0]
    feature_count = rows_in.shape[1]
    head_count = HEADS
    head_size = feature_count // head_count
    score_scale = 1.0 / math.sqrt(head_size)
    group_size = row_count * lax.axis_size("shard")
    seq_length = jnp.sum(jnp.where(jnp.arange(lengths.shape[0]) == assign[0], lengths, 0))
    query_pos = lax.axis_index("shard") * row_count + jnp.arange(row_count)
    key_pos = jnp.arange(group_size)
    row_valid = (query_pos < seq_length)[:, None]
    owned = (
        first_gain,
        first_shift,
        qkv_weight,
        qv_bias,
        out_weight,
        out_bias,
        second_gain,
        second_shift,
        up_weight,
        up_bias,
        down_weight,
        down_bias,
    )
    gathered = (
        lax.all_gather(owned[0], "shard", axis=0, tiled=True),
        lax.all_gather(owned[1], "shard", axis=0, tiled=True),
        lax.all_gather(owned[2], "shard", axis=0, tiled=True),
        lax.all_gather(owned[3], "shard", axis=0, tiled=True),
        lax.all_gather(owned[4], "shard", axis=0, tiled=True),
        lax.all_gather(owned[5], "shard", axis=0, tiled=True),
        lax.all_gather(owned[6], "shard", axis=0, tiled=True),
        lax.all_gather(owned[7], "shard", axis=0, tiled=True),
        lax.all_gather(owned[8], "shard", axis=0, tiled=True),
        lax.all_gather(owned[9], "shard", axis=0, tiled=True),
        lax.all_gather(owned[10], "shard", axis=0, tiled=True),
        lax.all_gather(owned[11], "shard", axis=0, tiled=True),
    )
    gain_first = gathered[0].astype(jnp.float32)
    shift_first = gathered[1].astype(jnp.float32)
    bias_qv = gathered[3].astype(jnp.float32)
    bias_out = gathered[5].astype(jnp.float32)
    gain_second = gathered[6].astype(jnp.float32)
    shift_second = gathered[7].astype(jnp.float32)
    bias_up = gathered[9].astype(jnp.float32)
    bias_down = gathered[11].astype(jnp.float32)
    normed = layer_norm(rows_in, gain_first, shift_first)
    normed_low = normed.astype(jnp.bfloat16)
    joint_out = jnp.dot(normed_low, gathered[2], preferred_element_type=jnp.float32)
    query_low = (joint_out[:, :feature_count] + bias_qv[:feature_count]).astype(jnp.bfloat16)
    key_low = joint_out[:, feature_count : 2 * feature_count].astype(jnp.bfloat16)
    value_low = (joint_out[:, 2 * feature_count :] + bias_qv[feature_count:]).astype(jnp.bfloat16)
    key_all, value_all = (
        lax.all_gather(key_low, "shard", axis=0, tiled=True),
        lax.all_gather(value_low, "shard", axis=0, tiled=True),
    )
    query_heads = query_low.reshape(row_count, head_count, head_size)
    scores = head_scores(
        query_heads,
        key_all.reshape(group_size, head_count, head_size),
        query_pos,
        key_pos,
        seq_length,
    )
    row_top = jnp.max(scores, -1, keepdims=True)
    exp_scores = jnp.exp(scores - row_top)
    row_total = jnp.sum(exp_scores, -1, keepdims=True)
    log_total = row_top + jnp.log(row_total)
    attn_probs = exp_scores / row_total
    mixed_low = (
        jnp.einsum(
            "hqk,khd->qhd",
            attn_probs.astype(jnp.bfloat16),
            value_all.reshape(group_size, head_count, head_size),
            preferred_element_type=jnp.float32,
        )
        .reshape(row_count, feature_count)
        .astype(jnp.bfloat16)
    )
    attended = jnp.dot(mixed_low, gathered[4], preferred_element_type=jnp.float32) + bias_out
    middle = rows_in + attended
    normed_two_low = layer_norm(middle, gain_second, shift_second).astype(jnp.bfloat16)
    hidden = jnp.dot(normed_two_low, gathered[8], preferred_element_type=jnp.float32) + bias_up
    active_low = gelu_tanh(hidden).astype(jnp.bfloat16)
    branch = jnp.dot(active_low, gathered[10], preferred_element_type=jnp.float32) + bias_down
    layer_out = middle + branch
    back_keys = (key_all, value_all)
    key_heads_back = back_keys[0].reshape(group_size, head_count, head_size)
    value_heads_back = back_keys[1].reshape(group_size, head_count, head_size)
    seed_grad = jnp.where(row_valid, cotangent.astype(jnp.float32), 0.0)
    branch_grad = seed_grad.astype(jnp.bfloat16)
    down_grad = jnp.dot(owner_order(active_low).T, branch_grad, preferred_element_type=jnp.float32)
    down_bias_grad = owner_order(jnp.sum(branch_grad.astype(jnp.float32), 0))
    active_grad = jnp.dot(branch_grad, gathered[10].T, preferred_element_type=jnp.float32)
    unused, gelu_pull = jax.vjp(gelu_tanh, hidden)
    hidden_grad = gelu_pull(active_grad)[0].astype(jnp.bfloat16)
    up_grad = jnp.dot(
        owner_order(normed_two_low).T, hidden_grad, preferred_element_type=jnp.float32
    )
    up_bias_grad = owner_order(jnp.sum(hidden_grad.astype(jnp.float32), 0))
    normed_two_grad = jnp.dot(hidden_grad, gathered[8].T, preferred_element_type=jnp.float32)
    unused_two, second_pull = jax.vjp(layer_norm, middle, gain_second, shift_second)
    middle_from_norm, gain_second_grad, shift_second_grad = second_pull(normed_two_grad)
    middle_grad = seed_grad + middle_from_norm
    down_sums = settle((down_grad, down_bias_grad, up_bias_grad))
    up_sums = settle((up_grad, owner_order(gain_second_grad), owner_order(shift_second_grad)))
    attended_grad = middle_grad.astype(jnp.bfloat16)
    out_grad = jnp.dot(owner_order(mixed_low).T, attended_grad, preferred_element_type=jnp.float32)
    out_bias_grad = owner_order(jnp.sum(attended_grad.astype(jnp.float32), 0))
    mixed_grad = (
        jnp.dot(attended_grad, gathered[4].T, preferred_element_type=jnp.float32)
        .astype(jnp.bfloat16)
        .reshape(row_count, head_count, head_size)
    )
    scores_back = head_scores(query_heads, key_heads_back, query_pos, key_pos, seq_length)
    probs_back = jnp.exp(scores_back - log_total)
    probs_grad = jnp.einsum(
        "qhd,khd->hqk", mixed_grad, value_heads_back, preferred_element_type=jnp.float32
    )
    value_part = jnp.einsum(
        "hqk,qhd->khd",
        probs_back.astype(jnp.bfloat16),
        mixed_grad,
        preferred_element_type=jnp.float32,
    ).reshape(group_size, feature_count)
    row_dot = jnp.sum(probs_back * probs_grad, -1, keepdims=True)
    score_grad = (probs_back * (probs_grad - row_dot)).astype(jnp.bfloat16)
    query_grad = (
        jnp.einsum("hqk,khd->qhd", score_grad, key_heads_back, preferred_element_type=jnp.float32)
        * score_scale
    )
    key_part = (
        jnp.einsum(
            "hqk,qhd->khd", score_grad, query_heads, preferred_element_type=jnp.float32
        ).reshape(group_size, feature_count)
        * score_scale
    )
    key_grad, value_grad = (
        lax.psum_scatter(
            key_part.astype(jnp.bfloat16), "shard", scatter_dimension=0, tiled=True
        ).astype(jnp.float32),
        lax.psum_scatter(
            value_part.astype(jnp.bfloat16), "shard", scatter_dimension=0, tiled=True
        ).astype(jnp.float32),
    )
    joint_grad = jnp.concatenate(
        [query_grad.reshape(row_count, feature_count), key_grad, value_grad], 1
    ).astype(jnp.bfloat16)
    qkv_grad = jnp.dot(owner_order(normed_low).T, joint_grad, preferred_element_type=jnp.float32)
    joint_sums = jnp.sum(joint_grad.astype(jnp.float32), 0)
    qv_bias_grad = owner_order(
        jnp.concatenate([joint_sums[:feature_count], joint_sums[2 * feature_count :]], 0)
    )
    normed_grad = jnp.dot(joint_grad, gathered[2].T, preferred_element_type=jnp.float32)
    unused_three, first_pull = jax.vjp(layer_norm, rows_in, gain_first, shift_first)
    rows_from_norm, gain_first_grad, shift_first_grad = first_pull(normed_grad)
    tokens_grad = middle_grad + rows_from_norm
    attn_sums = settle(
        (
            qkv_grad,
            qv_bias_grad,
            out_grad,
            out_bias_grad,
            owner_order(gain_first_grad),
            owner_order(shift_first_grad),
        )
    )
    return (
        layer_out,
        tokens_grad,
        attn_sums[4],
        attn_sums[5],
        attn_sums[0],
        attn_sums[1],
        attn_sums[2],
        attn_sums[3],
        up_sums[1],
        up_sums[2],
        up_sums[0],
        down_sums[2],
        down_sums[0],
        down_sums[1],
    )


PLANE = 8
DEPTH = 4
QUARTERS = 4
VMEM_BYTES = 60 * 2**20
ORDER = (0, 2, 1, 3, 4, 6, 5, 7)


def is_planes(mesh):
    return mesh.shape["rep"] == PLANE and mesh.shape["shard"] == DEPTH


def over_rep(value, flip):
    return lax.ppermute(value, "rep", [(i, i ^ flip) for i in range(PLANE)])


def over_z(value, step):
    return lax.ppermute(value, "shard", [(i, (i + step) % DEPTH) for i in range(DEPTH)])


def over_all(value, place):
    pairs = [(i, place(i)) for i in range(PLANE * DEPTH) if place(i) is not None]
    return lax.ppermute(value, ("rep", "shard"), pairs)


def home_of(index):
    rep, z = index // DEPTH, index % DEPTH
    y, x, core = rep >> 2, (rep >> 1) & 1, rep & 1
    return (4 * x + 2 * (z & 1) + (z >> 1)) * DEPTH + 2 * core + y


HOME = [home_of(i) for i in range(PLANE * DEPTH)]


def to_home(value):
    return over_all(value, lambda i: HOME[i])


def from_home(value):
    return over_all(value, HOME.index)


def after(value, *earlier):
    return lax.optimization_barrier((value, *earlier))[0]


def gather_plane(rows):
    near = over_rep(rows, 1)
    two, four, six = (over_rep(rows, flip) for flip in (2, 4, 6))
    return [rows, near, two, over_rep(two, 1), four, over_rep(four, 1), six, over_rep(six, 1)]


def add_halves(keep, received):
    count, features = keep.shape[2:]

    def kernel(keep_ref, received_ref, own_ref, two_ref, four_ref, six_ref, left, right, sems):
        outs = {0: own_ref, 2: two_ref, 4: four_ref, 6: six_ref}
        copies = {}
        for flip in (6, 2, 4, 0):
            y, x = flip >> 2, (flip >> 1) & 1
            copies[flip] = [
                pltpu.make_async_copy(ref.at[y, x], to.at[y, x], sems.at[i, flip // 2])
                for i, (ref, to) in enumerate(((keep_ref, left), (received_ref, right)))
            ]
            for copy in copies[flip]:
                copy.start()
        for flip in (6, 2, 4, 0):
            y, x = flip >> 2, (flip >> 1) & 1
            wait_all(copies[flip])
            total = left[y, x].astype(jnp.float32) + right[y, x].astype(jnp.float32)
            outs[flip][...] = total.astype(outs[flip].dtype)

    low = sds((count, features), jnp.bfloat16)
    return kernel_call(
        kernel,
        [ANYWHERE] * 2,
        [sds((count, features), jnp.float32), low, low, low],
        [
            pltpu.VMEM(keep.shape, keep.dtype),
            pltpu.VMEM(keep.shape, keep.dtype),
            pltpu.SemaphoreType.DMA((2, 4)),
        ],
        0,
        (keep, received),
    )


def send_parts(parts):
    own, *others = parts
    return [own] + [over_rep(part, flip) for part, flip in zip(others, (2, 4, 6))]


def scattered_over_z(blocks):
    return lax.psum_scatter(blocks, "shard", scatter_dimension=0, tiled=False)


def outer(left, right):
    return lax.dot_general(
        left, right, (((0,), (0,)), ((), ())), preferred_element_type=jnp.float32
    )


def columns_to_rows(parts):
    arrived = lax.all_to_all(parts, "rep", 0, 0, tiled=True)
    spread = arrived.reshape(PLANE, parts.shape[1], -1, 128)
    return jnp.transpose(spread, (1, 2, 0, 3)).reshape(parts.shape[1], -1).astype(jnp.float32)


def dot_nn(left, right):
    return jnp.dot(left, right, preferred_element_type=jnp.float32)


def dot_nt(left, right):
    return lax.dot_general(
        left, right, (((1,), (1,)), ((), ())), preferred_element_type=jnp.float32
    )


def place_pieces(pieces, whole, sems):
    z = lax.axis_index("shard")
    rows = pieces[0].shape[0]
    copies = []
    for step, piece in enumerate(pieces):
        plane = lax.rem(z + (DEPTH - step), DEPTH)
        at = pl.ds(pl.multiple_of(plane * rows, rows), rows)
        copies.append(pltpu.make_async_copy(piece, whole.at[at], sems.at[step]))
    for copy in copies:
        copy.start()
    return copies


def wait_all(copies):
    for copy in copies:
        copy.wait()


def quarter_of(rep):
    return 2 * (rep & 1) + ((rep >> 1) & 1)


def row_positions(shape, axis, rep, first):
    index = lax.broadcasted_iota(jnp.int32, shape, axis) + first
    return (((index >> 7) ^ quarter_of(rep)) << 7) + (index & 127)


def load_blocks(blocks, whole, sems):
    count = blocks[0].shape[0]
    copies = []
    for place, k in enumerate(ORDER):
        at = pl.ds(place * count, count)
        copies.append(pltpu.make_async_copy(blocks[k], whole.at[at], sems.at[place]))
        copies[-1].start()
    return copies


def load(ref, to, sem):
    copy = pltpu.make_async_copy(ref, to, sem)
    copy.start()
    return copy


def total_of(parts):
    own, two, four, six = parts
    return (own[...] + two[...].astype(jnp.float32)) + (
        four[...].astype(jnp.float32) + six[...].astype(jnp.float32)
    )


def unit_rows(v):
    centered = v - jnp.mean(v, 1, keepdims=True)
    rstd = lax.rsqrt(jnp.mean(centered * centered, 1, keepdims=True) + 1e-05)
    return centered * rstd, rstd


def norm_back(grad, xhat, rstd, gain):
    gx = grad * gain
    return rstd * (
        gx - jnp.mean(gx, 1, keepdims=True) - xhat * jnp.mean(gx * xhat, 1, keepdims=True)
    )


def scores_of(query, keys, slope, distance, allowed, scale):
    raw = dot_nt(query, keys) * scale - slope * distance
    return jnp.where(allowed, raw, -1e30)


VECTORS = ((0, 256), (1, 256), (6, 512), (2, 256), (3, 256), (4, 256), (8, 1024), (5, 256))
ANYWHERE = pl.BlockSpec(memory_space=pl.ANY)
LOCAL = pl.BlockSpec(memory_space=pltpu.VMEM)
SCALARS = pl.BlockSpec(memory_space=pltpu.SMEM)


def sds(shape, dtype):
    return jax.ShapeDtypeStruct(shape, dtype)


def kernel_call(kernel, ins, outs, scratch, flops, operands):
    return pl.pallas_call(
        kernel,
        out_shape=outs,
        in_specs=ins,
        out_specs=[LOCAL] * len(outs),
        scratch_shapes=scratch,
        compiler_params=pltpu.CompilerParams(vmem_limit_bytes=VMEM_BYTES),
        cost_estimate=pl.CostEstimate(flops=flops, bytes_accessed=2**23, transcendentals=2**20),
    )(*operands)


def own_eighths(qkv_weight, out_weight, up_weight, down_weight):
    def kernel(qkv_ref, out_ref, up_ref, down_ref, qkv_own, out_own, up_own, down_own, sems):
        rep = lax.axis_index("rep")
        moves = []
        for ref, own_ref in ((qkv_ref, qkv_own), (up_ref, up_own)):
            for j in range(own_ref.shape[1] // 128):
                at = pl.ds(pl.multiple_of(1024 * j + 128 * rep, 128), 128)
                moves.append((ref.at[:, at], own_ref.at[:, pl.ds(128 * j, 128)]))
        for ref, own_ref, index in ((out_ref, out_own, rep & 1), (down_ref, down_own, rep)):
            count = own_ref.shape[0]
            at = pl.ds(pl.multiple_of(index * count, count), count)
            moves.append((ref.at[at, :], own_ref))
        copies = [
            pltpu.make_async_copy(src, dst, sems.at[i]) for i, (src, dst) in enumerate(moves)
        ]
        for copy in copies:
            copy.start()
        wait_all(copies)

    height, features = qkv_weight.shape[0], out_weight.shape[1]
    low = jnp.bfloat16
    return kernel_call(
        kernel,
        [ANYWHERE] * 4,
        [
            sds((height, qkv_weight.shape[1] // PLANE), low),
            sds((features // PLANE, features), low),
            sds((height, up_weight.shape[1] // PLANE), low),
            sds((down_weight.shape[0] // PLANE, features), low),
        ],
        [pltpu.SemaphoreType.DMA((9,))],
        0,
        (qkv_weight, out_weight, up_weight, down_weight),
    )


def first_norm(tokens, packs):
    def kernel(tokens_ref, p0, p1, p2, p3, vectors_ref, normed_ref):
        z = lax.axis_index("shard")
        packs = [ref[...].astype(jnp.float32) for ref in (p0, p1, p2, p3)]
        vectors_ref[...] = jnp.zeros_like(vectors_ref)
        for plane in range(DEPTH):
            back = lax.rem(z + (DEPTH - plane), DEPTH)
            pack = packs[3]
            for step in range(3):
                pack = jnp.where(back == step, packs[step], pack)
            start = 0
            for row, size in VECTORS:
                for i in range(size // 128):
                    at = plane * size + i * 128
                    lanes = pl.ds(at % 1024, 128)
                    vectors_ref[row + at // 1024 : row + at // 1024 + 1, lanes] = pack[
                        start + i : start + i + 1
                    ]
                start += size // 128
        xhat, unused = unit_rows(tokens_ref[...].astype(jnp.float32))
        normed = xhat * vectors_ref[0:1, :] + vectors_ref[1:2, :]
        normed_ref[...] = normed.astype(jnp.bfloat16)

    return kernel_call(
        kernel,
        [LOCAL] * 5,
        [sds((16, tokens.shape[1]), jnp.float32), sds(tokens.shape, jnp.bfloat16)],
        [],
        0,
        (tokens, *packs),
    )


def second_norm(tokens, vectors, parts):
    def kernel(tokens_ref, vectors_ref, own, two, four, six, middle_ref, normed_ref):
        attended = total_of((own, two, four, six)) + vectors_ref[2:3, :]
        middle = tokens_ref[...].astype(jnp.float32) + attended
        middle_ref[...] = middle
        xhat, unused = unit_rows(middle)
        normed = xhat * vectors_ref[3:4, :] + vectors_ref[4:5, :]
        normed_ref[...] = normed.astype(jnp.bfloat16)

    return kernel_call(
        kernel,
        [LOCAL] * 6,
        [sds(tokens.shape, jnp.float32), sds(tokens.shape, jnp.bfloat16)],
        [],
        0,
        (tokens, vectors, *parts),
    )


def second_norm_back(lens, vectors, middle, cotangent, parts):
    rows, features = middle.shape

    def kernel(
        lens_ref, vectors_ref, middle_ref, cotangent_ref, own, two, four, six,
        grad_ref, low_ref, sums_ref,
    ):
        first = quarter_of(lax.axis_index("rep")) * rows
        position = lax.broadcasted_iota(jnp.int32, (rows, 1), 0) + first
        seed = cotangent_ref[...].astype(jnp.float32)
        seed = jnp.where(position < lens_ref[0], seed, 0.0)
        grad = total_of((own, two, four, six))
        xhat, rstd = unit_rows(middle_ref[...])
        total = seed + norm_back(grad, xhat, rstd, vectors_ref[3:4, :])
        grad_ref[...] = total
        low = total.astype(jnp.bfloat16)
        low_ref[...] = low
        sums_ref[0:1, :] = jnp.sum(grad * xhat, 0, keepdims=True)
        sums_ref[1:2, :] = jnp.sum(grad, 0, keepdims=True)
        sums_ref[2:3, :] = jnp.sum(low.astype(jnp.float32), 0, keepdims=True)
        sums_ref[3:4, :] = jnp.sum(seed, 0, keepdims=True)

    return kernel_call(
        kernel,
        [SCALARS] + [LOCAL] * 7,
        [
            sds((rows, features), jnp.float32),
            sds((rows, features), jnp.bfloat16),
            sds((4, features), jnp.float32),
        ],
        [],
        0,
        (lens, vectors, middle, cotangent, *parts),
    )


def first_norm_back(tokens, vectors, middle_grad, parts):
    rows, features = tokens.shape

    def kernel(tokens_ref, vectors_ref, base_ref, own, two, four, six, grad_ref, sums_ref):
        grad = total_of((own, two, four, six))
        xhat, rstd = unit_rows(tokens_ref[...].astype(jnp.float32))
        total = base_ref[...] + norm_back(grad, xhat, rstd, vectors_ref[0:1, :])
        grad_ref[...] = total.astype(jnp.bfloat16)
        sums_ref[0:1, :] = jnp.sum(grad * xhat, 0, keepdims=True)
        sums_ref[1:2, :] = jnp.sum(grad, 0, keepdims=True)

    return kernel_call(
        kernel,
        [LOCAL] * 7,
        [sds((rows, features), jnp.bfloat16), sds((2, features), jnp.float32)],
        [],
        0,
        (tokens, vectors, middle_grad, *parts),
    )


def attention_forward(lens, slopes, blocks, weights, out_part, vectors):
    rows, features = PLANE * blocks[0].shape[0], blocks[0].shape[1]
    span = rows // 2
    width = weights[0].shape[1]
    own = width // 3
    head_size = own // 2
    scale = 1.0 / math.sqrt(head_size)
    step_rows = span // QUARTERS

    def kernel(
        lens_ref, slopes_ref, n0, n1, n2, n3, n4, n5, n6, n7, w0, w1, w2, w3, out_ref, vectors_ref,
        joint_ref, mixed_ref, keep_ref, give_ref, weight_ref, normed_ref, out_all, sems, more_sems,
    ):
        rep = lax.axis_index("rep")
        weight_copies = place_pieces((w0, w1, w2, w3), weight_ref, sems)
        copies = load_blocks((n0, n1, n2, n3, n4, n5, n6, n7), normed_ref, more_sems)
        out_copy = load(out_ref, out_all, sems.at[DEPTH])
        mine = pl.ds(pl.multiple_of(rep * own, own), own)
        bias_q, bias_v = vectors_ref[6:7, mine], vectors_ref[7:8, mine]
        wait_all(weight_copies)
        for s in range(2):
            for c in range(2):
                at = pl.ds((2 * s + c) * (span // 2), span // 2)
                wait_all(copies[4 * s + 2 * c : 4 * s + 2 * c + 2])
                joint = dot_nn(normed_ref[at, :], weight_ref[...])
                joint_ref[at, :own] = (joint[:, :own] + bias_q).astype(jnp.bfloat16)
                joint_ref[at, own : 2 * own] = joint[:, own : 2 * own].astype(jnp.bfloat16)
                joint_ref[at, 2 * own :] = (joint[:, 2 * own :] + bias_v).astype(jnp.bfloat16)
        lane = lax.broadcasted_iota(jnp.int32, (step_rows, own), 1)
        key_pos = row_positions((1, span), 1, rep, 0)
        for s in range(2):
            keys = joint_ref[pl.ds(s * span, span), own : 2 * own]
            values = joint_ref[pl.ds(s * span, span), 2 * own :]

            @pl.loop(0, QUARTERS)
            def _(i):
                first = pl.multiple_of(i * step_rows, step_rows)
                at = pl.ds(s * span + first, step_rows)
                query_pos = row_positions((step_rows, 1), 0, rep, first)
                allowed = (key_pos <= query_pos) & (key_pos < lens_ref[s])
                distance = (query_pos - key_pos).astype(jnp.float32)
                query = joint_ref[at, :own]
                mixed = jnp.zeros((step_rows, own), jnp.float32)
                for j in range(2):
                    mine = (lane >= j * head_size) & (lane < (j + 1) * head_size)
                    masked = jnp.where(mine, query, jnp.zeros_like(query))
                    scores = scores_of(masked, keys, slopes_ref[j], distance, allowed, scale)
                    top = jnp.max(scores, 1, keepdims=True)
                    exps = jnp.exp(scores - top)
                    probs = exps / jnp.sum(exps, 1, keepdims=True)
                    mixed = jnp.where(mine, dot_nn(probs.astype(jnp.bfloat16), values), mixed)
                mixed_ref[at, :] = mixed.astype(jnp.bfloat16)

            if s == 0:
                out_copy.wait()
            for c, part_ref in enumerate((keep_ref, give_ref)):
                at = pl.ds((2 * s + c) * (span // 2), span // 2)
                part = dot_nn(mixed_ref[at, :], out_all[...]).astype(jnp.bfloat16)
                part_ref[s] = part.reshape(2, span // 4, features)

    half = sds((2, 2, span // 4, features), jnp.bfloat16)
    return kernel_call(
        kernel,
        [SCALARS] * 2 + [ANYWHERE] * 13 + [LOCAL],
        [sds((rows, width), jnp.bfloat16), sds((rows, own), jnp.bfloat16), half, half],
        [
            pltpu.VMEM((features, width), jnp.bfloat16),
            pltpu.VMEM((rows, features), jnp.bfloat16),
            pltpu.VMEM((own, features), jnp.bfloat16),
            pltpu.SemaphoreType.DMA((DEPTH + 1,)),
            pltpu.SemaphoreType.DMA((PLANE,)),
        ],
        2 * rows * features * (width + own) + 8 * rows * span * own,
        (lens, slopes, *blocks, *weights, out_part, vectors),
    )


def attention_backward(lens, slopes, blocks, joint, weights, out_part):
    rows, features = PLANE * blocks[0].shape[0], blocks[0].shape[1]
    span = rows // 2
    width = weights[0].shape[1]
    own = width // 3
    head_size = own // 2
    scale = 1.0 / math.sqrt(head_size)
    step_rows = span // QUARTERS

    def kernel(
        lens_ref, slopes_ref, g0, g1, g2, g3, g4, g5, g6, g7, joint_hbm, w0, w1, w2, w3, out_ref,
        joint_grad_ref, sums_ref, keep_ref, give_ref,
        weight_ref, mixed_grad_ref, key_acc, value_acc, joint_ref, grad_ref, out_all, sems, more_sems,
    ):
        rep = lax.axis_index("rep")
        out_copy = load(out_ref, out_all, sems.at[DEPTH])
        grad_copies = load_blocks((g0, g1, g2, g3, g4, g5, g6, g7), grad_ref, more_sems)
        joint_copy = load(joint_hbm, joint_ref, sems.at[DEPTH + 1])
        copies = place_pieces((w0, w1, w2, w3), weight_ref, sems)
        out_copy.wait()
        for s in range(2):
            for c in range(2):
                at = pl.ds((2 * s + c) * (span // 2), span // 2)
                wait_all(grad_copies[4 * s + 2 * c : 4 * s + 2 * c + 2])
                mixed_grad = dot_nt(grad_ref[at, :], out_all[...])
                mixed_grad_ref[at, :] = mixed_grad.astype(jnp.bfloat16)
        joint_copy.wait()
        lane = lax.broadcasted_iota(jnp.int32, (step_rows, own), 1)
        lane_all = lax.broadcasted_iota(jnp.int32, (span, own), 1)
        key_pos = row_positions((1, span), 1, rep, 0)
        for s in range(2):
            keys = joint_ref[pl.ds(s * span, span), own : 2 * own]
            values = joint_ref[pl.ds(s * span, span), 2 * own :]
            key_acc[...] = jnp.zeros_like(key_acc)
            value_acc[...] = jnp.zeros_like(value_acc)

            @pl.loop(0, QUARTERS)
            def _(i):
                first = pl.multiple_of(i * step_rows, step_rows)
                at = pl.ds(s * span + first, step_rows)
                query_pos = row_positions((step_rows, 1), 0, rep, first)
                allowed = (key_pos <= query_pos) & (key_pos < lens_ref[s])
                distance = (query_pos - key_pos).astype(jnp.float32)
                query = joint_ref[at, :own]
                mixed_grad = mixed_grad_ref[at, :]
                query_grad = jnp.zeros((step_rows, own), jnp.float32)
                for j in range(2):
                    mine = (lane >= j * head_size) & (lane < (j + 1) * head_size)
                    masked = jnp.where(mine, query, jnp.zeros_like(query))
                    masked_grad = jnp.where(mine, mixed_grad, jnp.zeros_like(mixed_grad))
                    scores = scores_of(masked, keys, slopes_ref[j], distance, allowed, scale)
                    top = jnp.max(scores, 1, keepdims=True)
                    exps = jnp.exp(scores - top)
                    probs = exps / jnp.sum(exps, 1, keepdims=True)
                    probs_grad = dot_nt(masked_grad, values)
                    row_dot = jnp.sum(probs * probs_grad, 1, keepdims=True)
                    score_grad = (probs * (probs_grad - row_dot)).astype(jnp.bfloat16)
                    query_grad = jnp.where(mine, dot_nn(score_grad, keys), query_grad)
                    key_acc[...] += outer(score_grad, masked)
                    value_acc[...] += outer(probs.astype(jnp.bfloat16), masked_grad)
                joint_grad_ref[at, :own] = (query_grad * scale).astype(jnp.bfloat16)

            at = pl.ds(s * span, span)
            joint_grad_ref[at, own : 2 * own] = (key_acc[...] * scale).astype(jnp.bfloat16)
            joint_grad_ref[at, 2 * own :] = value_acc[...].astype(jnp.bfloat16)
        wait_all(copies)
        total = jnp.zeros((1, width), jnp.float32)
        for s in range(2):
            for c, part_ref in enumerate((keep_ref, give_ref)):
                at = pl.ds((2 * s + c) * (span // 2), span // 2)
                joint_grad = joint_grad_ref[at, :]
                total = total + jnp.sum(joint_grad.astype(jnp.float32), 0, keepdims=True)
                part = dot_nt(joint_grad, weight_ref[...]).astype(jnp.bfloat16)
                part_ref[s] = part.reshape(2, span // 4, features)
        sums_ref[...] = total

    half = sds((2, 2, span // 4, features), jnp.bfloat16)
    return kernel_call(
        kernel,
        [SCALARS] * 2 + [ANYWHERE] * 14,
        [sds((rows, width), jnp.bfloat16), sds((1, width), jnp.float32), half, half],
        [
            pltpu.VMEM((features, width), jnp.bfloat16),
            pltpu.VMEM((rows, own), jnp.bfloat16),
            pltpu.VMEM((span, own), jnp.float32),
            pltpu.VMEM((span, own), jnp.float32),
            pltpu.VMEM((rows, width), jnp.bfloat16),
            pltpu.VMEM((rows, features), jnp.bfloat16),
            pltpu.VMEM((own, features), jnp.bfloat16),
            pltpu.SemaphoreType.DMA((DEPTH + 2,)),
            pltpu.SemaphoreType.DMA((PLANE,)),
        ],
        2 * rows * features * (width + own) + 20 * rows * span * own,
        (lens, slopes, *blocks, joint, *weights, out_part),
    )


def feed_forward(blocks, grad, ups, down, vectors):
    count, features = blocks[0].shape
    rows = PLANE * count
    units = ups[0].shape[1]
    tile = 2 * count
    root = math.sqrt(2.0 / math.pi)
    bend = 0.044715

    def kernel(
        n0, n1, n2, n3, n4, n5, n6, n7, grad_hbm, u0, u1, u2, u3, down_hbm, vectors_ref,
        active_ref, hidden_grad_ref, sums_ref, branch_keep_ref, branch_give_ref, keep_ref, give_ref,
        up_ref, down_ref, normed_ref, grad_ref, sems, more_sems,
    ):
        rep = lax.axis_index("rep")
        up_copies = place_pieces((u0, u1, u2, u3), up_ref, more_sems)
        copies = load_blocks((n0, n1, n2, n3, n4, n5, n6, n7), normed_ref, sems)
        down_copy = load(down_hbm, down_ref, more_sems.at[DEPTH])
        grad_copy = load(grad_hbm, grad_ref, more_sems.at[DEPTH + 1])
        mine = pl.ds(pl.multiple_of(rep * 128, 128), 128)
        bias = jnp.concatenate([vectors_ref[8 + p : 9 + p, mine] for p in range(DEPTH)], 1)
        total = jnp.zeros((1, units), jnp.float32)
        for s in range(2):
            for c in range(2):
                sources = [rep ^ (4 * s + 2 * x + c) for x in range(2)]
                at = pl.ds((2 * s + c) * tile, tile)
                if (s, c) == (0, 0):
                    wait_all(up_copies)
                wait_all(copies[4 * s + 2 * c : 4 * s + 2 * c + 2])
                v = dot_nn(normed_ref[at, :], up_ref[...]) + bias
                square = v * v
                t = jnp.tanh(root * v * (1.0 + bend * square))
                half = 0.5 * (1.0 + t)
                active = (v * half).astype(jnp.bfloat16)
                slope = half + (0.5 * root) * v * (1.0 - t * t) * (1.0 + 3.0 * bend * square)
                if (s, c) == (0, 0):
                    grad_copy.wait()
                    down_copy.wait()
                grad = jnp.concatenate([grad_ref[source] for source in sources], 0)
                hidden_grad = (dot_nt(grad, down_ref[...]) * slope).astype(jnp.bfloat16)
                hidden_grad_ref[at, :] = hidden_grad
                total = total + jnp.sum(hidden_grad.astype(jnp.float32), 0, keepdims=True)
                back = dot_nt(hidden_grad, up_ref[...]).astype(jnp.bfloat16)
                (keep_ref, give_ref)[c][s] = back.reshape(2, count, features)
                branch = dot_nn(active, down_ref[...]).astype(jnp.bfloat16)
                (branch_keep_ref, branch_give_ref)[c][s] = branch.reshape(2, count, features)
                for x, source in enumerate(sources):
                    active_ref[source] = active[x * count : (x + 1) * count]
        sums_ref[...] = total

    half = sds((2, 2, count, features), jnp.bfloat16)
    return kernel_call(
        kernel,
        [ANYWHERE] * 14 + [LOCAL],
        [
            sds((PLANE, count, units), jnp.bfloat16),
            sds((rows, units), jnp.bfloat16),
            sds((1, units), jnp.float32),
            half,
            half,
            half,
            half,
        ],
        [
            pltpu.VMEM((features, units), jnp.bfloat16),
            pltpu.VMEM(down.shape, jnp.bfloat16),
            pltpu.VMEM((rows, features), jnp.bfloat16),
            pltpu.VMEM(grad.shape, jnp.bfloat16),
            pltpu.SemaphoreType.DMA((PLANE,)),
            pltpu.SemaphoreType.DMA((DEPTH + 2,)),
        ],
        8 * rows * features * units,
        (*blocks, grad, *ups, down, vectors),
    )


def feed_forward_weights(blocks, hidden_grad, active, grad):
    count, features = blocks[0].shape
    rows, units = hidden_grad.shape

    def kernel(
        n0, n1, n2, n3, n4, n5, n6, n7, hidden_grad_hbm, active_hbm, grad_hbm, up_ref, down_ref,
        normed_ref, hidden_grad_ref, active_ref, grad_ref, sems, more_sems,
    ):
        active_copies = [
            load(active_hbm, active_ref, more_sems.at[0]),
            load(grad_hbm, grad_ref, more_sems.at[1]),
        ]
        copies = [load(hidden_grad_hbm, hidden_grad_ref, more_sems.at[2])]
        copies += load_blocks((n0, n1, n2, n3, n4, n5, n6, n7), normed_ref, sems)
        wait_all(active_copies)
        grad = grad_ref[...].reshape(rows, features)
        for p in range(DEPTH):
            part = active_ref[:, :, p * 128 : (p + 1) * 128].reshape(rows, 128)
            down_ref[p] = outer(part, grad).astype(jnp.bfloat16)
        wait_all(copies)
        for r in range(PLANE):
            part = outer(normed_ref[:, r * 128 : (r + 1) * 128], hidden_grad_ref[...])
            up_ref[:, r] = part.astype(jnp.bfloat16).reshape(DEPTH, 32, units)

    low = jnp.bfloat16
    return kernel_call(
        kernel,
        [ANYWHERE] * 11,
        [sds((DEPTH, PLANE, 32, units), low), sds((DEPTH, units // DEPTH, features), low)],
        [
            pltpu.VMEM((rows, features), low),
            pltpu.VMEM((rows, units), low),
            pltpu.VMEM(active.shape, low),
            pltpu.VMEM(grad.shape, low),
            pltpu.SemaphoreType.DMA((PLANE,)),
            pltpu.SemaphoreType.DMA((3,)),
        ],
        4 * rows * features * units,
        (*blocks, hidden_grad, active, grad),
    )


def attention_weights(blocks, joint_grad, mixed, grads):
    count, features = blocks[0].shape
    rows, width = joint_grad.shape
    own = mixed.shape[1]

    def kernel(
        n0, n1, n2, n3, n4, n5, n6, n7, joint_grad_hbm, mixed_hbm, g0, g1, g2, g3, g4, g5, g6, g7,
        q0, q1, q2, q3, out_ref, normed_ref, joint_grad_ref, mixed_ref, grad_ref, sems, more_sems,
    ):
        z = lax.axis_index("shard")
        copies = [load(joint_grad_hbm, joint_grad_ref, more_sems.at[0])]
        copies += load_blocks((n0, n1, n2, n3, n4, n5, n6, n7), normed_ref, sems.at[0])
        out_copies = [load(mixed_hbm, mixed_ref, more_sems.at[1])]
        out_copies += load_blocks((g0, g1, g2, g3, g4, g5, g6, g7), grad_ref, sems.at[1])
        wait_all(copies)
        for r in range(PLANE):
            part = outer(normed_ref[:, r * 128 : (r + 1) * 128], joint_grad_ref[...])
            part = part.astype(jnp.bfloat16).reshape(DEPTH, 32, width)
            for step, ref in enumerate((q0, q1, q2, q3)):
                for p in range(DEPTH):

                    @pl.when(lax.rem(z + step, DEPTH) == p)
                    def _():
                        ref[r] = part[p]

        wait_all(out_copies)
        part = outer(mixed_ref[...], grad_ref[...])
        out_ref[...] = part.astype(jnp.bfloat16).reshape(DEPTH, own // DEPTH, features)

    low = jnp.bfloat16
    return kernel_call(
        kernel,
        [ANYWHERE] * 18,
        [sds((PLANE, 32, width), low)] * 4 + [sds((DEPTH, own // DEPTH, features), low)],
        [
            pltpu.VMEM((rows, features), low),
            pltpu.VMEM((rows, width), low),
            pltpu.VMEM((rows, own), low),
            pltpu.VMEM((rows, features), low),
            pltpu.SemaphoreType.DMA((2, PLANE)),
            pltpu.SemaphoreType.DMA((2,)),
        ],
        2 * rows * features * (width + own),
        (*blocks, joint_grad, mixed, *grads),
    )


def body_planes(
    tokens,
    cotangent,
    lengths,
    assign,
    first_gain,
    first_shift,
    qkv_weight,
    qv_bias,
    out_weight,
    out_bias,
    second_gain,
    second_shift,
    up_weight,
    up_bias,
    down_weight,
    down_bias,
):
    row_count, feature_count = tokens.shape
    rep = lax.axis_index("rep")
    z = lax.axis_index("shard")
    own = feature_count // PLANE
    devices = PLANE * DEPTH

    small = (
        first_gain,
        first_shift,
        qv_bias,
        out_bias,
        second_gain,
        second_shift,
        up_bias,
        down_bias,
    )
    whole = sum(item.shape[0] for item in small)
    start = 0
    packed = jnp.zeros((whole,), jnp.bfloat16)
    for item in small:
        packed = packed + jnp.pad(item, (start, whole - start - item.shape[0]))
        start += item.shape[0]
    packed = packed.reshape(-1, 128)
    packs = [packed] + [over_z(packed, step) for step in (1, 2, 3)]
    tokens = to_home(tokens)

    weights = after((qkv_weight, out_weight, up_weight, down_weight), tokens, packs)
    qkv_own, out_own, up_own, down_own = own_eighths(*weights)
    vectors, normed = first_norm(tokens, packs)
    normed_blocks = gather_plane(normed)
    qkv_own = after(qkv_own, normed)
    qkv_parts = [qkv_own] + [over_z(qkv_own, step) for step in (1, 2, 3)]
    out_own = after(out_own, qkv_parts)
    out_part = jnp.where(z == rep >> 1, out_own, jnp.zeros_like(out_own))
    for step in (1, 2, 3):
        out_part = out_part + over_all(
            out_own,
            lambda i, step=step: (
                i - i % DEPTH + (i % DEPTH + step) % DEPTH if i % DEPTH == i // 8 else None
            ),
        )
    up_own = after(up_own, out_part)
    up_parts = [up_own] + [over_z(up_own, step) for step in (1, 2, 3)]

    own_length = jnp.sum(jnp.where(jnp.arange(lengths.shape[0]) == assign[0], lengths, 0))
    ones = jnp.ones((16, feature_count), jnp.float32)
    length_rows = jnp.where(
        jnp.arange(16)[:, None] == 0, ones * (own_length // 16), ones * (own_length % 16)
    )
    moved = to_home(
        after(jnp.concatenate([cotangent, length_rows.astype(jnp.bfloat16)], 0), normed)
    )
    cotangent = moved[:row_count]
    length_parts = moved[row_count : row_count + 2, 0].astype(jnp.int32)
    seq_length = 16 * length_parts[0] + length_parts[1]
    other_length = over_rep(seq_length.astype(jnp.float32).reshape(1, 1), 4)
    lens = jnp.stack([seq_length, other_length.astype(jnp.int32)[0, 0]])
    heads = (2 * rep + jnp.arange(2)).astype(jnp.float32)
    slopes = jnp.exp2(-8.0 * (heads + 1.0) / HEADS)
    position = quarter_of(rep) * row_count + jnp.arange(row_count)
    branch_grad = jnp.where((position < seq_length)[:, None], cotangent, jnp.zeros_like(cotangent))

    branch_grad_plane = lax.all_gather(branch_grad, "rep", axis=0, tiled=False)
    down_all = lax.all_gather(after(down_own, branch_grad), "shard", axis=0, tiled=True)
    joint, mixed, keep, give = attention_forward(
        lens, slopes, normed_blocks, qkv_parts, out_part, vectors
    )
    parts = send_parts(add_halves(keep, over_rep(give, 1)))
    middle, normed_two = second_norm(tokens, vectors, after(parts, up_parts))
    normed_two_blocks = gather_plane(normed_two)
    active, hidden_grad, hidden_sums, branch_keep, branch_give, keep, give = feed_forward(
        normed_two_blocks, branch_grad_plane, up_parts, down_all, vectors
    )
    received = over_rep(give, 1)
    branch_received = over_rep(after(branch_give, received), 1)
    halves = add_halves(keep, received)
    up_slice, down_slice = feed_forward_weights(
        normed_two_blocks, after(hidden_grad, halves), active, branch_grad_plane
    )
    up_summed = scattered_over_z(up_slice)
    down_summed = scattered_over_z(down_slice)
    parts = after(send_parts(halves), up_slice, branch_received)
    middle_grad, attended_grad, second_sums = second_norm_back(
        lens, vectors, middle, cotangent, parts
    )
    attended_blocks = gather_plane(attended_grad)
    branch_halves = add_halves(branch_keep, after(branch_received, attended_grad))
    joint_grad, joint_sums, keep, give = attention_backward(
        after(lens, branch_halves), slopes, attended_blocks, joint, qkv_parts, out_part
    )
    branch_own, *branch_rest = send_parts(branch_halves)
    received = after(over_rep(give, 1), branch_rest)
    halves = add_halves(keep, received)
    *qkv_slices, out_slice = attention_weights(
        normed_blocks, after(joint_grad, halves), mixed, attended_blocks
    )
    parts = after(send_parts(halves), qkv_slices)
    tokens_grad, first_sums = first_norm_back(tokens, vectors, middle_grad, parts)
    tokens_grad = from_home(tokens_grad).astype(jnp.float32)
    qkv_summed = qkv_slices[0].astype(jnp.float32)
    for step in (1, 2, 3):
        qkv_summed = qkv_summed + over_z(qkv_slices[step], step).astype(jnp.float32)
    qkv_grad = columns_to_rows(qkv_summed.astype(jnp.bfloat16))
    out_grad = scattered_over_z(out_slice).astype(jnp.float32)

    branch = branch_own + sum(part.astype(jnp.float32) for part in branch_rest)
    layer_low = (middle + branch + vectors[5:6]).astype(jnp.bfloat16)
    layer_out = from_home(after(layer_low, halves)).astype(jnp.float32)
    down_grad = over_all(
        after(down_summed, halves),
        lambda i: (2 * (i % DEPTH) + i // 16) * DEPTH + (i // DEPTH) % DEPTH,
    ).astype(jnp.float32)
    up_grad = columns_to_rows(after(up_summed, halves))

    at_rep = (jnp.arange(PLANE) == rep)[None, :, None]

    def placed(sums):
        return jnp.where(at_rep, sums.reshape(-1, 1, 128), 0.0).reshape(-1)

    joint_parts = joint_sums.reshape(3, own)
    small_grads = (
        first_sums[0],
        first_sums[1],
        placed(jnp.concatenate([joint_parts[:1], joint_parts[2:]], 0)),
        second_sums[2],
        second_sums[0],
        second_sums[1],
        placed(hidden_sums),
        second_sums[3],
    )
    small_packed = jnp.concatenate(
        [g.reshape(devices, g.shape[0] // devices) for g in small_grads], 1
    ).astype(jnp.bfloat16)
    small_arrived = lax.all_to_all(small_packed, ("rep", "shard"), 0, 0, tiled=True)
    small_sums = jnp.sum(small_arrived.astype(jnp.float32), 0)
    sums = []
    start = 0
    for g in small_grads:
        size = g.shape[0] // devices
        sums.append(small_sums[start : start + size])
        start += size
    return (
        layer_out,
        tokens_grad,
        sums[0],
        sums[1],
        qkv_grad,
        sums[2],
        out_grad,
        sums[3],
        sums[4],
        sums[5],
        up_grad,
        sums[6],
        down_grad,
        sums[7],
    )


def solution(mesh):
    return jax.shard_map(
        body_planes if is_planes(mesh) else body_generic,
        mesh=mesh,
        in_specs=(
            P(("rep", "shard"), None),
            P(("rep", "shard"), None),
            P(),
            P("rep"),
            P("shard"),
            P("shard"),
            P("shard", None),
            P("shard"),
            P("shard", None),
            P("shard"),
            P("shard"),
            P("shard"),
            P("shard", None),
            P("shard"),
            P("shard", None),
            P("shard"),
        ),
        out_specs=(
            P(("rep", "shard"), None),
            P(("rep", "shard"), None),
            P(("rep", "shard")),
            P(("rep", "shard")),
            P(("rep", "shard"), None),
            P(("rep", "shard")),
            P(("rep", "shard"), None),
            P(("rep", "shard")),
            P(("rep", "shard")),
            P(("rep", "shard")),
            P(("rep", "shard"), None),
            P(("rep", "shard")),
            P(("rep", "shard"), None),
            P(("rep", "shard")),
        ),
        check_vma=False,
    )
```

```python
import math

import jax
import jax.numpy as jnp
from jax import lax
from jax.experimental import pallas as pl
from jax.experimental.pallas import tpu as pltpu
from jax.sharding import PartitionSpec as P

HEADS = 16


def for_sending(value):
    return jax.tree.map(lambda a: a.astype(jnp.bfloat16) if a.dtype == jnp.float32 else a, value)


def cut_along(value, dim, devices):
    before, after = (value.shape[:dim], value.shape[dim + 1 :])
    return jnp.moveaxis(value.reshape(*before, devices, -1, *after), dim, 0)


def summed_on_arrival(value, axis, dim):
    blocks = cut_along(value, dim, lax.axis_size(axis))
    arrived = lax.all_to_all(blocks, axis, split_axis=0, concat_axis=0, tiled=True)
    return arrived.astype(jnp.float32).sum(axis=0)


def layer_norm(rows_in, norm_gain, norm_shift):
    row_mean = jnp.mean(rows_in, -1, keepdims=True)
    centered = rows_in - row_mean
    variance = jnp.mean(centered * centered, -1, keepdims=True)
    return centered * lax.rsqrt(variance + 1e-05) * norm_gain + norm_shift


def gelu_tanh(values_in):
    return jax.nn.gelu(values_in, approximate=True)


def owner_order(values):
    rep_count = lax.axis_size("rep")
    shard_count = lax.axis_size("shard")
    lead = values.shape[:-1]
    width = values.shape[-1]
    block = width // (rep_count * shard_count)
    arranged = values.reshape(lead + (rep_count, shard_count, block))
    return jnp.swapaxes(arranged, -3, -2).reshape(lead + (width,))


def settle(grads):
    group_summed = jax.tree.map(
        lambda part: part.astype(jnp.float32),
        lax.psum_scatter(for_sending(grads), "shard", scatter_dimension=0, tiled=True),
    )
    return jax.tree.map(lambda part: summed_on_arrival(part, "rep", 0), for_sending(group_summed))


def head_scores(query_heads, key_heads, query_pos, key_pos, seq_length):
    head_count = query_heads.shape[1]
    score_scale = 1.0 / math.sqrt(query_heads.shape[2])
    slopes = jnp.exp2(-8.0 * (jnp.arange(head_count).astype(jnp.float32) + 1.0) / head_count)
    raw_scores = (
        jnp.einsum("qhd,khd->hqk", query_heads, key_heads, preferred_element_type=jnp.float32)
        * score_scale
    )
    distance = (query_pos[:, None] - key_pos[None, :]).astype(jnp.float32)
    raw_scores = raw_scores - slopes[:, None, None] * distance[None]
    allowed = (key_pos[None, :] <= query_pos[:, None]) & (key_pos[None, :] < seq_length)
    return jnp.where(allowed[None], raw_scores, -1e30)


def body_generic(
    tokens,
    cotangent,
    lengths,
    assign,
    first_gain,
    first_shift,
    qkv_weight,
    qv_bias,
    out_weight,
    out_bias,
    second_gain,
    second_shift,
    up_weight,
    up_bias,
    down_weight,
    down_bias,
):
    rows_in = tokens.astype(jnp.float32)
    row_count = rows_in.shape[0]
    feature_count = rows_in.shape[1]
    head_count = HEADS
    head_size = feature_count // head_count
    score_scale = 1.0 / math.sqrt(head_size)
    group_size = row_count * lax.axis_size("shard")
    seq_length = jnp.sum(jnp.where(jnp.arange(lengths.shape[0]) == assign[0], lengths, 0))
    query_pos = lax.axis_index("shard") * row_count + jnp.arange(row_count)
    key_pos = jnp.arange(group_size)
    row_valid = (query_pos < seq_length)[:, None]
    owned = (
        first_gain,
        first_shift,
        qkv_weight,
        qv_bias,
        out_weight,
        out_bias,
        second_gain,
        second_shift,
        up_weight,
        up_bias,
        down_weight,
        down_bias,
    )
    gathered = (
        lax.all_gather(owned[0], "shard", axis=0, tiled=True),
        lax.all_gather(owned[1], "shard", axis=0, tiled=True),
        lax.all_gather(owned[2], "shard", axis=0, tiled=True),
        lax.all_gather(owned[3], "shard", axis=0, tiled=True),
        lax.all_gather(owned[4], "shard", axis=0, tiled=True),
        lax.all_gather(owned[5], "shard", axis=0, tiled=True),
        lax.all_gather(owned[6], "shard", axis=0, tiled=True),
        lax.all_gather(owned[7], "shard", axis=0, tiled=True),
        lax.all_gather(owned[8], "shard", axis=0, tiled=True),
        lax.all_gather(owned[9], "shard", axis=0, tiled=True),
        lax.all_gather(owned[10], "shard", axis=0, tiled=True),
        lax.all_gather(owned[11], "shard", axis=0, tiled=True),
    )
    gain_first = gathered[0].astype(jnp.float32)
    shift_first = gathered[1].astype(jnp.float32)
    bias_qv = gathered[3].astype(jnp.float32)
    bias_out = gathered[5].astype(jnp.float32)
    gain_second = gathered[6].astype(jnp.float32)
    shift_second = gathered[7].astype(jnp.float32)
    bias_up = gathered[9].astype(jnp.float32)
    bias_down = gathered[11].astype(jnp.float32)
    normed = layer_norm(rows_in, gain_first, shift_first)
    normed_low = normed.astype(jnp.bfloat16)
    joint_out = jnp.dot(normed_low, gathered[2], preferred_element_type=jnp.float32)
    query_low = (joint_out[:, :feature_count] + bias_qv[:feature_count]).astype(jnp.bfloat16)
    key_low = joint_out[:, feature_count : 2 * feature_count].astype(jnp.bfloat16)
    value_low = (joint_out[:, 2 * feature_count :] + bias_qv[feature_count:]).astype(jnp.bfloat16)
    key_all, value_all = (
        lax.all_gather(key_low, "shard", axis=0, tiled=True),
        lax.all_gather(value_low, "shard", axis=0, tiled=True),
    )
    query_heads = query_low.reshape(row_count, head_count, head_size)
    scores = head_scores(
        query_heads,
        key_all.reshape(group_size, head_count, head_size),
        query_pos,
        key_pos,
        seq_length,
    )
    row_top = jnp.max(scores, -1, keepdims=True)
    exp_scores = jnp.exp(scores - row_top)
    row_total = jnp.sum(exp_scores, -1, keepdims=True)
    log_total = row_top + jnp.log(row_total)
    attn_probs = exp_scores / row_total
    mixed_low = (
        jnp.einsum(
            "hqk,khd->qhd",
            attn_probs.astype(jnp.bfloat16),
            value_all.reshape(group_size, head_count, head_size),
            preferred_element_type=jnp.float32,
        )
        .reshape(row_count, feature_count)
        .astype(jnp.bfloat16)
    )
    attended = jnp.dot(mixed_low, gathered[4], preferred_element_type=jnp.float32) + bias_out
    middle = rows_in + attended
    normed_two_low = layer_norm(middle, gain_second, shift_second).astype(jnp.bfloat16)
    hidden = jnp.dot(normed_two_low, gathered[8], preferred_element_type=jnp.float32) + bias_up
    active_low = gelu_tanh(hidden).astype(jnp.bfloat16)
    branch = jnp.dot(active_low, gathered[10], preferred_element_type=jnp.float32) + bias_down
    layer_out = middle + branch
    back_keys = (key_all, value_all)
    key_heads_back = back_keys[0].reshape(group_size, head_count, head_size)
    value_heads_back = back_keys[1].reshape(group_size, head_count, head_size)
    seed_grad = jnp.where(row_valid, cotangent.astype(jnp.float32), 0.0)
    branch_grad = seed_grad.astype(jnp.bfloat16)
    down_grad = jnp.dot(owner_order(active_low).T, branch_grad, preferred_element_type=jnp.float32)
    down_bias_grad = owner_order(jnp.sum(branch_grad.astype(jnp.float32), 0))
    active_grad = jnp.dot(branch_grad, gathered[10].T, preferred_element_type=jnp.float32)
    unused, gelu_pull = jax.vjp(gelu_tanh, hidden)
    hidden_grad = gelu_pull(active_grad)[0].astype(jnp.bfloat16)
    up_grad = jnp.dot(
        owner_order(normed_two_low).T, hidden_grad, preferred_element_type=jnp.float32
    )
    up_bias_grad = owner_order(jnp.sum(hidden_grad.astype(jnp.float32), 0))
    normed_two_grad = jnp.dot(hidden_grad, gathered[8].T, preferred_element_type=jnp.float32)
    unused_two, second_pull = jax.vjp(layer_norm, middle, gain_second, shift_second)
    middle_from_norm, gain_second_grad, shift_second_grad = second_pull(normed_two_grad)
    middle_grad = seed_grad + middle_from_norm
    down_sums = settle((down_grad, down_bias_grad, up_bias_grad))
    up_sums = settle((up_grad, owner_order(gain_second_grad), owner_order(shift_second_grad)))
    attended_grad = middle_grad.astype(jnp.bfloat16)
    out_grad = jnp.dot(owner_order(mixed_low).T, attended_grad, preferred_element_type=jnp.float32)
    out_bias_grad = owner_order(jnp.sum(attended_grad.astype(jnp.float32), 0))
    mixed_grad = (
        jnp.dot(attended_grad, gathered[4].T, preferred_element_type=jnp.float32)
        .astype(jnp.bfloat16)
        .reshape(row_count, head_count, head_size)
    )
    scores_back = head_scores(query_heads, key_heads_back, query_pos, key_pos, seq_length)
    probs_back = jnp.exp(scores_back - log_total)
    probs_grad = jnp.einsum(
        "qhd,khd->hqk", mixed_grad, value_heads_back, preferred_element_type=jnp.float32
    )
    value_part = jnp.einsum(
        "hqk,qhd->khd",
        probs_back.astype(jnp.bfloat16),
        mixed_grad,
        preferred_element_type=jnp.float32,
    ).reshape(group_size, feature_count)
    row_dot = jnp.sum(probs_back * probs_grad, -1, keepdims=True)
    score_grad = (probs_back * (probs_grad - row_dot)).astype(jnp.bfloat16)
    query_grad = (
        jnp.einsum("hqk,khd->qhd", score_grad, key_heads_back, preferred_element_type=jnp.float32)
        * score_scale
    )
    key_part = (
        jnp.einsum(
            "hqk,qhd->khd", score_grad, query_heads, preferred_element_type=jnp.float32
        ).reshape(group_size, feature_count)
        * score_scale
    )
    key_grad, value_grad = (
        lax.psum_scatter(
            key_part.astype(jnp.bfloat16), "shard", scatter_dimension=0, tiled=True
        ).astype(jnp.float32),
        lax.psum_scatter(
            value_part.astype(jnp.bfloat16), "shard", scatter_dimension=0, tiled=True
        ).astype(jnp.float32),
    )
    joint_grad = jnp.concatenate(
        [query_grad.reshape(row_count, feature_count), key_grad, value_grad], 1
    ).astype(jnp.bfloat16)
    qkv_grad = jnp.dot(owner_order(normed_low).T, joint_grad, preferred_element_type=jnp.float32)
    joint_sums = jnp.sum(joint_grad.astype(jnp.float32), 0)
    qv_bias_grad = owner_order(
        jnp.concatenate([joint_sums[:feature_count], joint_sums[2 * feature_count :]], 0)
    )
    normed_grad = jnp.dot(joint_grad, gathered[2].T, preferred_element_type=jnp.float32)
    unused_three, first_pull = jax.vjp(layer_norm, rows_in, gain_first, shift_first)
    rows_from_norm, gain_first_grad, shift_first_grad = first_pull(normed_grad)
    tokens_grad = middle_grad + rows_from_norm
    attn_sums = settle(
        (
            qkv_grad,
            qv_bias_grad,
            out_grad,
            out_bias_grad,
            owner_order(gain_first_grad),
            owner_order(shift_first_grad),
        )
    )
    return (
        layer_out,
        tokens_grad,
        attn_sums[4],
        attn_sums[5],
        attn_sums[0],
        attn_sums[1],
        attn_sums[2],
        attn_sums[3],
        up_sums[1],
        up_sums[2],
        up_sums[0],
        down_sums[2],
        down_sums[0],
        down_sums[1],
    )


PLANE = 8
DEPTH = 4
QUARTERS = 4
VMEM_BYTES = 60 * 2**20
ORDER = (0, 2, 1, 3, 4, 6, 5, 7)


def is_planes(mesh):
    return mesh.shape["rep"] == PLANE and mesh.shape["shard"] == DEPTH


def over_rep(value, flip):
    return lax.ppermute(value, "rep", [(i, i ^ flip) for i in range(PLANE)])


def over_z(value, step):
    return lax.ppermute(value, "shard", [(i, (i + step) % DEPTH) for i in range(DEPTH)])


def over_all(value, place):
    pairs = [(i, place(i)) for i in range(PLANE * DEPTH) if place(i) is not None]
    return lax.ppermute(value, ("rep", "shard"), pairs)


def home_of(index):
    rep, z = index // DEPTH, index % DEPTH
    y, x, core = rep >> 2, (rep >> 1) & 1, rep & 1
    return (4 * x + 2 * (z & 1) + (z >> 1)) * DEPTH + 2 * core + y


HOME = [home_of(i) for i in range(PLANE * DEPTH)]


def to_home(value):
    return over_all(value, lambda i: HOME[i])


def from_home(value):
    return over_all(value, HOME.index)


def after(value, *earlier):
    return lax.optimization_barrier((value, *earlier))[0]


def gather_plane(rows, earlier=()):
    near = over_rep(rows, 1)
    two, four, six = after(tuple(over_rep(rows, flip) for flip in (2, 4, 6)), earlier)
    return [rows, near, two, over_rep(two, 1), four, over_rep(four, 1), six, over_rep(six, 1)]


def add_halves(keep, received):
    count, features = keep.shape[2:]

    def kernel(keep_ref, received_ref, own_ref, two_ref, four_ref, six_ref, left, right, sems):
        outs = {0: own_ref, 2: two_ref, 4: four_ref, 6: six_ref}
        copies = {}
        for flip in (6, 2, 4, 0):
            y, x = flip >> 2, (flip >> 1) & 1
            copies[flip] = [
                pltpu.make_async_copy(ref.at[y, x], to.at[y, x], sems.at[i, flip // 2])
                for i, (ref, to) in enumerate(((keep_ref, left), (received_ref, right)))
            ]
            for copy in copies[flip]:
                copy.start()
        for flip in (6, 2, 4, 0):
            y, x = flip >> 2, (flip >> 1) & 1
            wait_all(copies[flip])
            total = left[y, x].astype(jnp.float32) + right[y, x].astype(jnp.float32)
            outs[flip][...] = total.astype(outs[flip].dtype)

    low = sds((count, features), jnp.bfloat16)
    return kernel_call(
        kernel,
        [ANYWHERE] * 2,
        [sds((count, features), jnp.float32), low, low, low],
        [
            pltpu.VMEM(keep.shape, keep.dtype),
            pltpu.VMEM(keep.shape, keep.dtype),
            pltpu.SemaphoreType.DMA((2, 4)),
        ],
        0,
        (keep, received),
    )


def send_parts(parts):
    own, *others = parts
    return [own] + [over_rep(part, flip) for part, flip in zip(others, (2, 4, 6))]


def scattered_over_z(blocks):
    return lax.psum_scatter(blocks, "shard", scatter_dimension=0, tiled=False)


def outer(left, right):
    return lax.dot_general(
        left, right, (((0,), (0,)), ((), ())), preferred_element_type=jnp.float32
    )


def spread_columns(arrived):
    count = arrived.shape[1]
    parts = arrived.reshape(PLANE, count, -1, 128)
    return jnp.transpose(parts, (1, 2, 0, 3)).reshape(count, -1).astype(jnp.float32)


def dot_nn(left, right):
    return jnp.dot(left, right, preferred_element_type=jnp.float32)


def dot_nt(left, right):
    return lax.dot_general(
        left, right, (((1,), (1,)), ((), ())), preferred_element_type=jnp.float32
    )


def place_pieces(pieces, whole, sems):
    z = lax.axis_index("shard")
    rows = pieces[0].shape[0]
    copies = []
    for step, piece in enumerate(pieces):
        plane = lax.rem(z + (DEPTH - step), DEPTH)
        at = pl.ds(pl.multiple_of(plane * rows, rows), rows)
        copies.append(pltpu.make_async_copy(piece, whole.at[at], sems.at[step]))
    for copy in copies:
        copy.start()
    return copies


def wait_all(copies):
    for copy in copies:
        copy.wait()


def quarter_of(rep):
    return 2 * (rep & 1) + ((rep >> 1) & 1)


def row_positions(shape, axis, rep, first):
    index = lax.broadcasted_iota(jnp.int32, shape, axis) + first
    return (((index >> 7) ^ quarter_of(rep)) << 7) + (index & 127)


def load_blocks(blocks, whole, sems):
    count = whole.shape[0] // PLANE
    copies = []
    for place, k in enumerate(ORDER):
        at = pl.ds(place * count, count)
        block = blocks[k].at[pl.ds(0, count)]
        copies.append(pltpu.make_async_copy(block, whole.at[at], sems.at[place]))
        copies[-1].start()
    return copies


def load(ref, to, sem):
    copy = pltpu.make_async_copy(ref, to, sem)
    copy.start()
    return copy


def total_of(parts):
    own, two, four, six = parts
    return (own[...] + two[...].astype(jnp.float32)) + (
        four[...].astype(jnp.float32) + six[...].astype(jnp.float32)
    )


def unit_rows(v):
    centered = v - jnp.mean(v, 1, keepdims=True)
    rstd = lax.rsqrt(jnp.mean(centered * centered, 1, keepdims=True) + 1e-05)
    return centered * rstd, rstd


def norm_back(grad, xhat, rstd, gain):
    gx = grad * gain
    return rstd * (
        gx - jnp.mean(gx, 1, keepdims=True) - xhat * jnp.mean(gx * xhat, 1, keepdims=True)
    )


def scores_of(query, keys, slope, distance, allowed, scale):
    raw = dot_nt(query, keys) * scale - slope * distance
    return jnp.where(allowed, raw, -1e30)


VECTORS = ((0, 256), (1, 256), (6, 512), (2, 256), (3, 256), (4, 256), (8, 1024), (5, 256))
ANYWHERE = pl.BlockSpec(memory_space=pl.ANY)
LOCAL = pl.BlockSpec(memory_space=pltpu.VMEM)
SCALARS = pl.BlockSpec(memory_space=pltpu.SMEM)


def sds(shape, dtype):
    return jax.ShapeDtypeStruct(shape, dtype)


def kernel_call(kernel, ins, outs, scratch, flops, operands):
    return pl.pallas_call(
        kernel,
        out_shape=outs,
        in_specs=ins,
        out_specs=[LOCAL] * len(outs),
        scratch_shapes=scratch,
        compiler_params=pltpu.CompilerParams(vmem_limit_bytes=VMEM_BYTES),
        cost_estimate=pl.CostEstimate(flops=flops, bytes_accessed=2**23, transcendentals=2**20),
    )(*operands)


def own_eighths(qkv_weight, out_weight, up_weight, down_weight):
    height, features = qkv_weight.shape[0], out_weight.shape[1]
    units = up_weight.shape[1] // PLANE
    half = features // 2

    def kernel(qkv_ref, out_ref, up_ref, down_ref, qkv_own, out_own, wide_own, sems):
        rep = lax.axis_index("rep")
        moves = []
        for ref, own_ref in ((qkv_ref, qkv_own), (up_ref, wide_own)):
            for j in range(ref.shape[1] // (128 * PLANE)):
                at = pl.ds(pl.multiple_of(1024 * j + 128 * rep, 128), 128)
                moves.append((ref.at[:, at], own_ref.at[:, pl.ds(128 * j, 128)]))
        count = out_own.shape[0]
        at = pl.ds(pl.multiple_of((rep & 1) * count, count), count)
        moves.append((out_ref.at[at, :], out_own))
        count = down_ref.shape[0] // PLANE
        at = pl.ds(pl.multiple_of(rep * count, count), count)
        for j in range(2):
            moves.append(
                (
                    down_ref.at[at, pl.ds(j * half, half)],
                    wide_own.at[pl.ds(j * count, count), pl.ds(units, half)],
                )
            )
        copies = [
            pltpu.make_async_copy(src, dst, sems.at[i]) for i, (src, dst) in enumerate(moves)
        ]
        for copy in copies:
            copy.start()
        wait_all(copies)

    low = jnp.bfloat16
    return kernel_call(
        kernel,
        [ANYWHERE] * 4,
        [
            sds((height, qkv_weight.shape[1] // PLANE), low),
            sds((features // PLANE, features), low),
            sds((height, units + half), low),
        ],
        [pltpu.SemaphoreType.DMA((10,))],
        0,
        (qkv_weight, out_weight, up_weight, down_weight),
    )


def first_norm(moved, packs):
    count, features = moved.shape[0] // 2, moved.shape[1]

    def kernel(moved_ref, p0, p1, p2, p3, vectors_ref, normed_ref, tokens_ref):
        z = lax.axis_index("shard")
        packs = [ref[...].astype(jnp.float32) for ref in (p0, p1, p2, p3)]
        vectors_ref[...] = jnp.zeros_like(vectors_ref)
        for plane in range(DEPTH):
            back = lax.rem(z + (DEPTH - plane), DEPTH)
            pack = packs[3]
            for step in range(3):
                pack = jnp.where(back == step, packs[step], pack)
            start = 0
            for row, size in VECTORS:
                for i in range(size // 128):
                    at = plane * size + i * 128
                    lanes = pl.ds(at % 1024, 128)
                    vectors_ref[row + at // 1024 : row + at // 1024 + 1, lanes] = pack[
                        start + i : start + i + 1
                    ]
                start += size // 128
        tokens = moved_ref[:count]
        tokens_ref[...] = tokens
        xhat, unused = unit_rows(tokens.astype(jnp.float32))
        normed = xhat * vectors_ref[0:1, :] + vectors_ref[1:2, :]
        normed_ref[...] = normed.astype(jnp.bfloat16)

    return kernel_call(
        kernel,
        [LOCAL] * 5,
        [sds((16, features), jnp.float32), *[sds((count, features), jnp.bfloat16)] * 2],
        [],
        0,
        (moved, *packs),
    )


def second_norm(tokens, vectors, parts):
    def kernel(tokens_ref, vectors_ref, own, two, four, six, middle_ref, normed_ref):
        attended = total_of((own, two, four, six)) + vectors_ref[2:3, :]
        middle = tokens_ref[...].astype(jnp.float32) + attended
        middle_ref[...] = middle
        xhat, unused = unit_rows(middle)
        normed = xhat * vectors_ref[3:4, :] + vectors_ref[4:5, :]
        normed_ref[...] = normed.astype(jnp.bfloat16)

    return kernel_call(
        kernel,
        [LOCAL] * 6,
        [sds(tokens.shape, jnp.float32), sds(tokens.shape, jnp.bfloat16)],
        [],
        0,
        (tokens, vectors, *parts),
    )


def second_norm_back(vectors, middle, seed_low, parts):
    rows, features = middle.shape

    def kernel(
        vectors_ref, middle_ref, seed_ref, own, two, four, six,
        grad_ref, low_ref, sums_ref,
    ):
        seed = seed_ref[...].astype(jnp.float32)
        grad = total_of((own, two, four, six))
        xhat, rstd = unit_rows(middle_ref[...])
        total = seed + norm_back(grad, xhat, rstd, vectors_ref[3:4, :])
        grad_ref[...] = total
        low = total.astype(jnp.bfloat16)
        low_ref[...] = low
        sums_ref[0:1, :] = jnp.sum(grad * xhat, 0, keepdims=True)
        sums_ref[1:2, :] = jnp.sum(grad, 0, keepdims=True)
        sums_ref[2:3, :] = jnp.sum(low.astype(jnp.float32), 0, keepdims=True)
        sums_ref[3:4, :] = jnp.sum(seed, 0, keepdims=True)

    return kernel_call(
        kernel,
        [LOCAL] * 7,
        [
            sds((rows, features), jnp.float32),
            sds((rows, features), jnp.bfloat16),
            sds((4, features), jnp.float32),
        ],
        [],
        0,
        (vectors, middle, seed_low, *parts),
    )


def first_norm_back(tokens, vectors, middle_grad, parts):
    rows, features = tokens.shape

    def kernel(tokens_ref, vectors_ref, base_ref, own, two, four, six, grad_ref, sums_ref):
        grad = total_of((own, two, four, six))
        xhat, rstd = unit_rows(tokens_ref[...].astype(jnp.float32))
        total = base_ref[...] + norm_back(grad, xhat, rstd, vectors_ref[0:1, :])
        grad_ref[...] = total.astype(jnp.bfloat16)
        sums_ref[0:1, :] = jnp.sum(grad * xhat, 0, keepdims=True)
        sums_ref[1:2, :] = jnp.sum(grad, 0, keepdims=True)

    return kernel_call(
        kernel,
        [LOCAL] * 7,
        [sds((rows, features), jnp.bfloat16), sds((2, features), jnp.float32)],
        [],
        0,
        (tokens, vectors, middle_grad, *parts),
    )


def attention_forward(lens, slopes, blocks, weights, vectors):
    rows, features = PLANE * blocks[0].shape[0], blocks[0].shape[1]
    span = rows // 2
    width = weights[0].shape[1]
    own = width // 3
    head_size = own // 2
    scale = 1.0 / math.sqrt(head_size)
    step_rows = span // QUARTERS

    def kernel(
        own_length, other_length, slopes_ref, n0, n1, n2, n3, n4, n5, n6, n7, w0, w1, w2, w3,
        vectors_ref, joint_ref, mixed_ref, weight_ref, normed_ref, sems, more_sems,
    ):
        rep = lax.axis_index("rep")
        weight_copies = place_pieces((w0, w1, w2, w3), weight_ref, sems)
        copies = load_blocks((n0, n1, n2, n3, n4, n5, n6, n7), normed_ref, more_sems)
        mine = pl.ds(pl.multiple_of(rep * own, own), own)
        bias_q, bias_v = vectors_ref[6:7, mine], vectors_ref[7:8, mine]
        wait_all(weight_copies)
        for s in range(2):
            for c in range(2):
                at = pl.ds((2 * s + c) * (span // 2), span // 2)
                wait_all(copies[4 * s + 2 * c : 4 * s + 2 * c + 2])
                joint = dot_nn(normed_ref[at, :], weight_ref[...])
                joint_ref[at, :own] = (joint[:, :own] + bias_q).astype(jnp.bfloat16)
                joint_ref[at, own : 2 * own] = joint[:, own : 2 * own].astype(jnp.bfloat16)
                joint_ref[at, 2 * own :] = (joint[:, 2 * own :] + bias_v).astype(jnp.bfloat16)
        lane = lax.broadcasted_iota(jnp.int32, (step_rows, own), 1)
        key_pos = row_positions((1, span), 1, rep, 0)
        for s in range(2):
            keys = joint_ref[pl.ds(s * span, span), own : 2 * own]
            values = joint_ref[pl.ds(s * span, span), 2 * own :]
            length = (own_length, other_length)[s][0:1, 0:1]
            inside = key_pos.astype(jnp.float32) < length

            @pl.loop(0, QUARTERS)
            def _(i):
                first = pl.multiple_of(i * step_rows, step_rows)
                at = pl.ds(s * span + first, step_rows)
                query_pos = row_positions((step_rows, 1), 0, rep, first)
                allowed = (key_pos <= query_pos) & inside
                distance = (query_pos - key_pos).astype(jnp.float32)
                query = joint_ref[at, :own]
                mixed = jnp.zeros((step_rows, own), jnp.float32)
                for j in range(2):
                    mine = (lane >= j * head_size) & (lane < (j + 1) * head_size)
                    masked = jnp.where(mine, query, jnp.zeros_like(query))
                    scores = scores_of(masked, keys, slopes_ref[j], distance, allowed, scale)
                    top = jnp.max(scores, 1, keepdims=True)
                    exps = jnp.exp(scores - top)
                    probs = exps / jnp.sum(exps, 1, keepdims=True)
                    mixed = jnp.where(mine, dot_nn(probs.astype(jnp.bfloat16), values), mixed)
                mixed_ref[at, :] = mixed.astype(jnp.bfloat16)

    return kernel_call(
        kernel,
        [LOCAL] * 2 + [SCALARS] + [ANYWHERE] * 12 + [LOCAL],
        [sds((rows, width), jnp.bfloat16), sds((rows, own), jnp.bfloat16)],
        [
            pltpu.VMEM((features, width), jnp.bfloat16),
            pltpu.VMEM((rows, features), jnp.bfloat16),
            pltpu.SemaphoreType.DMA((DEPTH,)),
            pltpu.SemaphoreType.DMA((PLANE,)),
        ],
        2 * rows * features * width + 8 * rows * span * own,
        (*lens, slopes, *blocks, *weights, vectors),
    )


def out_projection(mixed, out_part):
    rows, features = mixed.shape[0], out_part.shape[1]
    tile = rows // 4

    def kernel(mixed_ref, out_ref, keep_ref, give_ref):
        for s in range(2):
            for c, part_ref in enumerate((keep_ref, give_ref)):
                at = pl.ds((2 * s + c) * tile, tile)
                part = dot_nn(mixed_ref[at, :], out_ref[...]).astype(jnp.bfloat16)
                part_ref[s] = part.reshape(2, tile // 2, features)

    half = sds((2, 2, tile // 2, features), jnp.bfloat16)
    return kernel_call(
        kernel, [LOCAL] * 2, [half, half], [], 2 * rows * features * mixed.shape[1], (mixed, out_part)
    )


def attention_backward(lens, slopes, blocks, joint, weights, out_part):
    rows, features = PLANE * blocks[0].shape[0], blocks[0].shape[1]
    span = rows // 2
    width = weights[0].shape[1]
    own = width // 3
    head_size = own // 2
    scale = 1.0 / math.sqrt(head_size)
    step_rows = span // QUARTERS

    def kernel(
        own_length, other_length, slopes_ref, g0, g1, g2, g3, g4, g5, g6, g7,
        joint_hbm, w0, w1, w2, w3, out_ref,
        joint_grad_ref, sums_ref, keep_ref, give_ref,
        weight_ref, mixed_grad_ref, key_acc, value_acc, joint_ref, grad_ref, out_all, sems, more_sems,
    ):
        rep = lax.axis_index("rep")
        out_copy = load(out_ref, out_all, sems.at[DEPTH])
        grad_copies = load_blocks((g0, g1, g2, g3, g4, g5, g6, g7), grad_ref, more_sems)
        joint_copy = load(joint_hbm, joint_ref, sems.at[DEPTH + 1])
        copies = place_pieces((w0, w1, w2, w3), weight_ref, sems)
        out_copy.wait()
        for s in range(2):
            for c in range(2):
                at = pl.ds((2 * s + c) * (span // 2), span // 2)
                wait_all(grad_copies[4 * s + 2 * c : 4 * s + 2 * c + 2])
                mixed_grad = dot_nt(grad_ref[at, :], out_all[...])
                mixed_grad_ref[at, :] = mixed_grad.astype(jnp.bfloat16)
        joint_copy.wait()
        lane = lax.broadcasted_iota(jnp.int32, (step_rows, own), 1)
        lane_all = lax.broadcasted_iota(jnp.int32, (span, own), 1)
        key_pos = row_positions((1, span), 1, rep, 0)
        for s in range(2):
            keys = joint_ref[pl.ds(s * span, span), own : 2 * own]
            values = joint_ref[pl.ds(s * span, span), 2 * own :]
            length = (own_length, other_length)[s][0:1, 0:1]
            inside = key_pos.astype(jnp.float32) < length
            key_acc[...] = jnp.zeros_like(key_acc)
            value_acc[...] = jnp.zeros_like(value_acc)

            @pl.loop(0, QUARTERS)
            def _(i):
                first = pl.multiple_of(i * step_rows, step_rows)
                at = pl.ds(s * span + first, step_rows)
                query_pos = row_positions((step_rows, 1), 0, rep, first)
                allowed = (key_pos <= query_pos) & inside
                distance = (query_pos - key_pos).astype(jnp.float32)
                query = joint_ref[at, :own]
                mixed_grad = mixed_grad_ref[at, :]
                query_grad = jnp.zeros((step_rows, own), jnp.float32)
                for j in range(2):
                    mine = (lane >= j * head_size) & (lane < (j + 1) * head_size)
                    masked = jnp.where(mine, query, jnp.zeros_like(query))
                    masked_grad = jnp.where(mine, mixed_grad, jnp.zeros_like(mixed_grad))
                    scores = scores_of(masked, keys, slopes_ref[j], distance, allowed, scale)
                    top = jnp.max(scores, 1, keepdims=True)
                    exps = jnp.exp(scores - top)
                    probs = exps / jnp.sum(exps, 1, keepdims=True)
                    probs_grad = dot_nt(masked_grad, values)
                    row_dot = jnp.sum(probs * probs_grad, 1, keepdims=True)
                    score_grad = (probs * (probs_grad - row_dot)).astype(jnp.bfloat16)
                    query_grad = jnp.where(mine, dot_nn(score_grad, keys), query_grad)
                    key_acc[...] += outer(score_grad, masked)
                    value_acc[...] += outer(probs.astype(jnp.bfloat16), masked_grad)
                joint_grad_ref[at, :own] = (query_grad * scale).astype(jnp.bfloat16)

            at = pl.ds(s * span, span)
            joint_grad_ref[at, own : 2 * own] = (key_acc[...] * scale).astype(jnp.bfloat16)
            joint_grad_ref[at, 2 * own :] = value_acc[...].astype(jnp.bfloat16)
        wait_all(copies)
        total = jnp.zeros((1, width), jnp.float32)
        for s in range(2):
            for c, part_ref in enumerate((keep_ref, give_ref)):
                at = pl.ds((2 * s + c) * (span // 2), span // 2)
                joint_grad = joint_grad_ref[at, :]
                total = total + jnp.sum(joint_grad.astype(jnp.float32), 0, keepdims=True)
                part = dot_nt(joint_grad, weight_ref[...]).astype(jnp.bfloat16)
                part_ref[s] = part.reshape(2, span // 4, features)
        sums_ref[...] = total

    half = sds((2, 2, span // 4, features), jnp.bfloat16)
    return kernel_call(
        kernel,
        [LOCAL] * 2 + [SCALARS] + [ANYWHERE] * 14,
        [sds((rows, width), jnp.bfloat16), sds((1, width), jnp.float32), half, half],
        [
            pltpu.VMEM((features, width), jnp.bfloat16),
            pltpu.VMEM((rows, own), jnp.bfloat16),
            pltpu.VMEM((span, own), jnp.float32),
            pltpu.VMEM((span, own), jnp.float32),
            pltpu.VMEM((rows, width), jnp.bfloat16),
            pltpu.VMEM((rows, features), jnp.bfloat16),
            pltpu.VMEM((own, features), jnp.bfloat16),
            pltpu.SemaphoreType.DMA((DEPTH + 2,)),
            pltpu.SemaphoreType.DMA((PLANE,)),
        ],
        2 * rows * features * (width + own) + 20 * rows * span * own,
        (*lens, slopes, *blocks, joint, *weights, out_part),
    )


def feed_forward(blocks, grads, wide, vectors):
    count, features = blocks[0].shape
    rows = PLANE * count
    half_width = features // 2
    units = wide.shape[1] - half_width
    tile = 2 * count
    root = math.sqrt(2.0 / math.pi)
    bend = 0.044715

    def kernel(
        n0, n1, n2, n3, n4, n5, n6, n7, g0, g1, g2, g3, g4, g5, g6, g7, wide_hbm, vectors_ref,
        active_ref, hidden_grad_ref, sums_ref, branch_keep_ref, branch_give_ref, keep_ref, give_ref,
        up_ref, down_ref, normed_ref, grad_ref, sems, grad_sems, more_sems,
    ):
        rep = lax.axis_index("rep")
        up_copies = [load(wide_hbm.at[:, pl.ds(0, units)], up_ref, more_sems.at[0])]
        copies = load_blocks((n0, n1, n2, n3, n4, n5, n6, n7), normed_ref, sems)
        grad_copies = load_blocks((g0, g1, g2, g3, g4, g5, g6, g7), grad_ref, grad_sems)
        down_copies = []
        for p in range(DEPTH):
            for j in range(2):
                source = wide_hbm.at[pl.ds((2 * p + j) * 128, 128), pl.ds(units, half_width)]
                to = down_ref.at[pl.ds(p * 128, 128), pl.ds(j * half_width, half_width)]
                down_copies.append(load(source, to, more_sems.at[2 + 2 * p + j]))
        mine = pl.ds(pl.multiple_of(rep * 128, 128), 128)
        bias = jnp.concatenate([vectors_ref[8 + p : 9 + p, mine] for p in range(DEPTH)], 1)
        total = jnp.zeros((1, units), jnp.float32)
        for s in range(2):
            for c in range(2):
                at = pl.ds((2 * s + c) * tile, tile)
                if (s, c) == (0, 0):
                    wait_all(up_copies)
                wait_all(copies[4 * s + 2 * c : 4 * s + 2 * c + 2])
                v = dot_nn(normed_ref[at, :], up_ref[...]) + bias
                square = v * v
                t = jnp.tanh(root * v * (1.0 + bend * square))
                half = 0.5 * (1.0 + t)
                active = (v * half).astype(jnp.bfloat16)
                slope = half + (0.5 * root) * v * (1.0 - t * t) * (1.0 + 3.0 * bend * square)
                if (s, c) == (0, 0):
                    wait_all(grad_copies)
                    wait_all(down_copies)
                hidden_grad = (dot_nt(grad_ref[at, :], down_ref[...]) * slope).astype(jnp.bfloat16)
                hidden_grad_ref[at, :] = hidden_grad
                total = total + jnp.sum(hidden_grad.astype(jnp.float32), 0, keepdims=True)
                back = dot_nt(hidden_grad, up_ref[...]).astype(jnp.bfloat16)
                (keep_ref, give_ref)[c][s] = back.reshape(2, count, features)
                branch = dot_nn(active, down_ref[...]).astype(jnp.bfloat16)
                active_ref[at, :] = active
                (branch_keep_ref, branch_give_ref)[c][s] = branch.reshape(2, count, features)
        sums_ref[...] = total

    half = sds((2, 2, count, features), jnp.bfloat16)
    return kernel_call(
        kernel,
        [ANYWHERE] * 17 + [LOCAL],
        [
            sds((rows, units), jnp.bfloat16),
            sds((rows, units), jnp.bfloat16),
            sds((1, units), jnp.float32),
            half,
            half,
            half,
            half,
        ],
        [
            pltpu.VMEM((features, units), jnp.bfloat16),
            pltpu.VMEM((units, features), jnp.bfloat16),
            pltpu.VMEM((rows, features), jnp.bfloat16),
            pltpu.VMEM((rows, features), jnp.bfloat16),
            pltpu.SemaphoreType.DMA((PLANE,)),
            pltpu.SemaphoreType.DMA((PLANE,)),
            pltpu.SemaphoreType.DMA((2 + 2 * DEPTH,)),
        ],
        8 * rows * features * units,
        (*blocks, *grads, wide, vectors),
    )


def feed_forward_weights(blocks, hidden_grad, active, grads):
    count, features = blocks[0].shape
    rows, units = hidden_grad.shape

    def kernel(
        n0, n1, n2, n3, n4, n5, n6, n7, g0, g1, g2, g3, g4, g5, g6, g7, hidden_grad_hbm, active_hbm,
        wide_ref, normed_ref, hidden_grad_ref, active_ref, grad_ref, sems, grad_sems, more_sems,
    ):
        active_copies = [load(active_hbm, active_ref, more_sems.at[0])]
        active_copies += load_blocks((g0, g1, g2, g3, g4, g5, g6, g7), grad_ref, grad_sems)
        copies = [load(hidden_grad_hbm, hidden_grad_ref, more_sems.at[1])]
        copies += load_blocks((n0, n1, n2, n3, n4, n5, n6, n7), normed_ref, sems)
        wait_all(active_copies)
        for p in range(DEPTH):
            part = active_ref[:, p * 128 : (p + 1) * 128]
            down = outer(part, grad_ref[...]).astype(jnp.bfloat16)
            wide_ref[p, :128, units:] = down[:, : features // 2]
            wide_ref[p, 128:, units:] = down[:, features // 2 :]
        wait_all(copies)
        for r in range(PLANE):
            part = outer(normed_ref[:, r * 128 : (r + 1) * 128], hidden_grad_ref[...])
            part = part.astype(jnp.bfloat16).reshape(DEPTH, 32, units)
            wide_ref[:, r * 32 : (r + 1) * 32, :units] = part

    low = jnp.bfloat16
    return kernel_call(
        kernel,
        [ANYWHERE] * 18,
        [sds((DEPTH, PLANE * 32, units + features // 2), low)],
        [
            pltpu.VMEM((rows, features), low),
            pltpu.VMEM((rows, units), low),
            pltpu.VMEM((rows, units), low),
            pltpu.VMEM((rows, features), low),
            pltpu.SemaphoreType.DMA((PLANE,)),
            pltpu.SemaphoreType.DMA((PLANE,)),
            pltpu.SemaphoreType.DMA((2,)),
        ],
        4 * rows * features * units,
        (*blocks, *grads, hidden_grad, active),
    )[0]


def qkv_weights(blocks, joint_grad):
    features = blocks[0].shape[1]
    rows, width = joint_grad.shape

    def kernel(
        n0, n1, n2, n3, n4, n5, n6, n7, joint_grad_hbm,
        q0, q1, q2, q3, normed_ref, joint_grad_ref, sems, more_sems,
    ):
        z = lax.axis_index("shard")
        copies = [load(joint_grad_hbm, joint_grad_ref, more_sems.at[0])]
        copies += load_blocks((n0, n1, n2, n3, n4, n5, n6, n7), normed_ref, sems)
        wait_all(copies)
        for r in range(PLANE):
            part = outer(normed_ref[:, r * 128 : (r + 1) * 128], joint_grad_ref[...])
            part = part.astype(jnp.bfloat16).reshape(DEPTH, 32, width)
            for step, ref in enumerate((q0, q1, q2, q3)):
                for p in range(DEPTH):

                    @pl.when(lax.rem(z + step, DEPTH) == p)
                    def _():
                        ref[r] = part[p]

    low = jnp.bfloat16
    return kernel_call(
        kernel,
        [ANYWHERE] * 9,
        [sds((PLANE, 32, width), low)] * 4,
        [
            pltpu.VMEM((rows, features), low),
            pltpu.VMEM((rows, width), low),
            pltpu.SemaphoreType.DMA((PLANE,)),
            pltpu.SemaphoreType.DMA((1,)),
        ],
        2 * rows * features * width,
        (*blocks, joint_grad),
    )


def out_weights(mixed, grads):
    count, features = grads[0].shape
    rows, own = mixed.shape

    def kernel(mixed_ref, g0, g1, g2, g3, g4, g5, g6, g7, out_ref, grad_ref, sems):
        wait_all(load_blocks((g0, g1, g2, g3, g4, g5, g6, g7), grad_ref, sems))
        part = outer(mixed_ref[...], grad_ref[...])
        out_ref[...] = part.astype(jnp.bfloat16).reshape(DEPTH, own // DEPTH, features)

    return kernel_call(
        kernel,
        [LOCAL] + [ANYWHERE] * 8,
        [sds((DEPTH, own // DEPTH, features), jnp.bfloat16)],
        [pltpu.VMEM((rows, features), jnp.bfloat16), pltpu.SemaphoreType.DMA((PLANE,))],
        2 * rows * features * own,
        (mixed, *grads),
    )[0]


def body_planes(
    tokens,
    cotangent,
    lengths,
    assign,
    first_gain,
    first_shift,
    qkv_weight,
    qv_bias,
    out_weight,
    out_bias,
    second_gain,
    second_shift,
    up_weight,
    up_bias,
    down_weight,
    down_bias,
):
    row_count, feature_count = tokens.shape
    rep = lax.axis_index("rep")
    z = lax.axis_index("shard")
    own = feature_count // PLANE
    devices = PLANE * DEPTH

    small = (
        first_gain,
        first_shift,
        qv_bias,
        out_bias,
        second_gain,
        second_shift,
        up_bias,
        down_bias,
    )
    whole = sum(item.shape[0] for item in small)
    start = 0
    packed = jnp.zeros((whole,), jnp.bfloat16)
    for item in small:
        packed = packed + jnp.pad(item, (start, whole - start - item.shape[0]))
        start += item.shape[0]
    packed = packed.reshape(-1, 128)
    packs = [packed] + [over_z(packed, step) for step in (1, 2, 3)]
    moved = to_home(jnp.concatenate([tokens, cotangent], 0))
    own_length = jnp.sum(jnp.where(jnp.arange(lengths.shape[0]) == assign[0], lengths, 0))
    length = to_home(jnp.full((8, 128), own_length.astype(jnp.float32)))
    lens = (length, over_rep(length, 4))

    weights = after((qkv_weight, out_weight, up_weight, down_weight), moved, packs, lens)
    qkv_own, out_own, wide_own = own_eighths(*weights)
    vectors, normed, tokens = first_norm(moved, packs)
    qkv_own = after(qkv_own, normed)
    qkv_parts = [qkv_own] + [over_z(qkv_own, step) for step in (1, 2, 3)]
    normed_blocks = gather_plane(normed, qkv_parts)
    cotangent = after(moved, normed_blocks)[row_count:]
    position = quarter_of(rep) * row_count + jnp.arange(row_count)
    valid = position.astype(jnp.float32) < length[0, 0]
    branch_grad = jnp.where(valid[:, None], cotangent, jnp.zeros_like(cotangent))
    branch_near = [over_rep(branch_grad, flip) for flip in (1, 2, 4, 6)]
    heads = (2 * rep + jnp.arange(2)).astype(jnp.float32)
    slopes = jnp.exp2(-8.0 * (heads + 1.0) / HEADS)
    joint, mixed = attention_forward(lens, slopes, normed_blocks, qkv_parts, vectors)
    out_moved = [
        over_all(
            after(out_own, qkv_parts),
            lambda i, step=step: (
                i - i % DEPTH + (i % DEPTH + step) % DEPTH if i % DEPTH == i // 8 else None
            ),
        )
        for step in (1, 2, 3)
    ]
    out_part = jnp.where(z == rep >> 1, out_own, jnp.zeros_like(out_own))
    out_moved, branch_near = after((out_moved, branch_near), mixed)
    for piece in out_moved:
        out_part = out_part + piece
    branch_blocks = [branch_grad, branch_near[0]]
    for block in branch_near[1:]:
        branch_blocks += [block, over_rep(block, 1)]
    wide_all = lax.all_gather(after(wide_own, out_part), "shard", axis=0, tiled=True)
    keep, give = out_projection(mixed, out_part)
    parts = send_parts(add_halves(keep, over_rep(give, 1)))
    middle, normed_two = second_norm(tokens, vectors, parts)
    normed_two_blocks = gather_plane(normed_two)
    active, hidden_grad, hidden_sums, branch_keep, branch_give, keep, give = feed_forward(
        normed_two_blocks, branch_blocks, wide_all, vectors
    )
    received = over_rep(give, 1)
    parts = send_parts(add_halves(keep, received))
    branch_received = over_rep(after(branch_give, received), 1)
    branch_halves = add_halves(branch_keep, after(branch_received, parts[0]))
    wide_slice = feed_forward_weights(
        normed_two_blocks, after(hidden_grad, parts[0]), active, branch_blocks
    )
    middle_grad, attended_grad, second_sums = second_norm_back(
        vectors, middle, branch_grad, after(parts, wide_slice, branch_halves)
    )
    wide_summed = scattered_over_z(after(wide_slice, attended_grad))
    attended_blocks = gather_plane(attended_grad)
    branch_own, *branch_rest = send_parts(branch_halves)
    joint_grad, joint_sums, keep, give = attention_backward(
        lens, slopes, attended_blocks, joint, qkv_parts, out_part
    )
    received = over_rep(after(give, branch_rest), 1)
    qkv_slices = qkv_weights(normed_blocks, joint_grad)
    parts = send_parts(add_halves(keep, after(received, qkv_slices)))
    qkv_slices = [qkv_slices[0]] + [over_z(qkv_slices[step], step) for step in (1, 2, 3)]
    out_slice = out_weights(after(mixed, parts[0]), attended_blocks)
    tokens_grad, first_sums = first_norm_back(
        tokens, vectors, middle_grad, after(parts, out_slice, qkv_slices)
    )
    tokens_grad = from_home(tokens_grad)
    units = wide_summed.shape[1] - feature_count // 2
    wide_summed, qkv_slices = after((wide_summed, qkv_slices), first_sums)
    up_summed = wide_summed[:, :units].reshape(PLANE, -1, units)
    qkv_summed = qkv_slices[0].astype(jnp.float32)
    for step in (1, 2, 3):
        qkv_summed = qkv_summed + qkv_slices[step].astype(jnp.float32)
    both = jnp.concatenate([up_summed, qkv_summed.astype(jnp.bfloat16)], 2)
    arrived = lax.all_to_all(both, "rep", 0, 0, tiled=True)
    up_grad = spread_columns(arrived[:, :, :units])
    qkv_grad = spread_columns(arrived[:, :, units:])
    out_grad = scattered_over_z(out_slice).astype(jnp.float32)
    down_summed = jnp.concatenate([wide_summed[:128, units:], wide_summed[128:, units:]], 1)
    down_grad = over_all(
        down_summed,
        lambda i: (2 * (i % DEPTH) + i // 16) * DEPTH + (i // DEPTH) % DEPTH,
    )
    branch = branch_own + sum(part.astype(jnp.float32) for part in branch_rest)
    layer_low = (middle + branch + vectors[5:6]).astype(jnp.bfloat16)
    layer_out = from_home(after(layer_low, parts[0]))

    at_rep = (jnp.arange(PLANE) == rep)[None, :, None]

    def placed(sums):
        return jnp.where(at_rep, sums.reshape(-1, 1, 128), 0.0).reshape(-1)

    joint_parts = joint_sums.reshape(3, own)
    small_grads = (
        first_sums[0],
        first_sums[1],
        placed(jnp.concatenate([joint_parts[:1], joint_parts[2:]], 0)),
        second_sums[2],
        second_sums[0],
        second_sums[1],
        placed(hidden_sums),
        second_sums[3],
    )
    small_packed = jnp.concatenate(
        [g.reshape(devices, g.shape[0] // devices) for g in small_grads], 1
    ).astype(jnp.bfloat16)
    small_arrived = lax.all_to_all(after(small_packed, arrived), ("rep", "shard"), 0, 0, tiled=True)
    layer_out, tokens_grad, down_grad = (
        moved_back.astype(jnp.float32)
        for moved_back in after((layer_out, tokens_grad, down_grad), small_arrived)
    )
    small_sums = jnp.sum(small_arrived.astype(jnp.float32), 0)
    sums = []
    start = 0
    for g in small_grads:
        size = g.shape[0] // devices
        sums.append(small_sums[start : start + size])
        start += size
    return (
        layer_out,
        tokens_grad,
        sums[0],
        sums[1],
        qkv_grad,
        sums[2],
        out_grad,
        sums[3],
        sums[4],
        sums[5],
        up_grad,
        sums[6],
        down_grad,
        sums[7],
    )


def solution(mesh):
    return jax.shard_map(
        body_planes if is_planes(mesh) else body_generic,
        mesh=mesh,
        in_specs=(
            P(("rep", "shard"), None),
            P(("rep", "shard"), None),
            P(),
            P("rep"),
            P("shard"),
            P("shard"),
            P("shard", None),
            P("shard"),
            P("shard", None),
            P("shard"),
            P("shard"),
            P("shard"),
            P("shard", None),
            P("shard"),
            P("shard", None),
            P("shard"),
        ),
        out_specs=(
            P(("rep", "shard"), None),
            P(("rep", "shard"), None),
            P(("rep", "shard")),
            P(("rep", "shard")),
            P(("rep", "shard"), None),
            P(("rep", "shard")),
            P(("rep", "shard"), None),
            P(("rep", "shard")),
            P(("rep", "shard")),
            P(("rep", "shard")),
            P(("rep", "shard"), None),
            P(("rep", "shard")),
            P(("rep", "shard"), None),
            P(("rep", "shard")),
        ),
        check_vma=False,
    )
```

```python
import math

import jax
import jax.numpy as jnp
from jax import lax
from jax.experimental import pallas as pl
from jax.experimental.pallas import tpu as pltpu
from jax.sharding import PartitionSpec as P

HEADS = 16


def for_sending(value):
    return jax.tree.map(lambda a: a.astype(jnp.bfloat16) if a.dtype == jnp.float32 else a, value)


def cut_along(value, dim, devices):
    before, after = (value.shape[:dim], value.shape[dim + 1 :])
    return jnp.moveaxis(value.reshape(*before, devices, -1, *after), dim, 0)


def summed_on_arrival(value, axis, dim):
    blocks = cut_along(value, dim, lax.axis_size(axis))
    arrived = lax.all_to_all(blocks, axis, split_axis=0, concat_axis=0, tiled=True)
    return arrived.astype(jnp.float32).sum(axis=0)


def layer_norm(rows_in, norm_gain, norm_shift):
    row_mean = jnp.mean(rows_in, -1, keepdims=True)
    centered = rows_in - row_mean
    variance = jnp.mean(centered * centered, -1, keepdims=True)
    return centered * lax.rsqrt(variance + 1e-05) * norm_gain + norm_shift


def gelu_tanh(values_in):
    return jax.nn.gelu(values_in, approximate=True)


def owner_order(values):
    rep_count = lax.axis_size("rep")
    shard_count = lax.axis_size("shard")
    lead = values.shape[:-1]
    width = values.shape[-1]
    block = width // (rep_count * shard_count)
    arranged = values.reshape(lead + (rep_count, shard_count, block))
    return jnp.swapaxes(arranged, -3, -2).reshape(lead + (width,))


def settle(grads):
    group_summed = jax.tree.map(
        lambda part: part.astype(jnp.float32),
        lax.psum_scatter(for_sending(grads), "shard", scatter_dimension=0, tiled=True),
    )
    return jax.tree.map(lambda part: summed_on_arrival(part, "rep", 0), for_sending(group_summed))


def head_scores(query_heads, key_heads, query_pos, key_pos, seq_length):
    head_count = query_heads.shape[1]
    score_scale = 1.0 / math.sqrt(query_heads.shape[2])
    slopes = jnp.exp2(-8.0 * (jnp.arange(head_count).astype(jnp.float32) + 1.0) / head_count)
    raw_scores = (
        jnp.einsum("qhd,khd->hqk", query_heads, key_heads, preferred_element_type=jnp.float32)
        * score_scale
    )
    distance = (query_pos[:, None] - key_pos[None, :]).astype(jnp.float32)
    raw_scores = raw_scores - slopes[:, None, None] * distance[None]
    allowed = (key_pos[None, :] <= query_pos[:, None]) & (key_pos[None, :] < seq_length)
    return jnp.where(allowed[None], raw_scores, -1e30)


def body_generic(
    tokens,
    cotangent,
    lengths,
    assign,
    first_gain,
    first_shift,
    qkv_weight,
    qv_bias,
    out_weight,
    out_bias,
    second_gain,
    second_shift,
    up_weight,
    up_bias,
    down_weight,
    down_bias,
):
    rows_in = tokens.astype(jnp.float32)
    row_count = rows_in.shape[0]
    feature_count = rows_in.shape[1]
    head_count = HEADS
    head_size = feature_count // head_count
    score_scale = 1.0 / math.sqrt(head_size)
    group_size = row_count * lax.axis_size("shard")
    seq_length = jnp.sum(jnp.where(jnp.arange(lengths.shape[0]) == assign[0], lengths, 0))
    query_pos = lax.axis_index("shard") * row_count + jnp.arange(row_count)
    key_pos = jnp.arange(group_size)
    row_valid = (query_pos < seq_length)[:, None]
    owned = (
        first_gain,
        first_shift,
        qkv_weight,
        qv_bias,
        out_weight,
        out_bias,
        second_gain,
        second_shift,
        up_weight,
        up_bias,
        down_weight,
        down_bias,
    )
    gathered = (
        lax.all_gather(owned[0], "shard", axis=0, tiled=True),
        lax.all_gather(owned[1], "shard", axis=0, tiled=True),
        lax.all_gather(owned[2], "shard", axis=0, tiled=True),
        lax.all_gather(owned[3], "shard", axis=0, tiled=True),
        lax.all_gather(owned[4], "shard", axis=0, tiled=True),
        lax.all_gather(owned[5], "shard", axis=0, tiled=True),
        lax.all_gather(owned[6], "shard", axis=0, tiled=True),
        lax.all_gather(owned[7], "shard", axis=0, tiled=True),
        lax.all_gather(owned[8], "shard", axis=0, tiled=True),
        lax.all_gather(owned[9], "shard", axis=0, tiled=True),
        lax.all_gather(owned[10], "shard", axis=0, tiled=True),
        lax.all_gather(owned[11], "shard", axis=0, tiled=True),
    )
    gain_first = gathered[0].astype(jnp.float32)
    shift_first = gathered[1].astype(jnp.float32)
    bias_qv = gathered[3].astype(jnp.float32)
    bias_out = gathered[5].astype(jnp.float32)
    gain_second = gathered[6].astype(jnp.float32)
    shift_second = gathered[7].astype(jnp.float32)
    bias_up = gathered[9].astype(jnp.float32)
    bias_down = gathered[11].astype(jnp.float32)
    normed = layer_norm(rows_in, gain_first, shift_first)
    normed_low = normed.astype(jnp.bfloat16)
    joint_out = jnp.dot(normed_low, gathered[2], preferred_element_type=jnp.float32)
    query_low = (joint_out[:, :feature_count] + bias_qv[:feature_count]).astype(jnp.bfloat16)
    key_low = joint_out[:, feature_count : 2 * feature_count].astype(jnp.bfloat16)
    value_low = (joint_out[:, 2 * feature_count :] + bias_qv[feature_count:]).astype(jnp.bfloat16)
    key_all, value_all = (
        lax.all_gather(key_low, "shard", axis=0, tiled=True),
        lax.all_gather(value_low, "shard", axis=0, tiled=True),
    )
    query_heads = query_low.reshape(row_count, head_count, head_size)
    scores = head_scores(
        query_heads,
        key_all.reshape(group_size, head_count, head_size),
        query_pos,
        key_pos,
        seq_length,
    )
    row_top = jnp.max(scores, -1, keepdims=True)
    exp_scores = jnp.exp(scores - row_top)
    row_total = jnp.sum(exp_scores, -1, keepdims=True)
    log_total = row_top + jnp.log(row_total)
    attn_probs = exp_scores / row_total
    mixed_low = (
        jnp.einsum(
            "hqk,khd->qhd",
            attn_probs.astype(jnp.bfloat16),
            value_all.reshape(group_size, head_count, head_size),
            preferred_element_type=jnp.float32,
        )
        .reshape(row_count, feature_count)
        .astype(jnp.bfloat16)
    )
    attended = jnp.dot(mixed_low, gathered[4], preferred_element_type=jnp.float32) + bias_out
    middle = rows_in + attended
    normed_two_low = layer_norm(middle, gain_second, shift_second).astype(jnp.bfloat16)
    hidden = jnp.dot(normed_two_low, gathered[8], preferred_element_type=jnp.float32) + bias_up
    active_low = gelu_tanh(hidden).astype(jnp.bfloat16)
    branch = jnp.dot(active_low, gathered[10], preferred_element_type=jnp.float32) + bias_down
    layer_out = middle + branch
    back_keys = (key_all, value_all)
    key_heads_back = back_keys[0].reshape(group_size, head_count, head_size)
    value_heads_back = back_keys[1].reshape(group_size, head_count, head_size)
    seed_grad = jnp.where(row_valid, cotangent.astype(jnp.float32), 0.0)
    branch_grad = seed_grad.astype(jnp.bfloat16)
    down_grad = jnp.dot(owner_order(active_low).T, branch_grad, preferred_element_type=jnp.float32)
    down_bias_grad = owner_order(jnp.sum(branch_grad.astype(jnp.float32), 0))
    active_grad = jnp.dot(branch_grad, gathered[10].T, preferred_element_type=jnp.float32)
    unused, gelu_pull = jax.vjp(gelu_tanh, hidden)
    hidden_grad = gelu_pull(active_grad)[0].astype(jnp.bfloat16)
    up_grad = jnp.dot(
        owner_order(normed_two_low).T, hidden_grad, preferred_element_type=jnp.float32
    )
    up_bias_grad = owner_order(jnp.sum(hidden_grad.astype(jnp.float32), 0))
    normed_two_grad = jnp.dot(hidden_grad, gathered[8].T, preferred_element_type=jnp.float32)
    unused_two, second_pull = jax.vjp(layer_norm, middle, gain_second, shift_second)
    middle_from_norm, gain_second_grad, shift_second_grad = second_pull(normed_two_grad)
    middle_grad = seed_grad + middle_from_norm
    down_sums = settle((down_grad, down_bias_grad, up_bias_grad))
    up_sums = settle((up_grad, owner_order(gain_second_grad), owner_order(shift_second_grad)))
    attended_grad = middle_grad.astype(jnp.bfloat16)
    out_grad = jnp.dot(owner_order(mixed_low).T, attended_grad, preferred_element_type=jnp.float32)
    out_bias_grad = owner_order(jnp.sum(attended_grad.astype(jnp.float32), 0))
    mixed_grad = (
        jnp.dot(attended_grad, gathered[4].T, preferred_element_type=jnp.float32)
        .astype(jnp.bfloat16)
        .reshape(row_count, head_count, head_size)
    )
    scores_back = head_scores(query_heads, key_heads_back, query_pos, key_pos, seq_length)
    probs_back = jnp.exp(scores_back - log_total)
    probs_grad = jnp.einsum(
        "qhd,khd->hqk", mixed_grad, value_heads_back, preferred_element_type=jnp.float32
    )
    value_part = jnp.einsum(
        "hqk,qhd->khd",
        probs_back.astype(jnp.bfloat16),
        mixed_grad,
        preferred_element_type=jnp.float32,
    ).reshape(group_size, feature_count)
    row_dot = jnp.sum(probs_back * probs_grad, -1, keepdims=True)
    score_grad = (probs_back * (probs_grad - row_dot)).astype(jnp.bfloat16)
    query_grad = (
        jnp.einsum("hqk,khd->qhd", score_grad, key_heads_back, preferred_element_type=jnp.float32)
        * score_scale
    )
    key_part = (
        jnp.einsum(
            "hqk,qhd->khd", score_grad, query_heads, preferred_element_type=jnp.float32
        ).reshape(group_size, feature_count)
        * score_scale
    )
    key_grad, value_grad = (
        lax.psum_scatter(
            key_part.astype(jnp.bfloat16), "shard", scatter_dimension=0, tiled=True
        ).astype(jnp.float32),
        lax.psum_scatter(
            value_part.astype(jnp.bfloat16), "shard", scatter_dimension=0, tiled=True
        ).astype(jnp.float32),
    )
    joint_grad = jnp.concatenate(
        [query_grad.reshape(row_count, feature_count), key_grad, value_grad], 1
    ).astype(jnp.bfloat16)
    qkv_grad = jnp.dot(owner_order(normed_low).T, joint_grad, preferred_element_type=jnp.float32)
    joint_sums = jnp.sum(joint_grad.astype(jnp.float32), 0)
    qv_bias_grad = owner_order(
        jnp.concatenate([joint_sums[:feature_count], joint_sums[2 * feature_count :]], 0)
    )
    normed_grad = jnp.dot(joint_grad, gathered[2].T, preferred_element_type=jnp.float32)
    unused_three, first_pull = jax.vjp(layer_norm, rows_in, gain_first, shift_first)
    rows_from_norm, gain_first_grad, shift_first_grad = first_pull(normed_grad)
    tokens_grad = middle_grad + rows_from_norm
    attn_sums = settle(
        (
            qkv_grad,
            qv_bias_grad,
            out_grad,
            out_bias_grad,
            owner_order(gain_first_grad),
            owner_order(shift_first_grad),
        )
    )
    return (
        layer_out,
        tokens_grad,
        attn_sums[4],
        attn_sums[5],
        attn_sums[0],
        attn_sums[1],
        attn_sums[2],
        attn_sums[3],
        up_sums[1],
        up_sums[2],
        up_sums[0],
        down_sums[2],
        down_sums[0],
        down_sums[1],
    )


PLANE = 8
DEPTH = 4
QUARTERS = 4
VMEM_BYTES = 60 * 2**20
ORDER = (0, 2, 1, 3, 4, 6, 5, 7)


def is_planes(mesh):
    return mesh.shape["rep"] == PLANE and mesh.shape["shard"] == DEPTH


def over_rep(value, flip):
    return lax.ppermute(value, "rep", [(i, i ^ flip) for i in range(PLANE)])


def over_z(value, step):
    return lax.ppermute(value, "shard", [(i, (i + step) % DEPTH) for i in range(DEPTH)])


def over_all(value, place):
    pairs = [(i, place(i)) for i in range(PLANE * DEPTH) if place(i) is not None]
    return lax.ppermute(value, ("rep", "shard"), pairs)


def home_of(index):
    rep, z = index // DEPTH, index % DEPTH
    y, x, core = rep >> 2, (rep >> 1) & 1, rep & 1
    return (4 * x + 2 * (z & 1) + (z >> 1)) * DEPTH + 2 * core + y


HOME = [home_of(i) for i in range(PLANE * DEPTH)]


def to_home(value):
    return over_all(value, lambda i: HOME[i])


def from_home(value):
    return over_all(value, HOME.index)


def after(value, *earlier):
    return lax.optimization_barrier((value, *earlier))[0]


def gather_plane(rows, earlier=()):
    near = over_rep(rows, 1)
    two, four, six = after(tuple(over_rep(rows, flip) for flip in (2, 4, 6)), earlier)
    return [rows, near, two, over_rep(two, 1), four, over_rep(four, 1), six, over_rep(six, 1)]


def add_halves(keep, received):
    count, features = keep.shape[2:]

    def kernel(keep_ref, received_ref, own_ref, two_ref, four_ref, six_ref, left, right, sems):
        outs = {0: own_ref, 2: two_ref, 4: four_ref, 6: six_ref}
        copies = {}
        for flip in (6, 2, 4, 0):
            y, x = flip >> 2, (flip >> 1) & 1
            copies[flip] = [
                pltpu.make_async_copy(ref.at[y, x], to.at[y, x], sems.at[i, flip // 2])
                for i, (ref, to) in enumerate(((keep_ref, left), (received_ref, right)))
            ]
            for copy in copies[flip]:
                copy.start()
        for flip in (6, 2, 4, 0):
            y, x = flip >> 2, (flip >> 1) & 1
            wait_all(copies[flip])
            total = left[y, x].astype(jnp.float32) + right[y, x].astype(jnp.float32)
            outs[flip][...] = total.astype(outs[flip].dtype)

    low = sds((count, features), jnp.bfloat16)
    return kernel_call(
        kernel,
        [ANYWHERE] * 2,
        [sds((count, features), jnp.float32), low, low, low],
        [
            pltpu.VMEM(keep.shape, keep.dtype),
            pltpu.VMEM(keep.shape, keep.dtype),
            pltpu.SemaphoreType.DMA((2, 4)),
        ],
        0,
        (keep, received),
    )


def send_parts(parts):
    own, *others = parts
    return [own] + [over_rep(part, flip) for part, flip in zip(others, (2, 4, 6))]


def scattered_over_z(blocks):
    return lax.psum_scatter(blocks, "shard", scatter_dimension=0, tiled=False)


def outer(left, right):
    return lax.dot_general(
        left, right, (((0,), (0,)), ((), ())), preferred_element_type=jnp.float32
    )


def spread_columns(arrived):
    count = arrived.shape[1]
    parts = arrived.reshape(PLANE, count, -1, 128)
    return jnp.transpose(parts, (1, 2, 0, 3)).reshape(count, -1).astype(jnp.float32)


def dot_nn(left, right):
    return jnp.dot(left, right, preferred_element_type=jnp.float32)


def dot_nt(left, right):
    return lax.dot_general(
        left, right, (((1,), (1,)), ((), ())), preferred_element_type=jnp.float32
    )


def place_pieces(pieces, whole, sems):
    z = lax.axis_index("shard")
    rows = pieces[0].shape[0]
    copies = []
    for step, piece in enumerate(pieces):
        plane = lax.rem(z + (DEPTH - step), DEPTH)
        at = pl.ds(pl.multiple_of(plane * rows, rows), rows)
        copies.append(pltpu.make_async_copy(piece, whole.at[at], sems.at[step]))
    for copy in copies:
        copy.start()
    return copies


def wait_all(copies):
    for copy in copies:
        copy.wait()


def quarter_of(rep):
    return 2 * (rep & 1) + ((rep >> 1) & 1)


def row_positions(shape, axis, rep, first):
    index = lax.broadcasted_iota(jnp.int32, shape, axis) + first
    return (((index >> 7) ^ quarter_of(rep)) << 7) + (index & 127)


def load_blocks(blocks, whole, sems):
    count = whole.shape[0] // PLANE
    copies = []
    for place, k in enumerate(ORDER):
        at = pl.ds(place * count, count)
        block = blocks[k].at[pl.ds(0, count)]
        copies.append(pltpu.make_async_copy(block, whole.at[at], sems.at[place]))
        copies[-1].start()
    return copies


def load(ref, to, sem):
    copy = pltpu.make_async_copy(ref, to, sem)
    copy.start()
    return copy


def total_of(parts):
    own, two, four, six = parts
    return (own[...] + two[...].astype(jnp.float32)) + (
        four[...].astype(jnp.float32) + six[...].astype(jnp.float32)
    )


def unit_rows(v):
    centered = v - jnp.mean(v, 1, keepdims=True)
    rstd = lax.rsqrt(jnp.mean(centered * centered, 1, keepdims=True) + 1e-05)
    return centered * rstd, rstd


def norm_back(grad, xhat, rstd, gain):
    gx = grad * gain
    return rstd * (
        gx - jnp.mean(gx, 1, keepdims=True) - xhat * jnp.mean(gx * xhat, 1, keepdims=True)
    )


def scores_of(query, keys, slope, distance, allowed, scale):
    raw = dot_nt(query, keys) * scale - slope * distance
    return jnp.where(allowed, raw, -1e30)


VECTORS = ((0, 256), (1, 256), (6, 512), (2, 256), (3, 256), (4, 256), (8, 1024), (5, 256))
ANYWHERE = pl.BlockSpec(memory_space=pl.ANY)
LOCAL = pl.BlockSpec(memory_space=pltpu.VMEM)
SCALARS = pl.BlockSpec(memory_space=pltpu.SMEM)


def sds(shape, dtype):
    return jax.ShapeDtypeStruct(shape, dtype)


def kernel_call(kernel, ins, outs, scratch, flops, operands):
    return pl.pallas_call(
        kernel,
        out_shape=outs,
        in_specs=ins,
        out_specs=[LOCAL] * len(outs),
        scratch_shapes=scratch,
        compiler_params=pltpu.CompilerParams(vmem_limit_bytes=VMEM_BYTES),
        cost_estimate=pl.CostEstimate(flops=flops, bytes_accessed=2**23, transcendentals=2**20),
    )(*operands)


def own_eighths(qkv_weight, out_weight, up_weight, down_weight):
    height, features = qkv_weight.shape[0], out_weight.shape[1]
    units = up_weight.shape[1] // PLANE
    half = features // 2

    def kernel(qkv_ref, out_ref, up_ref, down_ref, qkv_own, out_own, wide_own, sems):
        rep = lax.axis_index("rep")
        moves = []
        for ref, own_ref in ((qkv_ref, qkv_own), (up_ref, wide_own)):
            for j in range(ref.shape[1] // (128 * PLANE)):
                at = pl.ds(pl.multiple_of(1024 * j + 128 * rep, 128), 128)
                moves.append((ref.at[:, at], own_ref.at[:, pl.ds(128 * j, 128)]))
        count = out_own.shape[0]
        at = pl.ds(pl.multiple_of((rep & 1) * count, count), count)
        moves.append((out_ref.at[at, :], out_own))
        count = down_ref.shape[0] // PLANE
        at = pl.ds(pl.multiple_of(rep * count, count), count)
        for j in range(2):
            moves.append(
                (
                    down_ref.at[at, pl.ds(j * half, half)],
                    wide_own.at[pl.ds(j * count, count), pl.ds(units, half)],
                )
            )
        copies = [
            pltpu.make_async_copy(src, dst, sems.at[i]) for i, (src, dst) in enumerate(moves)
        ]
        for copy in copies:
            copy.start()
        wait_all(copies)

    low = jnp.bfloat16
    return kernel_call(
        kernel,
        [ANYWHERE] * 4,
        [
            sds((height, qkv_weight.shape[1] // PLANE), low),
            sds((features // PLANE, features), low),
            sds((height, units + half), low),
        ],
        [pltpu.SemaphoreType.DMA((10,))],
        0,
        (qkv_weight, out_weight, up_weight, down_weight),
    )


def first_norm(moved, packs):
    count, features = moved.shape[0] // 2, moved.shape[1]

    def kernel(moved_ref, p0, p1, p2, p3, vectors_ref, normed_ref, tokens_ref):
        z = lax.axis_index("shard")
        packs = [ref[...].astype(jnp.float32) for ref in (p0, p1, p2, p3)]
        vectors_ref[...] = jnp.zeros_like(vectors_ref)
        for plane in range(DEPTH):
            back = lax.rem(z + (DEPTH - plane), DEPTH)
            pack = packs[3]
            for step in range(3):
                pack = jnp.where(back == step, packs[step], pack)
            start = 0
            for row, size in VECTORS:
                for i in range(size // 128):
                    at = plane * size + i * 128
                    lanes = pl.ds(at % 1024, 128)
                    vectors_ref[row + at // 1024 : row + at // 1024 + 1, lanes] = pack[
                        start + i : start + i + 1
                    ]
                start += size // 128
        tokens = moved_ref[:count]
        tokens_ref[...] = tokens
        xhat, unused = unit_rows(tokens.astype(jnp.float32))
        normed = xhat * vectors_ref[0:1, :] + vectors_ref[1:2, :]
        normed_ref[...] = normed.astype(jnp.bfloat16)

    return kernel_call(
        kernel,
        [LOCAL] * 5,
        [sds((16, features), jnp.float32), *[sds((count, features), jnp.bfloat16)] * 2],
        [],
        0,
        (moved, *packs),
    )


def second_norm(tokens, vectors, parts):
    def kernel(tokens_ref, vectors_ref, own, two, four, six, middle_ref, normed_ref):
        attended = total_of((own, two, four, six)) + vectors_ref[2:3, :]
        middle = tokens_ref[...].astype(jnp.float32) + attended
        middle_ref[...] = middle
        xhat, unused = unit_rows(middle)
        normed = xhat * vectors_ref[3:4, :] + vectors_ref[4:5, :]
        normed_ref[...] = normed.astype(jnp.bfloat16)

    return kernel_call(
        kernel,
        [LOCAL] * 6,
        [sds(tokens.shape, jnp.float32), sds(tokens.shape, jnp.bfloat16)],
        [],
        0,
        (tokens, vectors, *parts),
    )


def second_norm_back(vectors, middle, seed_low, parts):
    rows, features = middle.shape

    def kernel(
        vectors_ref, middle_ref, seed_ref, own, two, four, six,
        grad_ref, low_ref, sums_ref,
    ):
        seed = seed_ref[...].astype(jnp.float32)
        grad = total_of((own, two, four, six))
        xhat, rstd = unit_rows(middle_ref[...])
        total = seed + norm_back(grad, xhat, rstd, vectors_ref[3:4, :])
        grad_ref[...] = total
        low = total.astype(jnp.bfloat16)
        low_ref[...] = low
        sums_ref[0:1, :] = jnp.sum(grad * xhat, 0, keepdims=True)
        sums_ref[1:2, :] = jnp.sum(grad, 0, keepdims=True)
        sums_ref[2:3, :] = jnp.sum(low.astype(jnp.float32), 0, keepdims=True)
        sums_ref[3:4, :] = jnp.sum(seed, 0, keepdims=True)

    return kernel_call(
        kernel,
        [LOCAL] * 7,
        [
            sds((rows, features), jnp.float32),
            sds((rows, features), jnp.bfloat16),
            sds((4, features), jnp.float32),
        ],
        [],
        0,
        (vectors, middle, seed_low, *parts),
    )


def first_norm_back(tokens, vectors, middle_grad, parts):
    rows, features = tokens.shape

    def kernel(tokens_ref, vectors_ref, base_ref, own, two, four, six, grad_ref, sums_ref):
        grad = total_of((own, two, four, six))
        xhat, rstd = unit_rows(tokens_ref[...].astype(jnp.float32))
        total = base_ref[...] + norm_back(grad, xhat, rstd, vectors_ref[0:1, :])
        grad_ref[...] = total.astype(jnp.bfloat16)
        sums_ref[0:1, :] = jnp.sum(grad * xhat, 0, keepdims=True)
        sums_ref[1:2, :] = jnp.sum(grad, 0, keepdims=True)

    return kernel_call(
        kernel,
        [LOCAL] * 7,
        [sds((rows, features), jnp.bfloat16), sds((2, features), jnp.float32)],
        [],
        0,
        (tokens, vectors, middle_grad, *parts),
    )


def attention_forward(lens, slopes, blocks, weights, vectors):
    rows, features = PLANE * blocks[0].shape[0], blocks[0].shape[1]
    span = rows // 2
    width = weights[0].shape[1]
    own = width // 3
    head_size = own // 2
    scale = 1.0 / math.sqrt(head_size)
    step_rows = span // QUARTERS

    def kernel(
        own_length, other_length, slopes_ref, n0, n1, n2, n3, n4, n5, n6, n7, w0, w1, w2, w3,
        vectors_ref, joint_ref, mixed_ref, probs_ref, weight_ref, normed_ref, sems, more_sems,
    ):
        rep = lax.axis_index("rep")
        weight_copies = place_pieces((w0, w1, w2, w3), weight_ref, sems)
        copies = load_blocks((n0, n1, n2, n3, n4, n5, n6, n7), normed_ref, more_sems)
        mine = pl.ds(pl.multiple_of(rep * own, own), own)
        bias_q, bias_v = vectors_ref[6:7, mine], vectors_ref[7:8, mine]
        wait_all(weight_copies)
        for s in range(2):
            for c in range(2):
                at = pl.ds((2 * s + c) * (span // 2), span // 2)
                wait_all(copies[4 * s + 2 * c : 4 * s + 2 * c + 2])
                joint = dot_nn(normed_ref[at, :], weight_ref[...])
                joint_ref[at, :own] = (joint[:, :own] + bias_q).astype(jnp.bfloat16)
                joint_ref[at, own : 2 * own] = joint[:, own : 2 * own].astype(jnp.bfloat16)
                joint_ref[at, 2 * own :] = (joint[:, 2 * own :] + bias_v).astype(jnp.bfloat16)
        lane = lax.broadcasted_iota(jnp.int32, (step_rows, own), 1)
        key_pos = row_positions((1, span), 1, rep, 0)
        for s in range(2):
            keys = joint_ref[pl.ds(s * span, span), own : 2 * own]
            values = joint_ref[pl.ds(s * span, span), 2 * own :]
            length = (own_length, other_length)[s][0:1, 0:1]
            inside = key_pos.astype(jnp.float32) < length

            @pl.loop(0, QUARTERS)
            def _(i):
                first = pl.multiple_of(i * step_rows, step_rows)
                at = pl.ds(s * span + first, step_rows)
                query_pos = row_positions((step_rows, 1), 0, rep, first)
                allowed = (key_pos <= query_pos) & inside
                distance = (query_pos - key_pos).astype(jnp.float32)
                query = joint_ref[at, :own]
                mixed = jnp.zeros((step_rows, own), jnp.float32)
                for j in range(2):
                    mine = (lane >= j * head_size) & (lane < (j + 1) * head_size)
                    masked = jnp.where(mine, query, jnp.zeros_like(query))
                    scores = scores_of(masked, keys, slopes_ref[j], distance, allowed, scale)
                    top = jnp.max(scores, 1, keepdims=True)
                    exps = jnp.exp(scores - top)
                    probs = exps * (1.0 / jnp.sum(exps, 1, keepdims=True))
                    probs_low = probs.astype(jnp.bfloat16)
                    probs_ref[j, at, :] = probs_low
                    mixed = jnp.where(mine, dot_nn(probs_low, values), mixed)
                mixed_ref[at, :] = mixed.astype(jnp.bfloat16)

    return kernel_call(
        kernel,
        [LOCAL] * 2 + [SCALARS] + [ANYWHERE] * 12 + [LOCAL],
        [
            sds((rows, width), jnp.bfloat16),
            sds((rows, own), jnp.bfloat16),
            sds((2, rows, span), jnp.bfloat16),
        ],
        [
            pltpu.VMEM((features, width), jnp.bfloat16),
            pltpu.VMEM((rows, features), jnp.bfloat16),
            pltpu.SemaphoreType.DMA((DEPTH,)),
            pltpu.SemaphoreType.DMA((PLANE,)),
        ],
        2 * rows * features * width + 8 * rows * span * own,
        (*lens, slopes, *blocks, *weights, vectors),
    )


def out_projection(mixed, out_part):
    rows, features = mixed.shape[0], out_part.shape[1]
    tile = rows // 4

    def kernel(mixed_ref, out_ref, keep_ref, give_ref):
        for s in range(2):
            for c, part_ref in enumerate((keep_ref, give_ref)):
                at = pl.ds((2 * s + c) * tile, tile)
                part = dot_nn(mixed_ref[at, :], out_ref[...]).astype(jnp.bfloat16)
                part_ref[s] = part.reshape(2, tile // 2, features)

    half = sds((2, 2, tile // 2, features), jnp.bfloat16)
    return kernel_call(
        kernel, [LOCAL] * 2, [half, half], [], 2 * rows * features * mixed.shape[1], (mixed, out_part)
    )


def attention_backward(probs, blocks, joint, weights, out_part):
    rows, features = PLANE * blocks[0].shape[0], blocks[0].shape[1]
    span = rows // 2
    width = weights[0].shape[1]
    own = width // 3
    head_size = own // 2
    scale = 1.0 / math.sqrt(head_size)
    step_rows = span // QUARTERS

    def kernel(
        probs_hbm, g0, g1, g2, g3, g4, g5, g6, g7,
        joint_hbm, w0, w1, w2, w3, out_ref,
        joint_grad_ref, sums_ref, keep_ref, give_ref,
        weight_ref, mixed_grad_ref, key_acc, value_acc, joint_ref, grad_ref, out_all, probs_ref, sems,
        more_sems, probs_sem,
    ):
        out_copy = load(out_ref, out_all, sems.at[DEPTH])
        grad_copies = load_blocks((g0, g1, g2, g3, g4, g5, g6, g7), grad_ref, more_sems)
        joint_copy = load(joint_hbm, joint_ref, sems.at[DEPTH + 1])
        probs_copy = load(probs_hbm, probs_ref, probs_sem.at[0])
        copies = place_pieces((w0, w1, w2, w3), weight_ref, sems)
        out_copy.wait()
        for s in range(2):
            for c in range(2):
                at = pl.ds((2 * s + c) * (span // 2), span // 2)
                wait_all(grad_copies[4 * s + 2 * c : 4 * s + 2 * c + 2])
                mixed_grad = dot_nt(grad_ref[at, :], out_all[...])
                mixed_grad_ref[at, :] = mixed_grad.astype(jnp.bfloat16)
        joint_copy.wait()
        probs_copy.wait()
        lane = lax.broadcasted_iota(jnp.int32, (step_rows, own), 1)
        lane_all = lax.broadcasted_iota(jnp.int32, (span, own), 1)
        for s in range(2):
            keys = joint_ref[pl.ds(s * span, span), own : 2 * own]
            values = joint_ref[pl.ds(s * span, span), 2 * own :]
            key_acc[...] = jnp.zeros_like(key_acc)
            value_acc[...] = jnp.zeros_like(value_acc)

            @pl.loop(0, QUARTERS)
            def _(i):
                first = pl.multiple_of(i * step_rows, step_rows)
                at = pl.ds(s * span + first, step_rows)
                query = joint_ref[at, :own]
                mixed_grad = mixed_grad_ref[at, :]
                query_grad = jnp.zeros((step_rows, own), jnp.float32)
                for j in range(2):
                    mine = (lane >= j * head_size) & (lane < (j + 1) * head_size)
                    masked = jnp.where(mine, query, jnp.zeros_like(query))
                    masked_grad = jnp.where(mine, mixed_grad, jnp.zeros_like(mixed_grad))
                    probs_low = probs_ref[j, at, :]
                    probs = probs_low.astype(jnp.float32)
                    probs_grad = dot_nt(masked_grad, values)
                    row_dot = jnp.sum(probs * probs_grad, 1, keepdims=True)
                    score_grad = (probs * (probs_grad - row_dot)).astype(jnp.bfloat16)
                    query_grad = jnp.where(mine, dot_nn(score_grad, keys), query_grad)
                    key_acc[...] += outer(score_grad, masked)
                    value_acc[...] += outer(probs_low, masked_grad)
                joint_grad_ref[at, :own] = (query_grad * scale).astype(jnp.bfloat16)

            at = pl.ds(s * span, span)
            joint_grad_ref[at, own : 2 * own] = (key_acc[...] * scale).astype(jnp.bfloat16)
            joint_grad_ref[at, 2 * own :] = value_acc[...].astype(jnp.bfloat16)
        wait_all(copies)
        total = jnp.zeros((1, width), jnp.float32)
        for s in range(2):
            for c, part_ref in enumerate((keep_ref, give_ref)):
                at = pl.ds((2 * s + c) * (span // 2), span // 2)
                joint_grad = joint_grad_ref[at, :]
                total = total + jnp.sum(joint_grad.astype(jnp.float32), 0, keepdims=True)
                part = dot_nt(joint_grad, weight_ref[...]).astype(jnp.bfloat16)
                part_ref[s] = part.reshape(2, span // 4, features)
        sums_ref[...] = total

    half = sds((2, 2, span // 4, features), jnp.bfloat16)
    return kernel_call(
        kernel,
        [ANYWHERE] * 15,
        [sds((rows, width), jnp.bfloat16), sds((1, width), jnp.float32), half, half],
        [
            pltpu.VMEM((features, width), jnp.bfloat16),
            pltpu.VMEM((rows, own), jnp.bfloat16),
            pltpu.VMEM((span, own), jnp.float32),
            pltpu.VMEM((span, own), jnp.float32),
            pltpu.VMEM((rows, width), jnp.bfloat16),
            pltpu.VMEM((rows, features), jnp.bfloat16),
            pltpu.VMEM((own, features), jnp.bfloat16),
            pltpu.VMEM(probs.shape, jnp.bfloat16),
            pltpu.SemaphoreType.DMA((DEPTH + 2,)),
            pltpu.SemaphoreType.DMA((PLANE,)),
            pltpu.SemaphoreType.DMA((1,)),
        ],
        2 * rows * features * (width + own) + 20 * rows * span * own,
        (probs, *blocks, joint, *weights, out_part),
    )


def feed_forward(blocks, grads, wide, vectors):
    count, features = blocks[0].shape
    rows = PLANE * count
    half_width = features // 2
    units = wide.shape[1] - half_width
    tile = 2 * count
    root = math.sqrt(2.0 / math.pi)
    bend = 0.044715

    def kernel(
        n0, n1, n2, n3, n4, n5, n6, n7, g0, g1, g2, g3, g4, g5, g6, g7, wide_hbm, vectors_ref,
        active_ref, hidden_grad_ref, sums_ref, branch_keep_ref, branch_give_ref, keep_ref, give_ref,
        up_ref, down_ref, normed_ref, grad_ref, sems, grad_sems, more_sems,
    ):
        rep = lax.axis_index("rep")
        up_copies = [load(wide_hbm.at[:, pl.ds(0, units)], up_ref, more_sems.at[0])]
        copies = load_blocks((n0, n1, n2, n3, n4, n5, n6, n7), normed_ref, sems)
        grad_copies = load_blocks((g0, g1, g2, g3, g4, g5, g6, g7), grad_ref, grad_sems)
        down_copies = []
        for p in range(DEPTH):
            for j in range(2):
                source = wide_hbm.at[pl.ds((2 * p + j) * 128, 128), pl.ds(units, half_width)]
                to = down_ref.at[pl.ds(p * 128, 128), pl.ds(j * half_width, half_width)]
                down_copies.append(load(source, to, more_sems.at[2 + 2 * p + j]))
        mine = pl.ds(pl.multiple_of(rep * 128, 128), 128)
        bias = jnp.concatenate([vectors_ref[8 + p : 9 + p, mine] for p in range(DEPTH)], 1)
        total = jnp.zeros((1, units), jnp.float32)
        for s in range(2):
            for c in range(2):
                at = pl.ds((2 * s + c) * tile, tile)
                if (s, c) == (0, 0):
                    wait_all(up_copies)
                wait_all(copies[4 * s + 2 * c : 4 * s + 2 * c + 2])
                v = dot_nn(normed_ref[at, :], up_ref[...]) + bias
                square = v * v
                t = jnp.tanh(root * v * (1.0 + bend * square))
                half = 0.5 * (1.0 + t)
                active = (v * half).astype(jnp.bfloat16)
                slope = half + (0.5 * root) * v * (1.0 - t * t) * (1.0 + 3.0 * bend * square)
                if (s, c) == (0, 0):
                    wait_all(grad_copies)
                    wait_all(down_copies)
                hidden_grad = (dot_nt(grad_ref[at, :], down_ref[...]) * slope).astype(jnp.bfloat16)
                hidden_grad_ref[at, :] = hidden_grad
                total = total + jnp.sum(hidden_grad.astype(jnp.float32), 0, keepdims=True)
                back = dot_nt(hidden_grad, up_ref[...]).astype(jnp.bfloat16)
                (keep_ref, give_ref)[c][s] = back.reshape(2, count, features)
                branch = dot_nn(active, down_ref[...]).astype(jnp.bfloat16)
                active_ref[at, :] = active
                (branch_keep_ref, branch_give_ref)[c][s] = branch.reshape(2, count, features)
        sums_ref[...] = total

    half = sds((2, 2, count, features), jnp.bfloat16)
    return kernel_call(
        kernel,
        [ANYWHERE] * 17 + [LOCAL],
        [
            sds((rows, units), jnp.bfloat16),
            sds((rows, units), jnp.bfloat16),
            sds((1, units), jnp.float32),
            half,
            half,
            half,
            half,
        ],
        [
            pltpu.VMEM((features, units), jnp.bfloat16),
            pltpu.VMEM((units, features), jnp.bfloat16),
            pltpu.VMEM((rows, features), jnp.bfloat16),
            pltpu.VMEM((rows, features), jnp.bfloat16),
            pltpu.SemaphoreType.DMA((PLANE,)),
            pltpu.SemaphoreType.DMA((PLANE,)),
            pltpu.SemaphoreType.DMA((2 + 2 * DEPTH,)),
        ],
        8 * rows * features * units,
        (*blocks, *grads, wide, vectors),
    )


def feed_forward_weights(blocks, hidden_grad, active, grads):
    count, features = blocks[0].shape
    rows, units = hidden_grad.shape

    def kernel(
        n0, n1, n2, n3, n4, n5, n6, n7, g0, g1, g2, g3, g4, g5, g6, g7, hidden_grad_hbm, active_hbm,
        wide_ref, normed_ref, hidden_grad_ref, active_ref, grad_ref, sems, grad_sems, more_sems,
    ):
        active_copies = [load(active_hbm, active_ref, more_sems.at[0])]
        active_copies += load_blocks((g0, g1, g2, g3, g4, g5, g6, g7), grad_ref, grad_sems)
        copies = [load(hidden_grad_hbm, hidden_grad_ref, more_sems.at[1])]
        copies += load_blocks((n0, n1, n2, n3, n4, n5, n6, n7), normed_ref, sems)
        wait_all(active_copies)
        for p in range(DEPTH):
            part = active_ref[:, p * 128 : (p + 1) * 128]
            down = outer(part, grad_ref[...]).astype(jnp.bfloat16)
            wide_ref[p, :128, units:] = down[:, : features // 2]
            wide_ref[p, 128:, units:] = down[:, features // 2 :]
        wait_all(copies)
        for r in range(PLANE):
            part = outer(normed_ref[:, r * 128 : (r + 1) * 128], hidden_grad_ref[...])
            part = part.astype(jnp.bfloat16).reshape(DEPTH, 32, units)
            wide_ref[:, r * 32 : (r + 1) * 32, :units] = part

    low = jnp.bfloat16
    return kernel_call(
        kernel,
        [ANYWHERE] * 18,
        [sds((DEPTH, PLANE * 32, units + features // 2), low)],
        [
            pltpu.VMEM((rows, features), low),
            pltpu.VMEM((rows, units), low),
            pltpu.VMEM((rows, units), low),
            pltpu.VMEM((rows, features), low),
            pltpu.SemaphoreType.DMA((PLANE,)),
            pltpu.SemaphoreType.DMA((PLANE,)),
            pltpu.SemaphoreType.DMA((2,)),
        ],
        4 * rows * features * units,
        (*blocks, *grads, hidden_grad, active),
    )[0]


def qkv_weights(blocks, joint_grad):
    features = blocks[0].shape[1]
    rows, width = joint_grad.shape

    def kernel(
        n0, n1, n2, n3, n4, n5, n6, n7, joint_grad_hbm,
        q0, q1, q2, q3, normed_ref, joint_grad_ref, sems, more_sems,
    ):
        z = lax.axis_index("shard")
        copies = [load(joint_grad_hbm, joint_grad_ref, more_sems.at[0])]
        copies += load_blocks((n0, n1, n2, n3, n4, n5, n6, n7), normed_ref, sems)
        wait_all(copies)
        for r in range(PLANE):
            part = outer(normed_ref[:, r * 128 : (r + 1) * 128], joint_grad_ref[...])
            part = part.astype(jnp.bfloat16).reshape(DEPTH, 32, width)
            for step, ref in enumerate((q0, q1, q2, q3)):
                for p in range(DEPTH):

                    @pl.when(lax.rem(z + step, DEPTH) == p)
                    def _():
                        ref[r] = part[p]

    low = jnp.bfloat16
    return kernel_call(
        kernel,
        [ANYWHERE] * 9,
        [sds((PLANE, 32, width), low)] * 4,
        [
            pltpu.VMEM((rows, features), low),
            pltpu.VMEM((rows, width), low),
            pltpu.SemaphoreType.DMA((PLANE,)),
            pltpu.SemaphoreType.DMA((1,)),
        ],
        2 * rows * features * width,
        (*blocks, joint_grad),
    )


def out_weights(mixed, grads):
    count, features = grads[0].shape
    rows, own = mixed.shape

    def kernel(mixed_ref, g0, g1, g2, g3, g4, g5, g6, g7, out_ref, grad_ref, sems):
        wait_all(load_blocks((g0, g1, g2, g3, g4, g5, g6, g7), grad_ref, sems))
        part = outer(mixed_ref[...], grad_ref[...])
        out_ref[...] = part.astype(jnp.bfloat16).reshape(DEPTH, own // DEPTH, features)

    return kernel_call(
        kernel,
        [LOCAL] + [ANYWHERE] * 8,
        [sds((DEPTH, own // DEPTH, features), jnp.bfloat16)],
        [pltpu.VMEM((rows, features), jnp.bfloat16), pltpu.SemaphoreType.DMA((PLANE,))],
        2 * rows * features * own,
        (mixed, *grads),
    )[0]


def body_planes(
    tokens,
    cotangent,
    lengths,
    assign,
    first_gain,
    first_shift,
    qkv_weight,
    qv_bias,
    out_weight,
    out_bias,
    second_gain,
    second_shift,
    up_weight,
    up_bias,
    down_weight,
    down_bias,
):
    row_count, feature_count = tokens.shape
    rep = lax.axis_index("rep")
    z = lax.axis_index("shard")
    own = feature_count // PLANE
    devices = PLANE * DEPTH

    small = (
        first_gain,
        first_shift,
        qv_bias,
        out_bias,
        second_gain,
        second_shift,
        up_bias,
        down_bias,
    )
    whole = sum(item.shape[0] for item in small)
    start = 0
    packed = jnp.zeros((whole,), jnp.bfloat16)
    for item in small:
        packed = packed + jnp.pad(item, (start, whole - start - item.shape[0]))
        start += item.shape[0]
    packed = packed.reshape(-1, 128)
    packs = [packed] + [over_z(packed, step) for step in (1, 2, 3)]
    moved = to_home(jnp.concatenate([tokens, cotangent], 0))
    own_length = jnp.sum(jnp.where(jnp.arange(lengths.shape[0]) == assign[0], lengths, 0))
    length = to_home(jnp.full((8, 128), own_length.astype(jnp.float32)))
    lens = (length, over_rep(length, 4))

    weights = after((qkv_weight, out_weight, up_weight, down_weight), moved, packs, lens)
    qkv_own, out_own, wide_own = own_eighths(*weights)
    vectors, normed, tokens = first_norm(moved, packs)
    qkv_own = after(qkv_own, normed)
    qkv_parts = [qkv_own] + [over_z(qkv_own, step) for step in (1, 2, 3)]
    normed_blocks = gather_plane(normed, qkv_parts)
    cotangent = after(moved, normed_blocks)[row_count:]
    position = quarter_of(rep) * row_count + jnp.arange(row_count)
    valid = position.astype(jnp.float32) < length[0, 0]
    branch_grad = jnp.where(valid[:, None], cotangent, jnp.zeros_like(cotangent))
    branch_near = [over_rep(branch_grad, flip) for flip in (1, 2, 4, 6)]
    heads = (2 * rep + jnp.arange(2)).astype(jnp.float32)
    slopes = jnp.exp2(-8.0 * (heads + 1.0) / HEADS)
    joint, mixed, probs = attention_forward(lens, slopes, normed_blocks, qkv_parts, vectors)
    out_moved = [
        over_all(
            after(out_own, qkv_parts),
            lambda i, step=step: (
                i - i % DEPTH + (i % DEPTH + step) % DEPTH if i % DEPTH == i // 8 else None
            ),
        )
        for step in (1, 2, 3)
    ]
    out_part = jnp.where(z == rep >> 1, out_own, jnp.zeros_like(out_own))
    out_moved, branch_near = after((out_moved, branch_near), mixed)
    for piece in out_moved:
        out_part = out_part + piece
    branch_blocks = [branch_grad, branch_near[0]]
    for block in branch_near[1:]:
        branch_blocks += [block, over_rep(block, 1)]
    wide_all = lax.all_gather(after(wide_own, out_part), "shard", axis=0, tiled=True)
    keep, give = out_projection(mixed, out_part)
    parts = send_parts(add_halves(keep, over_rep(give, 1)))
    middle, normed_two = second_norm(tokens, vectors, parts)
    normed_two_blocks = gather_plane(normed_two)
    active, hidden_grad, hidden_sums, branch_keep, branch_give, keep, give = feed_forward(
        normed_two_blocks, branch_blocks, wide_all, vectors
    )
    received = over_rep(give, 1)
    parts = send_parts(add_halves(keep, received))
    branch_received = over_rep(after(branch_give, received), 1)
    branch_halves = add_halves(branch_keep, after(branch_received, parts[0]))
    wide_slice = feed_forward_weights(
        normed_two_blocks, after(hidden_grad, parts[0]), active, branch_blocks
    )
    middle_grad, attended_grad, second_sums = second_norm_back(
        vectors, middle, branch_grad, after(parts, wide_slice, branch_halves)
    )
    wide_summed = scattered_over_z(after(wide_slice, attended_grad))
    attended_blocks = gather_plane(attended_grad)
    branch_own, *branch_rest = send_parts(branch_halves)
    joint_grad, joint_sums, keep, give = attention_backward(
        probs, attended_blocks, joint, qkv_parts, out_part
    )
    received = over_rep(after(give, branch_rest), 1)
    qkv_slices = qkv_weights(normed_blocks, joint_grad)
    parts = send_parts(add_halves(keep, after(received, qkv_slices)))
    qkv_slices = [qkv_slices[0]] + [over_z(qkv_slices[step], step) for step in (1, 2, 3)]
    out_slice = out_weights(after(mixed, parts[0]), attended_blocks)
    tokens_grad, first_sums = first_norm_back(
        tokens, vectors, middle_grad, after(parts, out_slice, qkv_slices)
    )
    tokens_grad = from_home(tokens_grad)
    units = wide_summed.shape[1] - feature_count // 2
    wide_summed, qkv_slices = after((wide_summed, qkv_slices), first_sums)
    up_summed = wide_summed[:, :units].reshape(PLANE, -1, units)
    qkv_summed = qkv_slices[0].astype(jnp.float32)
    for step in (1, 2, 3):
        qkv_summed = qkv_summed + qkv_slices[step].astype(jnp.float32)
    both = jnp.concatenate([up_summed, qkv_summed.astype(jnp.bfloat16)], 2)
    arrived = lax.all_to_all(both, "rep", 0, 0, tiled=True)
    up_grad = spread_columns(arrived[:, :, :units])
    qkv_grad = spread_columns(arrived[:, :, units:])
    out_grad = scattered_over_z(out_slice).astype(jnp.float32)
    down_summed = jnp.concatenate([wide_summed[:128, units:], wide_summed[128:, units:]], 1)
    down_grad = over_all(
        down_summed,
        lambda i: (2 * (i % DEPTH) + i // 16) * DEPTH + (i // DEPTH) % DEPTH,
    )
    branch = branch_own + sum(part.astype(jnp.float32) for part in branch_rest)
    layer_low = (middle + branch + vectors[5:6]).astype(jnp.bfloat16)
    layer_out = from_home(after(layer_low, parts[0]))

    at_rep = (jnp.arange(PLANE) == rep)[None, :, None]

    def placed(sums):
        return jnp.where(at_rep, sums.reshape(-1, 1, 128), 0.0).reshape(-1)

    joint_parts = joint_sums.reshape(3, own)
    small_grads = (
        first_sums[0],
        first_sums[1],
        placed(jnp.concatenate([joint_parts[:1], joint_parts[2:]], 0)),
        second_sums[2],
        second_sums[0],
        second_sums[1],
        placed(hidden_sums),
        second_sums[3],
    )
    small_packed = jnp.concatenate(
        [g.reshape(devices, g.shape[0] // devices) for g in small_grads], 1
    ).astype(jnp.bfloat16)
    small_arrived = lax.all_to_all(after(small_packed, arrived), ("rep", "shard"), 0, 0, tiled=True)
    layer_out, tokens_grad, down_grad = (
        moved_back.astype(jnp.float32)
        for moved_back in after((layer_out, tokens_grad, down_grad), arrived)
    )
    small_sums = jnp.sum(small_arrived.astype(jnp.float32), 0)
    sums = []
    start = 0
    for g in small_grads:
        size = g.shape[0] // devices
        sums.append(small_sums[start : start + size])
        start += size
    return (
        layer_out,
        tokens_grad,
        sums[0],
        sums[1],
        qkv_grad,
        sums[2],
        out_grad,
        sums[3],
        sums[4],
        sums[5],
        up_grad,
        sums[6],
        down_grad,
        sums[7],
    )


def solution(mesh):
    return jax.shard_map(
        body_planes if is_planes(mesh) else body_generic,
        mesh=mesh,
        in_specs=(
            P(("rep", "shard"), None),
            P(("rep", "shard"), None),
            P(),
            P("rep"),
            P("shard"),
            P("shard"),
            P("shard", None),
            P("shard"),
            P("shard", None),
            P("shard"),
            P("shard"),
            P("shard"),
            P("shard", None),
            P("shard"),
            P("shard", None),
            P("shard"),
        ),
        out_specs=(
            P(("rep", "shard"), None),
            P(("rep", "shard"), None),
            P(("rep", "shard")),
            P(("rep", "shard")),
            P(("rep", "shard"), None),
            P(("rep", "shard")),
            P(("rep", "shard"), None),
            P(("rep", "shard")),
            P(("rep", "shard")),
            P(("rep", "shard")),
            P(("rep", "shard"), None),
            P(("rep", "shard")),
            P(("rep", "shard"), None),
            P(("rep", "shard")),
        ),
        check_vma=False,
    )
```

```python
import math

import jax
import jax.numpy as jnp
from jax import lax
from jax.experimental import pallas as pl
from jax.experimental.pallas import tpu as pltpu
from jax.sharding import PartitionSpec as P

HEADS = 16


def for_sending(value):
    return jax.tree.map(lambda a: a.astype(jnp.bfloat16) if a.dtype == jnp.float32 else a, value)


def cut_along(value, dim, devices):
    before, after = (value.shape[:dim], value.shape[dim + 1 :])
    return jnp.moveaxis(value.reshape(*before, devices, -1, *after), dim, 0)


def summed_on_arrival(value, axis, dim):
    blocks = cut_along(value, dim, lax.axis_size(axis))
    arrived = lax.all_to_all(blocks, axis, split_axis=0, concat_axis=0, tiled=True)
    return arrived.astype(jnp.float32).sum(axis=0)


def layer_norm(rows_in, norm_gain, norm_shift):
    row_mean = jnp.mean(rows_in, -1, keepdims=True)
    centered = rows_in - row_mean
    variance = jnp.mean(centered * centered, -1, keepdims=True)
    return centered * lax.rsqrt(variance + 1e-05) * norm_gain + norm_shift


def gelu_tanh(values_in):
    return jax.nn.gelu(values_in, approximate=True)


def owner_order(values):
    rep_count = lax.axis_size("rep")
    shard_count = lax.axis_size("shard")
    lead = values.shape[:-1]
    width = values.shape[-1]
    block = width // (rep_count * shard_count)
    arranged = values.reshape(lead + (rep_count, shard_count, block))
    return jnp.swapaxes(arranged, -3, -2).reshape(lead + (width,))


def settle(grads):
    group_summed = jax.tree.map(
        lambda part: part.astype(jnp.float32),
        lax.psum_scatter(for_sending(grads), "shard", scatter_dimension=0, tiled=True),
    )
    return jax.tree.map(lambda part: summed_on_arrival(part, "rep", 0), for_sending(group_summed))


def head_scores(query_heads, key_heads, query_pos, key_pos, seq_length):
    head_count = query_heads.shape[1]
    score_scale = 1.0 / math.sqrt(query_heads.shape[2])
    slopes = jnp.exp2(-8.0 * (jnp.arange(head_count).astype(jnp.float32) + 1.0) / head_count)
    raw_scores = (
        jnp.einsum("qhd,khd->hqk", query_heads, key_heads, preferred_element_type=jnp.float32)
        * score_scale
    )
    distance = (query_pos[:, None] - key_pos[None, :]).astype(jnp.float32)
    raw_scores = raw_scores - slopes[:, None, None] * distance[None]
    allowed = (key_pos[None, :] <= query_pos[:, None]) & (key_pos[None, :] < seq_length)
    return jnp.where(allowed[None], raw_scores, -1e30)


def body_generic(
    tokens,
    cotangent,
    lengths,
    assign,
    first_gain,
    first_shift,
    qkv_weight,
    qv_bias,
    out_weight,
    out_bias,
    second_gain,
    second_shift,
    up_weight,
    up_bias,
    down_weight,
    down_bias,
):
    rows_in = tokens.astype(jnp.float32)
    row_count = rows_in.shape[0]
    feature_count = rows_in.shape[1]
    head_count = HEADS
    head_size = feature_count // head_count
    score_scale = 1.0 / math.sqrt(head_size)
    group_size = row_count * lax.axis_size("shard")
    seq_length = jnp.sum(jnp.where(jnp.arange(lengths.shape[0]) == assign[0], lengths, 0))
    query_pos = lax.axis_index("shard") * row_count + jnp.arange(row_count)
    key_pos = jnp.arange(group_size)
    row_valid = (query_pos < seq_length)[:, None]
    owned = (
        first_gain,
        first_shift,
        qkv_weight,
        qv_bias,
        out_weight,
        out_bias,
        second_gain,
        second_shift,
        up_weight,
        up_bias,
        down_weight,
        down_bias,
    )
    gathered = (
        lax.all_gather(owned[0], "shard", axis=0, tiled=True),
        lax.all_gather(owned[1], "shard", axis=0, tiled=True),
        lax.all_gather(owned[2], "shard", axis=0, tiled=True),
        lax.all_gather(owned[3], "shard", axis=0, tiled=True),
        lax.all_gather(owned[4], "shard", axis=0, tiled=True),
        lax.all_gather(owned[5], "shard", axis=0, tiled=True),
        lax.all_gather(owned[6], "shard", axis=0, tiled=True),
        lax.all_gather(owned[7], "shard", axis=0, tiled=True),
        lax.all_gather(owned[8], "shard", axis=0, tiled=True),
        lax.all_gather(owned[9], "shard", axis=0, tiled=True),
        lax.all_gather(owned[10], "shard", axis=0, tiled=True),
        lax.all_gather(owned[11], "shard", axis=0, tiled=True),
    )
    gain_first = gathered[0].astype(jnp.float32)
    shift_first = gathered[1].astype(jnp.float32)
    bias_qv = gathered[3].astype(jnp.float32)
    bias_out = gathered[5].astype(jnp.float32)
    gain_second = gathered[6].astype(jnp.float32)
    shift_second = gathered[7].astype(jnp.float32)
    bias_up = gathered[9].astype(jnp.float32)
    bias_down = gathered[11].astype(jnp.float32)
    normed = layer_norm(rows_in, gain_first, shift_first)
    normed_low = normed.astype(jnp.bfloat16)
    joint_out = jnp.dot(normed_low, gathered[2], preferred_element_type=jnp.float32)
    query_low = (joint_out[:, :feature_count] + bias_qv[:feature_count]).astype(jnp.bfloat16)
    key_low = joint_out[:, feature_count : 2 * feature_count].astype(jnp.bfloat16)
    value_low = (joint_out[:, 2 * feature_count :] + bias_qv[feature_count:]).astype(jnp.bfloat16)
    key_all, value_all = (
        lax.all_gather(key_low, "shard", axis=0, tiled=True),
        lax.all_gather(value_low, "shard", axis=0, tiled=True),
    )
    query_heads = query_low.reshape(row_count, head_count, head_size)
    scores = head_scores(
        query_heads,
        key_all.reshape(group_size, head_count, head_size),
        query_pos,
        key_pos,
        seq_length,
    )
    row_top = jnp.max(scores, -1, keepdims=True)
    exp_scores = jnp.exp(scores - row_top)
    row_total = jnp.sum(exp_scores, -1, keepdims=True)
    log_total = row_top + jnp.log(row_total)
    attn_probs = exp_scores / row_total
    mixed_low = (
        jnp.einsum(
            "hqk,khd->qhd",
            attn_probs.astype(jnp.bfloat16),
            value_all.reshape(group_size, head_count, head_size),
            preferred_element_type=jnp.float32,
        )
        .reshape(row_count, feature_count)
        .astype(jnp.bfloat16)
    )
    attended = jnp.dot(mixed_low, gathered[4], preferred_element_type=jnp.float32) + bias_out
    middle = rows_in + attended
    normed_two_low = layer_norm(middle, gain_second, shift_second).astype(jnp.bfloat16)
    hidden = jnp.dot(normed_two_low, gathered[8], preferred_element_type=jnp.float32) + bias_up
    active_low = gelu_tanh(hidden).astype(jnp.bfloat16)
    branch = jnp.dot(active_low, gathered[10], preferred_element_type=jnp.float32) + bias_down
    layer_out = middle + branch
    back_keys = (key_all, value_all)
    key_heads_back = back_keys[0].reshape(group_size, head_count, head_size)
    value_heads_back = back_keys[1].reshape(group_size, head_count, head_size)
    seed_grad = jnp.where(row_valid, cotangent.astype(jnp.float32), 0.0)
    branch_grad = seed_grad.astype(jnp.bfloat16)
    down_grad = jnp.dot(owner_order(active_low).T, branch_grad, preferred_element_type=jnp.float32)
    down_bias_grad = owner_order(jnp.sum(branch_grad.astype(jnp.float32), 0))
    active_grad = jnp.dot(branch_grad, gathered[10].T, preferred_element_type=jnp.float32)
    unused, gelu_pull = jax.vjp(gelu_tanh, hidden)
    hidden_grad = gelu_pull(active_grad)[0].astype(jnp.bfloat16)
    up_grad = jnp.dot(
        owner_order(normed_two_low).T, hidden_grad, preferred_element_type=jnp.float32
    )
    up_bias_grad = owner_order(jnp.sum(hidden_grad.astype(jnp.float32), 0))
    normed_two_grad = jnp.dot(hidden_grad, gathered[8].T, preferred_element_type=jnp.float32)
    unused_two, second_pull = jax.vjp(layer_norm, middle, gain_second, shift_second)
    middle_from_norm, gain_second_grad, shift_second_grad = second_pull(normed_two_grad)
    middle_grad = seed_grad + middle_from_norm
    down_sums = settle((down_grad, down_bias_grad, up_bias_grad))
    up_sums = settle((up_grad, owner_order(gain_second_grad), owner_order(shift_second_grad)))
    attended_grad = middle_grad.astype(jnp.bfloat16)
    out_grad = jnp.dot(owner_order(mixed_low).T, attended_grad, preferred_element_type=jnp.float32)
    out_bias_grad = owner_order(jnp.sum(attended_grad.astype(jnp.float32), 0))
    mixed_grad = (
        jnp.dot(attended_grad, gathered[4].T, preferred_element_type=jnp.float32)
        .astype(jnp.bfloat16)
        .reshape(row_count, head_count, head_size)
    )
    scores_back = head_scores(query_heads, key_heads_back, query_pos, key_pos, seq_length)
    probs_back = jnp.exp(scores_back - log_total)
    probs_grad = jnp.einsum(
        "qhd,khd->hqk", mixed_grad, value_heads_back, preferred_element_type=jnp.float32
    )
    value_part = jnp.einsum(
        "hqk,qhd->khd",
        probs_back.astype(jnp.bfloat16),
        mixed_grad,
        preferred_element_type=jnp.float32,
    ).reshape(group_size, feature_count)
    row_dot = jnp.sum(probs_back * probs_grad, -1, keepdims=True)
    score_grad = (probs_back * (probs_grad - row_dot)).astype(jnp.bfloat16)
    query_grad = (
        jnp.einsum("hqk,khd->qhd", score_grad, key_heads_back, preferred_element_type=jnp.float32)
        * score_scale
    )
    key_part = (
        jnp.einsum(
            "hqk,qhd->khd", score_grad, query_heads, preferred_element_type=jnp.float32
        ).reshape(group_size, feature_count)
        * score_scale
    )
    key_grad, value_grad = (
        lax.psum_scatter(
            key_part.astype(jnp.bfloat16), "shard", scatter_dimension=0, tiled=True
        ).astype(jnp.float32),
        lax.psum_scatter(
            value_part.astype(jnp.bfloat16), "shard", scatter_dimension=0, tiled=True
        ).astype(jnp.float32),
    )
    joint_grad = jnp.concatenate(
        [query_grad.reshape(row_count, feature_count), key_grad, value_grad], 1
    ).astype(jnp.bfloat16)
    qkv_grad = jnp.dot(owner_order(normed_low).T, joint_grad, preferred_element_type=jnp.float32)
    joint_sums = jnp.sum(joint_grad.astype(jnp.float32), 0)
    qv_bias_grad = owner_order(
        jnp.concatenate([joint_sums[:feature_count], joint_sums[2 * feature_count :]], 0)
    )
    normed_grad = jnp.dot(joint_grad, gathered[2].T, preferred_element_type=jnp.float32)
    unused_three, first_pull = jax.vjp(layer_norm, rows_in, gain_first, shift_first)
    rows_from_norm, gain_first_grad, shift_first_grad = first_pull(normed_grad)
    tokens_grad = middle_grad + rows_from_norm
    attn_sums = settle(
        (
            qkv_grad,
            qv_bias_grad,
            out_grad,
            out_bias_grad,
            owner_order(gain_first_grad),
            owner_order(shift_first_grad),
        )
    )
    return (
        layer_out,
        tokens_grad,
        attn_sums[4],
        attn_sums[5],
        attn_sums[0],
        attn_sums[1],
        attn_sums[2],
        attn_sums[3],
        up_sums[1],
        up_sums[2],
        up_sums[0],
        down_sums[2],
        down_sums[0],
        down_sums[1],
    )


PLANE = 8
DEPTH = 4
QUARTERS = 4
VMEM_BYTES = 60 * 2**20
ORDER = (0, 2, 1, 3, 4, 6, 5, 7)


def is_planes(mesh):
    return mesh.shape["rep"] == PLANE and mesh.shape["shard"] == DEPTH


def over_rep(value, flip):
    return lax.ppermute(value, "rep", [(i, i ^ flip) for i in range(PLANE)])


def over_z(value, step):
    return lax.ppermute(value, "shard", [(i, (i + step) % DEPTH) for i in range(DEPTH)])


def over_all(value, place):
    pairs = [(i, place(i)) for i in range(PLANE * DEPTH) if place(i) is not None]
    return lax.ppermute(value, ("rep", "shard"), pairs)


def home_of(index):
    rep, z = index // DEPTH, index % DEPTH
    y, x, core = rep >> 2, (rep >> 1) & 1, rep & 1
    return (4 * x + 2 * (z & 1) + (z >> 1)) * DEPTH + 2 * core + y


HOME = [home_of(i) for i in range(PLANE * DEPTH)]


def to_home(value):
    return over_all(value, lambda i: HOME[i])


def from_home(value):
    return over_all(value, HOME.index)


def after(value, *earlier):
    return lax.optimization_barrier((value, *earlier))[0]


def gather_plane(rows, earlier=()):
    near = over_rep(rows, 1)
    two, four, six = after(tuple(over_rep(rows, flip) for flip in (2, 4, 6)), earlier)
    return [rows, near, two, over_rep(two, 1), four, over_rep(four, 1), six, over_rep(six, 1)]


def add_halves(keep, received):
    count, features = keep.shape[2:]

    def kernel(keep_ref, received_ref, own_ref, two_ref, four_ref, six_ref, left, right, sems):
        outs = {0: own_ref, 2: two_ref, 4: four_ref, 6: six_ref}
        copies = {}
        for flip in (6, 2, 4, 0):
            y, x = flip >> 2, (flip >> 1) & 1
            copies[flip] = [
                pltpu.make_async_copy(ref.at[y, x], to.at[y, x], sems.at[i, flip // 2])
                for i, (ref, to) in enumerate(((keep_ref, left), (received_ref, right)))
            ]
            for copy in copies[flip]:
                copy.start()
        for flip in (6, 2, 4, 0):
            y, x = flip >> 2, (flip >> 1) & 1
            wait_all(copies[flip])
            total = left[y, x].astype(jnp.float32) + right[y, x].astype(jnp.float32)
            outs[flip][...] = total.astype(outs[flip].dtype)

    low = sds((count, features), jnp.bfloat16)
    return kernel_call(
        kernel,
        [ANYWHERE] * 2,
        [sds((count, features), jnp.float32), low, low, low],
        [
            pltpu.VMEM(keep.shape, keep.dtype),
            pltpu.VMEM(keep.shape, keep.dtype),
            pltpu.SemaphoreType.DMA((2, 4)),
        ],
        0,
        (keep, received),
    )


def send_parts(parts):
    own, *others = parts
    return [own] + [over_rep(part, flip) for part, flip in zip(others, (2, 4, 6))]


def scattered_over_z(blocks):
    return lax.psum_scatter(blocks, "shard", scatter_dimension=0, tiled=False)


def outer(left, right):
    return lax.dot_general(
        left, right, (((0,), (0,)), ((), ())), preferred_element_type=jnp.float32
    )


def spread_columns(arrived):
    count = arrived.shape[1]
    parts = arrived.reshape(PLANE, count, -1, 128)
    return jnp.transpose(parts, (1, 2, 0, 3)).reshape(count, -1).astype(jnp.float32)


def dot_nn(left, right):
    return jnp.dot(left, right, preferred_element_type=jnp.float32)


def dot_nt(left, right):
    return lax.dot_general(
        left, right, (((1,), (1,)), ((), ())), preferred_element_type=jnp.float32
    )


def place_pieces(pieces, whole, sems):
    z = lax.axis_index("shard")
    rows = pieces[0].shape[0]
    copies = []
    for step, piece in enumerate(pieces):
        plane = lax.rem(z + (DEPTH - step), DEPTH)
        at = pl.ds(pl.multiple_of(plane * rows, rows), rows)
        copies.append(pltpu.make_async_copy(piece, whole.at[at], sems.at[step]))
    for copy in copies:
        copy.start()
    return copies


def wait_all(copies):
    for copy in copies:
        copy.wait()


def quarter_of(rep):
    return 2 * (rep & 1) + ((rep >> 1) & 1)


def row_positions(shape, axis, rep, first):
    index = lax.broadcasted_iota(jnp.int32, shape, axis) + first
    return (((index >> 7) ^ quarter_of(rep)) << 7) + (index & 127)


def load_blocks(blocks, whole, sems):
    count = whole.shape[0] // PLANE
    copies = []
    for place, k in enumerate(ORDER):
        at = pl.ds(place * count, count)
        block = blocks[k].at[pl.ds(0, count)]
        copies.append(pltpu.make_async_copy(block, whole.at[at], sems.at[place]))
        copies[-1].start()
    return copies


def load(ref, to, sem):
    copy = pltpu.make_async_copy(ref, to, sem)
    copy.start()
    return copy


def total_of(parts):
    own, two, four, six = parts
    return (own[...] + two[...].astype(jnp.float32)) + (
        four[...].astype(jnp.float32) + six[...].astype(jnp.float32)
    )


def unit_rows(v):
    centered = v - jnp.mean(v, 1, keepdims=True)
    rstd = lax.rsqrt(jnp.mean(centered * centered, 1, keepdims=True) + 1e-05)
    return centered * rstd, rstd


def norm_back(grad, xhat, rstd, gain):
    gx = grad * gain
    return rstd * (
        gx - jnp.mean(gx, 1, keepdims=True) - xhat * jnp.mean(gx * xhat, 1, keepdims=True)
    )


def scores_of(query, keys, slope, distance, allowed):
    raw = dot_nt(query, keys) - slope * distance
    return jnp.where(allowed, raw, -1e30)


VECTORS = ((0, 256), (1, 256), (6, 512), (2, 256), (3, 256), (4, 256), (8, 1024), (5, 256))
ANYWHERE = pl.BlockSpec(memory_space=pl.ANY)
LOCAL = pl.BlockSpec(memory_space=pltpu.VMEM)
SCALARS = pl.BlockSpec(memory_space=pltpu.SMEM)


def sds(shape, dtype):
    return jax.ShapeDtypeStruct(shape, dtype)


def kernel_call(kernel, ins, outs, scratch, flops, operands):
    return pl.pallas_call(
        kernel,
        out_shape=outs,
        in_specs=ins,
        out_specs=[LOCAL] * len(outs),
        scratch_shapes=scratch,
        compiler_params=pltpu.CompilerParams(vmem_limit_bytes=VMEM_BYTES),
        cost_estimate=pl.CostEstimate(flops=flops, bytes_accessed=2**23, transcendentals=2**20),
    )(*operands)


def own_eighths(qkv_weight, out_weight, up_weight, down_weight):
    height, features = qkv_weight.shape[0], out_weight.shape[1]
    units = up_weight.shape[1] // PLANE
    half = features // 2

    def kernel(qkv_ref, out_ref, up_ref, down_ref, qkv_own, out_own, wide_own, sems):
        rep = lax.axis_index("rep")
        moves = []
        for ref, own_ref in ((qkv_ref, qkv_own), (up_ref, wide_own)):
            for j in range(ref.shape[1] // (128 * PLANE)):
                at = pl.ds(pl.multiple_of(1024 * j + 128 * rep, 128), 128)
                moves.append((ref.at[:, at], own_ref.at[:, pl.ds(128 * j, 128)]))
        count = out_own.shape[0]
        at = pl.ds(pl.multiple_of((rep & 1) * count, count), count)
        moves.append((out_ref.at[at, :], out_own))
        count = down_ref.shape[0] // PLANE
        at = pl.ds(pl.multiple_of(rep * count, count), count)
        for j in range(2):
            moves.append(
                (
                    down_ref.at[at, pl.ds(j * half, half)],
                    wide_own.at[pl.ds(j * count, count), pl.ds(units, half)],
                )
            )
        copies = [
            pltpu.make_async_copy(src, dst, sems.at[i]) for i, (src, dst) in enumerate(moves)
        ]
        for copy in copies:
            copy.start()
        wait_all(copies)

    low = jnp.bfloat16
    return kernel_call(
        kernel,
        [ANYWHERE] * 4,
        [
            sds((height, qkv_weight.shape[1] // PLANE), low),
            sds((features // PLANE, features), low),
            sds((height, units + half), low),
        ],
        [pltpu.SemaphoreType.DMA((10,))],
        0,
        (qkv_weight, out_weight, up_weight, down_weight),
    )


def first_norm(moved, packs):
    count, features = moved.shape[0] // 2, moved.shape[1]

    def kernel(moved_ref, p0, p1, p2, p3, vectors_ref, normed_ref, tokens_ref):
        z = lax.axis_index("shard")
        packs = [ref[...].astype(jnp.float32) for ref in (p0, p1, p2, p3)]
        vectors_ref[...] = jnp.zeros_like(vectors_ref)
        for plane in range(DEPTH):
            back = lax.rem(z + (DEPTH - plane), DEPTH)
            pack = packs[3]
            for step in range(3):
                pack = jnp.where(back == step, packs[step], pack)
            start = 0
            for row, size in VECTORS:
                for i in range(size // 128):
                    at = plane * size + i * 128
                    lanes = pl.ds(at % 1024, 128)
                    vectors_ref[row + at // 1024 : row + at // 1024 + 1, lanes] = pack[
                        start + i : start + i + 1
                    ]
                start += size // 128
        tokens = moved_ref[:count]
        tokens_ref[...] = tokens
        xhat, unused = unit_rows(tokens.astype(jnp.float32))
        normed = xhat * vectors_ref[0:1, :] + vectors_ref[1:2, :]
        normed_ref[...] = normed.astype(jnp.bfloat16)

    return kernel_call(
        kernel,
        [LOCAL] * 5,
        [sds((16, features), jnp.float32), *[sds((count, features), jnp.bfloat16)] * 2],
        [],
        0,
        (moved, *packs),
    )


def second_norm(tokens, vectors, parts):
    def kernel(tokens_ref, vectors_ref, own, two, four, six, middle_ref, normed_ref):
        attended = total_of((own, two, four, six)) + vectors_ref[2:3, :]
        middle = tokens_ref[...].astype(jnp.float32) + attended
        middle_ref[...] = middle
        xhat, unused = unit_rows(middle)
        normed = xhat * vectors_ref[3:4, :] + vectors_ref[4:5, :]
        normed_ref[...] = normed.astype(jnp.bfloat16)

    return kernel_call(
        kernel,
        [LOCAL] * 6,
        [sds(tokens.shape, jnp.float32), sds(tokens.shape, jnp.bfloat16)],
        [],
        0,
        (tokens, vectors, *parts),
    )


def second_norm_back(vectors, middle, seed_low, parts):
    rows, features = middle.shape

    def kernel(
        vectors_ref, middle_ref, seed_ref, own, two, four, six,
        grad_ref, low_ref, sums_ref,
    ):
        seed = seed_ref[...].astype(jnp.float32)
        grad = total_of((own, two, four, six))
        xhat, rstd = unit_rows(middle_ref[...])
        total = seed + norm_back(grad, xhat, rstd, vectors_ref[3:4, :])
        grad_ref[...] = total
        low = total.astype(jnp.bfloat16)
        low_ref[...] = low
        sums_ref[0:1, :] = jnp.sum(grad * xhat, 0, keepdims=True)
        sums_ref[1:2, :] = jnp.sum(grad, 0, keepdims=True)
        sums_ref[2:3, :] = jnp.sum(low.astype(jnp.float32), 0, keepdims=True)
        sums_ref[3:4, :] = jnp.sum(seed, 0, keepdims=True)

    return kernel_call(
        kernel,
        [LOCAL] * 7,
        [
            sds((rows, features), jnp.float32),
            sds((rows, features), jnp.bfloat16),
            sds((4, features), jnp.float32),
        ],
        [],
        0,
        (vectors, middle, seed_low, *parts),
    )


def first_norm_back(tokens, vectors, middle_grad, parts):
    rows, features = tokens.shape

    def kernel(tokens_ref, vectors_ref, base_ref, own, two, four, six, grad_ref, sums_ref):
        grad = total_of((own, two, four, six))
        xhat, rstd = unit_rows(tokens_ref[...].astype(jnp.float32))
        total = base_ref[...] + norm_back(grad, xhat, rstd, vectors_ref[0:1, :])
        grad_ref[...] = total.astype(jnp.bfloat16)
        sums_ref[0:1, :] = jnp.sum(grad * xhat, 0, keepdims=True)
        sums_ref[1:2, :] = jnp.sum(grad, 0, keepdims=True)

    return kernel_call(
        kernel,
        [LOCAL] * 7,
        [sds((rows, features), jnp.bfloat16), sds((2, features), jnp.float32)],
        [],
        0,
        (tokens, vectors, middle_grad, *parts),
    )


def attention_forward(lens, slopes, blocks, weights, vectors):
    rows, features = PLANE * blocks[0].shape[0], blocks[0].shape[1]
    span = rows // 2
    width = weights[0].shape[1]
    own = width // 3
    head_size = own // 2
    scale = 1.0 / math.sqrt(head_size)
    step_rows = span // QUARTERS

    def kernel(
        own_length, other_length, slopes_ref, n0, n1, n2, n3, n4, n5, n6, n7, w0, w1, w2, w3,
        vectors_ref, joint_ref, mixed_ref, probs_ref, weight_ref, normed_ref, sems, more_sems,
    ):
        rep = lax.axis_index("rep")
        weight_copies = place_pieces((w0, w1, w2, w3), weight_ref, sems)
        copies = load_blocks((n0, n1, n2, n3, n4, n5, n6, n7), normed_ref, more_sems)
        mine = pl.ds(pl.multiple_of(rep * own, own), own)
        bias_q, bias_v = vectors_ref[6:7, mine], vectors_ref[7:8, mine]
        wait_all(weight_copies)
        for s in range(2):
            for c in range(2):
                at = pl.ds((2 * s + c) * (span // 2), span // 2)
                wait_all(copies[4 * s + 2 * c : 4 * s + 2 * c + 2])
                joint = dot_nn(normed_ref[at, :], weight_ref[...])
                joint_ref[at, :own] = (joint[:, :own] + bias_q).astype(jnp.bfloat16)
                joint_ref[at, own : 2 * own] = joint[:, own : 2 * own].astype(jnp.bfloat16)
                joint_ref[at, 2 * own :] = (joint[:, 2 * own :] + bias_v).astype(jnp.bfloat16)
        lane = lax.broadcasted_iota(jnp.int32, (step_rows, own), 1)
        key_pos = row_positions((1, span), 1, rep, 0)
        for s in range(2):
            keys = joint_ref[pl.ds(s * span, span), own : 2 * own]
            values = joint_ref[pl.ds(s * span, span), 2 * own :]
            length = (own_length, other_length)[s][0:1, 0:1]
            inside = key_pos.astype(jnp.float32) < length

            @pl.loop(0, QUARTERS)
            def _(i):
                first = pl.multiple_of(i * step_rows, step_rows)
                at = pl.ds(s * span + first, step_rows)
                query_pos = row_positions((step_rows, 1), 0, rep, first)
                allowed = (key_pos <= query_pos) & inside
                distance = query_pos.astype(jnp.float32) - key_pos.astype(jnp.float32)
                query = joint_ref[at, :own] * jnp.bfloat16(scale)
                mixed = jnp.zeros((step_rows, own), jnp.float32)
                for j in range(2):
                    mine = (lane >= j * head_size) & (lane < (j + 1) * head_size)
                    masked = jnp.where(mine, query, jnp.zeros_like(query))
                    scores = scores_of(masked, keys, slopes_ref[j], distance, allowed)
                    top = jnp.max(scores, 1, keepdims=True)
                    exps = jnp.exp(scores - top)
                    probs = exps * (1.0 / jnp.sum(exps, 1, keepdims=True))
                    probs_low = probs.astype(jnp.bfloat16)
                    probs_ref[j, at, :] = probs_low
                    mixed = jnp.where(mine, dot_nn(probs_low, values), mixed)
                mixed_ref[at, :] = mixed.astype(jnp.bfloat16)

    return kernel_call(
        kernel,
        [LOCAL] * 2 + [SCALARS] + [ANYWHERE] * 12 + [LOCAL],
        [
            sds((rows, width), jnp.bfloat16),
            sds((rows, own), jnp.bfloat16),
            sds((2, rows, span), jnp.bfloat16),
        ],
        [
            pltpu.VMEM((features, width), jnp.bfloat16),
            pltpu.VMEM((rows, features), jnp.bfloat16),
            pltpu.SemaphoreType.DMA((DEPTH,)),
            pltpu.SemaphoreType.DMA((PLANE,)),
        ],
        2 * rows * features * width + 8 * rows * span * own,
        (*lens, slopes, *blocks, *weights, vectors),
    )


def out_projection(mixed, out_part):
    rows, features = mixed.shape[0], out_part.shape[1]
    tile = rows // 4

    def kernel(mixed_ref, out_ref, keep_ref, give_ref):
        for s in range(2):
            for c, part_ref in enumerate((keep_ref, give_ref)):
                at = pl.ds((2 * s + c) * tile, tile)
                part = dot_nn(mixed_ref[at, :], out_ref[...]).astype(jnp.bfloat16)
                part_ref[s] = part.reshape(2, tile // 2, features)

    half = sds((2, 2, tile // 2, features), jnp.bfloat16)
    return kernel_call(
        kernel, [LOCAL] * 2, [half, half], [], 2 * rows * features * mixed.shape[1], (mixed, out_part)
    )


def attention_backward(probs, blocks, joint, weights, out_part):
    rows, features = PLANE * blocks[0].shape[0], blocks[0].shape[1]
    span = rows // 2
    width = weights[0].shape[1]
    own = width // 3
    head_size = own // 2
    scale = 1.0 / math.sqrt(head_size)
    step_rows = span // QUARTERS

    def kernel(
        probs_hbm, g0, g1, g2, g3, g4, g5, g6, g7,
        joint_hbm, w0, w1, w2, w3, out_ref,
        joint_grad_ref, sums_ref, keep_ref, give_ref,
        weight_ref, mixed_grad_ref, key_acc, value_acc, joint_ref, grad_ref, out_all, probs_ref, sems,
        more_sems, probs_sem,
    ):
        out_copy = load(out_ref, out_all, sems.at[DEPTH])
        grad_copies = load_blocks((g0, g1, g2, g3, g4, g5, g6, g7), grad_ref, more_sems)
        joint_copy = load(joint_hbm, joint_ref, sems.at[DEPTH + 1])
        probs_copy = load(probs_hbm, probs_ref, probs_sem.at[0])
        copies = place_pieces((w0, w1, w2, w3), weight_ref, sems)
        out_copy.wait()
        for s in range(2):
            for c in range(2):
                at = pl.ds((2 * s + c) * (span // 2), span // 2)
                wait_all(grad_copies[4 * s + 2 * c : 4 * s + 2 * c + 2])
                mixed_grad = dot_nt(grad_ref[at, :], out_all[...])
                mixed_grad_ref[at, :] = mixed_grad.astype(jnp.bfloat16)
        joint_copy.wait()
        probs_copy.wait()
        lane = lax.broadcasted_iota(jnp.int32, (step_rows, own), 1)
        lane_all = lax.broadcasted_iota(jnp.int32, (span, own), 1)
        for s in range(2):
            keys = joint_ref[pl.ds(s * span, span), own : 2 * own]
            values = joint_ref[pl.ds(s * span, span), 2 * own :]
            key_acc[...] = jnp.zeros_like(key_acc)
            value_acc[...] = jnp.zeros_like(value_acc)

            @pl.loop(0, QUARTERS)
            def _(i):
                first = pl.multiple_of(i * step_rows, step_rows)
                at = pl.ds(s * span + first, step_rows)
                query = joint_ref[at, :own]
                mixed_grad = mixed_grad_ref[at, :]
                query_grad = jnp.zeros((step_rows, own), jnp.float32)
                score_grads, queries, all_probs, mixed_grads = [], [], [], []
                for j in range(2):
                    mine = (lane >= j * head_size) & (lane < (j + 1) * head_size)
                    masked = jnp.where(mine, query, jnp.zeros_like(query))
                    masked_grad = jnp.where(mine, mixed_grad, jnp.zeros_like(mixed_grad))
                    probs_low = probs_ref[j, at, :]
                    probs = probs_low.astype(jnp.float32)
                    probs_grad = dot_nt(masked_grad, values)
                    row_dot = jnp.sum(probs * probs_grad, 1, keepdims=True)
                    score_grad = (probs * (probs_grad - row_dot)).astype(jnp.bfloat16)
                    query_grad = jnp.where(mine, dot_nn(score_grad, keys), query_grad)
                    score_grads.append(score_grad)
                    queries.append(masked)
                    all_probs.append(probs_low)
                    mixed_grads.append(masked_grad)
                key_acc[...] += outer(
                    jnp.concatenate(score_grads, 0), jnp.concatenate(queries, 0)
                )
                value_acc[...] += outer(
                    jnp.concatenate(all_probs, 0), jnp.concatenate(mixed_grads, 0)
                )
                joint_grad_ref[at, :own] = (query_grad * scale).astype(jnp.bfloat16)

            at = pl.ds(s * span, span)
            joint_grad_ref[at, own : 2 * own] = (key_acc[...] * scale).astype(jnp.bfloat16)
            joint_grad_ref[at, 2 * own :] = value_acc[...].astype(jnp.bfloat16)
        wait_all(copies)
        total = jnp.zeros((1, width), jnp.float32)
        for s in range(2):
            for c, part_ref in enumerate((keep_ref, give_ref)):
                at = pl.ds((2 * s + c) * (span // 2), span // 2)
                joint_grad = joint_grad_ref[at, :]
                total = total + jnp.sum(joint_grad.astype(jnp.float32), 0, keepdims=True)
                part = dot_nt(joint_grad, weight_ref[...]).astype(jnp.bfloat16)
                part_ref[s] = part.reshape(2, span // 4, features)
        sums_ref[...] = total

    half = sds((2, 2, span // 4, features), jnp.bfloat16)
    return kernel_call(
        kernel,
        [ANYWHERE] * 15,
        [sds((rows, width), jnp.bfloat16), sds((1, width), jnp.float32), half, half],
        [
            pltpu.VMEM((features, width), jnp.bfloat16),
            pltpu.VMEM((rows, own), jnp.bfloat16),
            pltpu.VMEM((span, own), jnp.float32),
            pltpu.VMEM((span, own), jnp.float32),
            pltpu.VMEM((rows, width), jnp.bfloat16),
            pltpu.VMEM((rows, features), jnp.bfloat16),
            pltpu.VMEM((own, features), jnp.bfloat16),
            pltpu.VMEM(probs.shape, jnp.bfloat16),
            pltpu.SemaphoreType.DMA((DEPTH + 2,)),
            pltpu.SemaphoreType.DMA((PLANE,)),
            pltpu.SemaphoreType.DMA((1,)),
        ],
        2 * rows * features * (width + own) + 20 * rows * span * own,
        (probs, *blocks, joint, *weights, out_part),
    )


def feed_forward(blocks, grads, wide, vectors):
    count, features = blocks[0].shape
    rows = PLANE * count
    half_width = features // 2
    units = wide.shape[1] - half_width
    tile = 2 * count
    root = math.sqrt(2.0 / math.pi)
    bend = 0.044715

    def kernel(
        n0, n1, n2, n3, n4, n5, n6, n7, g0, g1, g2, g3, g4, g5, g6, g7, wide_hbm, vectors_ref,
        active_ref, hidden_grad_ref, sums_ref, branch_keep_ref, branch_give_ref, keep_ref, give_ref,
        up_ref, down_ref, normed_ref, grad_ref, sems, grad_sems, more_sems,
    ):
        rep = lax.axis_index("rep")
        up_copies = [load(wide_hbm.at[:, pl.ds(0, units)], up_ref, more_sems.at[0])]
        copies = load_blocks((n0, n1, n2, n3, n4, n5, n6, n7), normed_ref, sems)
        grad_copies = load_blocks((g0, g1, g2, g3, g4, g5, g6, g7), grad_ref, grad_sems)
        down_copies = []
        for p in range(DEPTH):
            for j in range(2):
                source = wide_hbm.at[pl.ds((2 * p + j) * 128, 128), pl.ds(units, half_width)]
                to = down_ref.at[pl.ds(p * 128, 128), pl.ds(j * half_width, half_width)]
                down_copies.append(load(source, to, more_sems.at[2 + 2 * p + j]))
        mine = pl.ds(pl.multiple_of(rep * 128, 128), 128)
        bias = jnp.concatenate([vectors_ref[8 + p : 9 + p, mine] for p in range(DEPTH)], 1)
        total = jnp.zeros((1, units), jnp.float32)
        for s in range(2):
            for c in range(2):
                at = pl.ds((2 * s + c) * tile, tile)
                if (s, c) == (0, 0):
                    wait_all(up_copies)
                wait_all(copies[4 * s + 2 * c : 4 * s + 2 * c + 2])
                v = dot_nn(normed_ref[at, :], up_ref[...]) + bias
                square = v * v
                t = jnp.tanh(root * v * (1.0 + bend * square))
                half = 0.5 * (1.0 + t)
                active = (v * half).astype(jnp.bfloat16)
                slope = half + (0.5 * root) * v * (1.0 - t * t) * (1.0 + 3.0 * bend * square)
                if (s, c) == (0, 0):
                    wait_all(grad_copies)
                    wait_all(down_copies)
                hidden_grad = (dot_nt(grad_ref[at, :], down_ref[...]) * slope).astype(jnp.bfloat16)
                hidden_grad_ref[at, :] = hidden_grad
                total = total + jnp.sum(hidden_grad.astype(jnp.float32), 0, keepdims=True)
                back = dot_nt(hidden_grad, up_ref[...]).astype(jnp.bfloat16)
                (keep_ref, give_ref)[c][s] = back.reshape(2, count, features)
                branch = dot_nn(active, down_ref[...]).astype(jnp.bfloat16)
                active_ref[at, :] = active
                (branch_keep_ref, branch_give_ref)[c][s] = branch.reshape(2, count, features)
        sums_ref[...] = total

    half = sds((2, 2, count, features), jnp.bfloat16)
    return kernel_call(
        kernel,
        [ANYWHERE] * 17 + [LOCAL],
        [
            sds((rows, units), jnp.bfloat16),
            sds((rows, units), jnp.bfloat16),
            sds((1, units), jnp.float32),
            half,
            half,
            half,
            half,
        ],
        [
            pltpu.VMEM((features, units), jnp.bfloat16),
            pltpu.VMEM((units, features), jnp.bfloat16),
            pltpu.VMEM((rows, features), jnp.bfloat16),
            pltpu.VMEM((rows, features), jnp.bfloat16),
            pltpu.SemaphoreType.DMA((PLANE,)),
            pltpu.SemaphoreType.DMA((PLANE,)),
            pltpu.SemaphoreType.DMA((2 + 2 * DEPTH,)),
        ],
        8 * rows * features * units,
        (*blocks, *grads, wide, vectors),
    )


def feed_forward_weights(blocks, hidden_grad, active, grads):
    count, features = blocks[0].shape
    rows, units = hidden_grad.shape

    def kernel(
        n0, n1, n2, n3, n4, n5, n6, n7, g0, g1, g2, g3, g4, g5, g6, g7, hidden_grad_hbm, active_hbm,
        wide_ref, normed_ref, hidden_grad_ref, active_ref, grad_ref, sems, grad_sems, more_sems,
    ):
        active_copies = [load(active_hbm, active_ref, more_sems.at[0])]
        active_copies += load_blocks((g0, g1, g2, g3, g4, g5, g6, g7), grad_ref, grad_sems)
        copies = [load(hidden_grad_hbm, hidden_grad_ref, more_sems.at[1])]
        copies += load_blocks((n0, n1, n2, n3, n4, n5, n6, n7), normed_ref, sems)
        wait_all(active_copies)
        for p in range(DEPTH):
            part = active_ref[:, p * 128 : (p + 1) * 128]
            down = outer(part, grad_ref[...]).astype(jnp.bfloat16)
            wide_ref[p, :128, units:] = down[:, : features // 2]
            wide_ref[p, 128:, units:] = down[:, features // 2 :]
        wait_all(copies)
        for r in range(PLANE):
            part = outer(normed_ref[:, r * 128 : (r + 1) * 128], hidden_grad_ref[...])
            part = part.astype(jnp.bfloat16).reshape(DEPTH, 32, units)
            wide_ref[:, r * 32 : (r + 1) * 32, :units] = part

    low = jnp.bfloat16
    return kernel_call(
        kernel,
        [ANYWHERE] * 18,
        [sds((DEPTH, PLANE * 32, units + features // 2), low)],
        [
            pltpu.VMEM((rows, features), low),
            pltpu.VMEM((rows, units), low),
            pltpu.VMEM((rows, units), low),
            pltpu.VMEM((rows, features), low),
            pltpu.SemaphoreType.DMA((PLANE,)),
            pltpu.SemaphoreType.DMA((PLANE,)),
            pltpu.SemaphoreType.DMA((2,)),
        ],
        4 * rows * features * units,
        (*blocks, *grads, hidden_grad, active),
    )[0]


def qkv_weights(blocks, joint_grad):
    features = blocks[0].shape[1]
    rows, width = joint_grad.shape

    def kernel(
        n0, n1, n2, n3, n4, n5, n6, n7, joint_grad_hbm,
        q0, q1, q2, q3, normed_ref, joint_grad_ref, sems, more_sems,
    ):
        z = lax.axis_index("shard")
        copies = [load(joint_grad_hbm, joint_grad_ref, more_sems.at[0])]
        copies += load_blocks((n0, n1, n2, n3, n4, n5, n6, n7), normed_ref, sems)
        wait_all(copies)
        for r in range(PLANE):
            part = outer(normed_ref[:, r * 128 : (r + 1) * 128], joint_grad_ref[...])
            part = part.astype(jnp.bfloat16).reshape(DEPTH, 32, width)
            for step, ref in enumerate((q0, q1, q2, q3)):
                for p in range(DEPTH):

                    @pl.when(lax.rem(z + step, DEPTH) == p)
                    def _():
                        ref[r] = part[p]

    low = jnp.bfloat16
    return kernel_call(
        kernel,
        [ANYWHERE] * 9,
        [sds((PLANE, 32, width), low)] * 4,
        [
            pltpu.VMEM((rows, features), low),
            pltpu.VMEM((rows, width), low),
            pltpu.SemaphoreType.DMA((PLANE,)),
            pltpu.SemaphoreType.DMA((1,)),
        ],
        2 * rows * features * width,
        (*blocks, joint_grad),
    )


def out_weights(mixed, grads):
    count, features = grads[0].shape
    rows, own = mixed.shape

    def kernel(mixed_ref, g0, g1, g2, g3, g4, g5, g6, g7, out_ref, grad_ref, sems):
        wait_all(load_blocks((g0, g1, g2, g3, g4, g5, g6, g7), grad_ref, sems))
        part = outer(mixed_ref[...], grad_ref[...])
        out_ref[...] = part.astype(jnp.bfloat16).reshape(DEPTH, own // DEPTH, features)

    return kernel_call(
        kernel,
        [LOCAL] + [ANYWHERE] * 8,
        [sds((DEPTH, own // DEPTH, features), jnp.bfloat16)],
        [pltpu.VMEM((rows, features), jnp.bfloat16), pltpu.SemaphoreType.DMA((PLANE,))],
        2 * rows * features * own,
        (mixed, *grads),
    )[0]


def body_planes(
    tokens,
    cotangent,
    lengths,
    assign,
    first_gain,
    first_shift,
    qkv_weight,
    qv_bias,
    out_weight,
    out_bias,
    second_gain,
    second_shift,
    up_weight,
    up_bias,
    down_weight,
    down_bias,
):
    row_count, feature_count = tokens.shape
    rep = lax.axis_index("rep")
    z = lax.axis_index("shard")
    own = feature_count // PLANE
    devices = PLANE * DEPTH

    small = (
        first_gain,
        first_shift,
        qv_bias,
        out_bias,
        second_gain,
        second_shift,
        up_bias,
        down_bias,
    )
    whole = sum(item.shape[0] for item in small)
    start = 0
    packed = jnp.zeros((whole,), jnp.bfloat16)
    for item in small:
        packed = packed + jnp.pad(item, (start, whole - start - item.shape[0]))
        start += item.shape[0]
    packed = packed.reshape(-1, 128)
    packs = [packed] + [over_z(packed, step) for step in (1, 2, 3)]
    moved = to_home(jnp.concatenate([tokens, cotangent], 0))
    own_length = jnp.sum(jnp.where(jnp.arange(lengths.shape[0]) == assign[0], lengths, 0))
    length = to_home(jnp.full((8, 128), own_length.astype(jnp.float32)))
    lens = (length, over_rep(length, 4))

    weights = after((qkv_weight, out_weight, up_weight, down_weight), moved, packs, lens)
    qkv_own, out_own, wide_own = own_eighths(*weights)
    vectors, normed, tokens = first_norm(moved, packs)
    qkv_own = after(qkv_own, normed)
    qkv_parts = [qkv_own] + [over_z(qkv_own, step) for step in (1, 2, 3)]
    normed_blocks = gather_plane(normed, qkv_parts)
    cotangent = after(moved, normed_blocks)[row_count:]
    position = quarter_of(rep) * row_count + jnp.arange(row_count)
    valid = position.astype(jnp.float32) < length[0, 0]
    branch_grad = jnp.where(valid[:, None], cotangent, jnp.zeros_like(cotangent))
    branch_near = [over_rep(branch_grad, flip) for flip in (1, 2, 4, 6)]
    heads = (2 * rep + jnp.arange(2)).astype(jnp.float32)
    slopes = jnp.exp2(-8.0 * (heads + 1.0) / HEADS)
    joint, mixed, probs = attention_forward(lens, slopes, normed_blocks, qkv_parts, vectors)
    out_moved = [
        over_all(
            after(out_own, qkv_parts),
            lambda i, step=step: (
                i - i % DEPTH + (i % DEPTH + step) % DEPTH if i % DEPTH == i // 8 else None
            ),
        )
        for step in (1, 2, 3)
    ]
    out_part = jnp.where(z == rep >> 1, out_own, jnp.zeros_like(out_own))
    out_moved, branch_near = after((out_moved, branch_near), mixed)
    for piece in out_moved:
        out_part = out_part + piece
    branch_blocks = [branch_grad, branch_near[0]]
    for block in branch_near[1:]:
        branch_blocks += [block, over_rep(block, 1)]
    wide_all = lax.all_gather(after(wide_own, out_part), "shard", axis=0, tiled=True)
    keep, give = out_projection(mixed, out_part)
    parts = send_parts(add_halves(keep, over_rep(give, 1)))
    middle, normed_two = second_norm(tokens, vectors, parts)
    normed_two_blocks = gather_plane(normed_two)
    active, hidden_grad, hidden_sums, branch_keep, branch_give, keep, give = feed_forward(
        normed_two_blocks, branch_blocks, wide_all, vectors
    )
    received = over_rep(give, 1)
    parts = send_parts(add_halves(keep, received))
    branch_received = over_rep(after(branch_give, received), 1)
    branch_halves = add_halves(branch_keep, after(branch_received, parts[0]))
    wide_slice = feed_forward_weights(
        normed_two_blocks, after(hidden_grad, parts[0]), active, branch_blocks
    )
    middle_grad, attended_grad, second_sums = second_norm_back(
        vectors, middle, branch_grad, after(parts, wide_slice, branch_halves)
    )
    wide_summed = scattered_over_z(after(wide_slice, attended_grad))
    attended_blocks = gather_plane(attended_grad)
    branch_own, *branch_rest = send_parts(branch_halves)
    joint_grad, joint_sums, keep, give = attention_backward(
        probs, attended_blocks, joint, qkv_parts, out_part
    )
    received = over_rep(after(give, branch_rest), 1)
    qkv_slices = qkv_weights(normed_blocks, joint_grad)
    parts = send_parts(add_halves(keep, after(received, qkv_slices)))
    qkv_slices = [qkv_slices[0]] + [over_z(qkv_slices[step], step) for step in (1, 2, 3)]
    out_slice = out_weights(after(mixed, parts[0]), attended_blocks)
    tokens_grad, first_sums = first_norm_back(
        tokens, vectors, middle_grad, after(parts, out_slice, qkv_slices)
    )
    tokens_grad = from_home(tokens_grad)
    units = wide_summed.shape[1] - feature_count // 2
    wide_summed, qkv_slices = after((wide_summed, qkv_slices), first_sums)
    up_summed = wide_summed[:, :units].reshape(PLANE, -1, units)
    qkv_summed = qkv_slices[0].astype(jnp.float32)
    for step in (1, 2, 3):
        qkv_summed = qkv_summed + qkv_slices[step].astype(jnp.float32)
    both = jnp.concatenate([up_summed, qkv_summed.astype(jnp.bfloat16)], 2)
    arrived = lax.all_to_all(both, "rep", 0, 0, tiled=True)
    up_grad = spread_columns(arrived[:, :, :units])
    qkv_grad = spread_columns(arrived[:, :, units:])
    out_grad = scattered_over_z(out_slice).astype(jnp.float32)
    down_summed = jnp.concatenate([wide_summed[:128, units:], wide_summed[128:, units:]], 1)
    down_grad = over_all(
        down_summed,
        lambda i: (2 * (i % DEPTH) + i // 16) * DEPTH + (i // DEPTH) % DEPTH,
    )
    branch = branch_own + sum(part.astype(jnp.float32) for part in branch_rest)
    layer_low = (middle + branch + vectors[5:6]).astype(jnp.bfloat16)
    layer_out = from_home(after(layer_low, parts[0]))

    at_rep = (jnp.arange(PLANE) == rep)[None, :, None]

    def placed(sums):
        return jnp.where(at_rep, sums.reshape(-1, 1, 128), 0.0).reshape(-1)

    joint_parts = joint_sums.reshape(3, own)
    small_grads = (
        first_sums[0],
        first_sums[1],
        placed(jnp.concatenate([joint_parts[:1], joint_parts[2:]], 0)),
        second_sums[2],
        second_sums[0],
        second_sums[1],
        placed(hidden_sums),
        second_sums[3],
    )
    small_packed = jnp.concatenate(
        [g.reshape(devices, g.shape[0] // devices) for g in small_grads], 1
    ).astype(jnp.bfloat16)
    small_arrived = lax.all_to_all(after(small_packed, arrived), ("rep", "shard"), 0, 0, tiled=True)
    layer_out, tokens_grad, down_grad = (
        moved_back.astype(jnp.float32)
        for moved_back in after((layer_out, tokens_grad, down_grad), arrived)
    )
    small_sums = jnp.sum(small_arrived.astype(jnp.float32), 0)
    sums = []
    start = 0
    for g in small_grads:
        size = g.shape[0] // devices
        sums.append(small_sums[start : start + size])
        start += size
    return (
        layer_out,
        tokens_grad,
        sums[0],
        sums[1],
        qkv_grad,
        sums[2],
        out_grad,
        sums[3],
        sums[4],
        sums[5],
        up_grad,
        sums[6],
        down_grad,
        sums[7],
    )


def solution(mesh):
    return jax.shard_map(
        body_planes if is_planes(mesh) else body_generic,
        mesh=mesh,
        in_specs=(
            P(("rep", "shard"), None),
            P(("rep", "shard"), None),
            P(),
            P("rep"),
            P("shard"),
            P("shard"),
            P("shard", None),
            P("shard"),
            P("shard", None),
            P("shard"),
            P("shard"),
            P("shard"),
            P("shard", None),
            P("shard"),
            P("shard", None),
            P("shard"),
        ),
        out_specs=(
            P(("rep", "shard"), None),
            P(("rep", "shard"), None),
            P(("rep", "shard")),
            P(("rep", "shard")),
            P(("rep", "shard"), None),
            P(("rep", "shard")),
            P(("rep", "shard"), None),
            P(("rep", "shard")),
            P(("rep", "shard")),
            P(("rep", "shard")),
            P(("rep", "shard"), None),
            P(("rep", "shard")),
            P(("rep", "shard"), None),
            P(("rep", "shard")),
        ),
        check_vma=False,
    )
```
